32 devices in a mesh: gx: 4 (over x, core), gy: 8 (over z, y).
Axes of the slice: x: 2, y: 2, z: 4, core: 2. Of those that a mesh axis runs over, the one named last changes fastest.
Arguments:
- state: float32 [16, 256, 1024], P(None, 'gx', 'gy'), may hold values from -5.5 to 5.5
- kappa_x: float32 [16, 256, 1024], P(None, 'gx', 'gy'), may hold values from 300 to 30000
- kappa_y: float32 [16, 256, 1024], P(None, 'gx', 'gy'), may hold values from 300 to 30000
Outputs:
- updated: float32 [16, 256, 1024], P(None, 'gx', 'gy')
The draws below stay inside these ranges and needn't reach their ends.
All inputs are finite; a program needn't handle non-finite values.
Results may differ from the reference program's by a relative error of at most 0.025.
Values sent between devices are 32-bit elements; how exact they have to be, the bound alone decides.
A program may use at most 128 MiB of HBM per device.

```python
import math
import jax
import jax.numpy as jnp
from jax import lax

NZ = 16
NX = 256
NY = 1024


def wave_field(key, base, single, paired):
    keys = jax.random.split(key, 2)
    phase_x = jax.random.uniform(keys[0], (NZ, 1, 1), jnp.float32, 0.0, 2.0 * math.pi)
    phase_y = jax.random.uniform(keys[1], (NZ, 1, 1), jnp.float32, 0.0, 2.0 * math.pi)
    place_x = jnp.arange(NX, dtype=jnp.float32)[None, :, None] / NX
    place_y = jnp.arange(NY, dtype=jnp.float32)[None, None, :] / NY
    wave_x = jnp.cos(2.0 * math.pi * place_x + phase_x)
    wave_y = jnp.cos(2.0 * math.pi * place_y + phase_y)
    return base + single * (wave_x + wave_y) + paired * wave_x * wave_y


def kappa_field(key, base, single, paired):
    keys = jax.random.split(key, 2)
    smooth = wave_field(keys[0], base, single, paired)
    rough = jax.random.uniform(keys[1], (NZ, NX, NY), jnp.float32, -0.15, 0.15)
    return 300.0 * jnp.power(10.0, 0.15 + 1.7 * smooth + rough)


def draw_kappa_x(key, part):
    key = jax.random.fold_in(key, 11)
    return kappa_field(key, 0.5, 0.25, 0.0)


def draw_kappa_y(key, part):
    key = jax.random.fold_in(key, 17)
    return kappa_field(key, 0.5, 0.25, 0.0)


def draw_state(key, part):
    key = jax.random.fold_in(key, 23)
    keys = jax.random.split(key, 2)
    rough = jnp.clip(jax.random.normal(keys[0], (NZ, NX, NY), jnp.float32), -5.0, 5.0)
    return rough + wave_field(keys[1], 0.0, 0.0, 0.5)


def setup_inputs(seed: int = 0) -> dict:
    arg_keys = jax.random.split(jax.random.key(seed), 4)
    return {
        "state": draw_state(jax.random.fold_in(arg_keys[3], 71), 0),
        "kappa_x": draw_kappa_x(jax.random.fold_in(arg_keys[3], 71), 0),
        "kappa_y": draw_kappa_y(jax.random.fold_in(arg_keys[3], 71), 0),
    }


def faces(kappa, axis):
    length = kappa.shape[axis]
    widths = [(0, 0)] * kappa.ndim
    widths[axis] = (1, 1)
    padded = jnp.pad(kappa, widths)
    before = lax.slice_in_dim(padded, 0, length, axis=axis)
    centre = lax.slice_in_dim(padded, 1, length + 1, axis=axis)
    after = lax.slice_in_dim(padded, 2, length + 2, axis=axis)
    return (0.5 * (before + centre), 0.5 * (centre + after))

def apply_lap(field, left, right, axis):
    length = field.shape[axis]
    widths = [(0, 0)] * field.ndim
    widths[axis] = (1, 1)
    padded = jnp.pad(field, widths)
    before = lax.slice_in_dim(padded, 0, length, axis=axis)
    after = lax.slice_in_dim(padded, 2, length + 2, axis=axis)
    return right * (after - field) - left * (field - before)

def solve_lines(left, right, source, axis):
    left_last = jnp.moveaxis(left, axis, -1)
    right_last = jnp.moveaxis(right, axis, -1)
    source_last = jnp.moveaxis(source, axis, -1)
    lower = (-left_last).at[..., 0].set(0.0)
    upper = (-right_last).at[..., -1].set(0.0)
    diag = 1.0 + left_last + right_last
    solved = lax.linalg.tridiagonal_solve(lower, diag, upper, source_last[..., None])[..., 0]
    return jnp.moveaxis(solved, -1, axis)

def reference(state, kappa_x, kappa_y):
    left_x, right_x = faces(kappa_x, 1)
    left_y, right_y = faces(kappa_y, 2)
    lap_x = apply_lap(state, left_x, right_x, 1)
    lap_y = apply_lap(state, left_y, right_y, 2)
    source = state + lap_x + 2.0 * lap_y
    middle = solve_lines(left_x, right_x, source, 1)
    return solve_lines(left_y, right_y, middle - lap_y, 2)
```

```python
import functools

import jax
import jax.numpy as jnp
from jax import lax
from jax.experimental import pallas as pl
from jax.experimental.pallas import tpu as pltpu
from jax.sharding import PartitionSpec as P

MESH = pl.DeviceIdType.MESH
F32 = jnp.float32
SUB = 8


def recip(p):
    r = pl.reciprocal(p, approx=True)
    r = r * (2.0 - p * r)
    return r * (2.0 - p * r)


def factor_cells(face, coef):
    s = jnp.ones_like(face(0))
    to_p = face(0)
    at_p = jnp.zeros_like(s)
    for t in range(SUB - 1):
        right = face(t + 1)
        r = recip(s + to_p + right)
        a = right * r
        b = to_p * r
        coef[0, t] = r
        coef[1, t] = a
        coef[2, t] = b
        at_p = at_p + s * b
        s = 1.0 + s * a
        to_p = to_p * a
    return at_p, to_p, s


def halves(v):
    v = v.reshape((v.shape[0] // 2, 2) + v.shape[1:])
    return v[:, 0], v[:, 1]


def factor_tree(at_p, series, at_l, tree):
    level = 0
    at = 0
    while at_p.shape[0] > 1:
        pa, pb = halves(at_p)
        ga, gb = halves(series)
        la, lb = halves(at_l)
        c = la + pb
        r = recip(c + ga + gb)
        a = gb * r
        b = ga * r
        m = r.shape[0]
        tree[0, at : at + m] = r
        tree[1, at : at + m] = a
        tree[2, at : at + m] = b
        at_p = pa + c * b
        at_l = lb + c * a
        series = ga * a
        at += m
        level += 1
    return at_p[0], series[0], at_l[0]


def down_cells(source, coef, kept):
    d = source(0)
    at_p = None
    for t in range(SUB - 1):
        kept[t] = d
        share = coef[2, t] * d
        at_p = share if at_p is None else at_p + share
        d = source(t + 1) + coef[1, t] * d
    return at_p, d


def down_tree(at_p, at_l, tree, kept):
    at = 0
    while at_p.shape[0] > 1:
        pa, pb = halves(at_p)
        la, lb = halves(at_l)
        d = la + pb
        m = d.shape[0]
        kept[at : at + m] = d
        at_p = pa + tree[2, at : at + m] * d
        at_l = lb + tree[1, at : at + m] * d
        at += m
    return at_p[0], at_l[0]


def up_tree(u_p, u_l, tree, kept):
    nodes = u_l[None]
    total = kept.shape[0]
    m = 1
    at = total - 1
    while at >= 0:
        before = u_p[None] if m == 1 else jnp.concatenate([u_p[None], nodes[:-1]], axis=0)
        mid = (
            tree[0, at : at + m] * kept[at : at + m]
            + tree[1, at : at + m] * nodes
            + tree[2, at : at + m] * before
        )
        nodes = jnp.stack([mid, nodes], axis=1).reshape((2 * m,) + nodes.shape[1:])
        m *= 2
        at -= m
    before = jnp.concatenate([u_p[None], nodes[:-1]], axis=0)
    return before, nodes


def up_cells(before, nodes, coef, kept, put):
    u = nodes
    put(SUB - 1, u)
    for t in range(SUB - 2, -1, -1):
        u = coef[0, t] * kept[t] + coef[1, t] * u + coef[2, t] * before
        put(t, u)


def line_weights(me, n, every, weights, mine):
    zero = jnp.zeros(every.shape[2:], F32)
    ahead = []
    prior = None
    for j in range(n):
        p, g, l = every[j, 0], every[j, 1], every[j, 2]
        if prior is None:
            ahead.append((zero, zero, l + g))
            prior = l + g
        else:
            c = prior + p
            ratio = g * recip(c + g)
            now = l + c * ratio
            ahead.append((ratio, prior, now))
            prior = now
    back = [None] * n
    later = zero
    for j in range(n - 1, -1, -1):
        p, g, l = every[j, 0], every[j, 1], every[j, 2]
        c = later + l
        ratio = g * recip(c + g)
        now = p + c * ratio
        back[j] = (ratio, later, now)
        later = now
    own = [zero] * 6
    for j in range(n):
        here = me == j
        own = [jnp.where(here, v, o) for v, o in zip(ahead[j] + back[j], own)]
    rho, sf_prior, sf_now, tau, sb_later, sb_now = own
    inv_l = recip(sf_now + sb_later)
    inv_p = jnp.where(me > 0, recip(sf_prior + sb_now), zero)
    w_p = inv_p
    w_l = inv_l * rho
    for j in range(n - 1, -1, -1):
        left = me > j
        weights[j, 0] = jnp.where(left, w_p, zero)
        weights[j, 1] = jnp.where(left, w_l, zero)
        w_p = jnp.where(left, w_p * ahead[j][0], w_p)
        w_l = jnp.where(left, w_l * ahead[j][0], w_l)
    w_p = inv_p * tau
    w_l = inv_l
    for j in range(n):
        right = me < j
        weights[j, 0] = jnp.where(right, w_p, weights[j, 0])
        weights[j, 1] = jnp.where(right, w_l, weights[j, 1])
        w_p = jnp.where(right, w_p * back[j][0], w_p)
        w_l = jnp.where(right, w_l * back[j][0], w_l)
    mine[0] = rho
    mine[1] = tau
    mine[2] = inv_p
    mine[3] = inv_l


class Line:
    def __init__(self, axis, n, me, send, recv):
        self.axis, self.n, self.me, self.send, self.recv = axis, n, me, send, recv

    def copy(self, src, dst, slot, target):
        return pltpu.make_async_remote_copy(
            src_ref=src,
            dst_ref=dst,
            send_sem=self.send.at[slot],
            recv_sem=self.recv.at[slot],
            device_id={self.axis: target},
            device_id_type=MESH,
        )

    def others(self):
        for o in range(1, self.n):
            yield o, lax.rem(self.me + o, self.n), lax.rem(self.me + self.n - o, self.n)

    def start_all(self, src_of, buf, base):
        for o, target, _ in self.others():
            self.copy(src_of(o), buf.at[self.me], base + o - 1, target).start()

    def await_one(self, o, src, buf, base):
        source = lax.rem(self.me + self.n - o, self.n)
        self.copy(src, buf.at[source], base + o - 1, source).wait_recv()

    def done_sending(self, src_of, buf, base):
        for o, target, _ in self.others():
            self.copy(src_of(o), buf.at[self.me], base + o - 1, target).wait_send()


def share_coefs(line, mine, every):
    for i, v in enumerate(mine):
        every[line.me, i] = v
    line.start_all(lambda o: every.at[line.me], every, 0)


def await_coefs(line, every):
    for o, _, _ in line.others():
        line.await_one(o, every.at[line.me], every, 0)


def kernel(
    nx, ny, dims,
    u_hbm, kx_hbm, ky_hbm, out_ref,
    u_raw, kx_raw, ky_raw,
    u_x, gx, vx, turned, u_y, k_y,
    coef_x, kept_x, tree_x, tkept_x, every_x, weights_x, mine_x, out_x, got_x,
    coef_y, kept_y, tree_y, tkept_y, every_y, weights_y, mine_y, out_y, got_y,
    edge_x_out, edge_x_in, edge_y_out, edge_y_in,
    local_sem, xs, xr, ys, yr,
):
    nz, lx, ly = dims
    per = 128 // nz
    groups = lx // per
    ix = lax.axis_index("gx")
    iy = lax.axis_index("gy")
    loads = []
    for i, (src, dst) in enumerate(((ky_hbm, ky_raw), (u_hbm, u_raw), (kx_hbm, kx_raw))):
        cp = pltpu.make_async_copy(src, dst, local_sem.at[i])
        cp.start()
        loads.append(cp)
    line_x = Line("gx", nx, ix, xs, xr)
    line_y = Line("gy", ny, iy, ys, yr)
    barrier = pltpu.get_barrier_semaphore()
    for line in (line_x, line_y):
        for _, target, _ in line.others():
            pl.semaphore_signal(barrier, inc=1, device_id={line.axis: target}, device_id_type=MESH)

    def turn_in(block, g):
        turned[g * ly : (g + 1) * ly] = block.T

    def turned_row(y):
        return turned[pl.ds(y, groups, stride=ly), :]

    loads[0].wait()
    for g in range(groups):
        turn_in(jnp.concatenate([ky_raw[pl.ds(x, nz, stride=lx), :] for x in range(g * per, (g + 1) * per)], axis=0), g)
    for y in range(ly):
        k_y[y] = turned_row(y)
    loads[1].wait()
    for g in range(groups):
        rows = []
        for x in range(g * per, (g + 1) * per):
            row = u_raw[pl.ds(x, nz, stride=lx), :]
            u_x[x] = row
            rows.append(row)
        turn_in(jnp.concatenate(rows, axis=0), g)
    for y in range(ly):
        u_y[y] = turned_row(y)
    edge_y_out[0, 0] = k_y[0]
    edge_y_out[0, 1] = u_y[0]
    edge_y_out[1, 0] = k_y[ly - 1]
    edge_y_out[1, 1] = u_y[ly - 1]
    loads[2].wait()
    kx_last = kx_raw[pl.ds(lx - 1, nz, stride=lx), :]
    edge_x_out[...] = kx_last
    total = nx - 1 + ny - 1
    pl.semaphore_wait(barrier, total)

    hx = 2 * (nx - 1)
    hy = 2 * (ny - 1)

    def edge_x():
        return line_x.copy(edge_x_out, edge_x_in, hx, jnp.minimum(ix + 1, nx - 1))

    def edge_y_right():
        return line_y.copy(edge_y_out.at[1], edge_y_in.at[0], hy, jnp.minimum(iy + 1, ny - 1))

    def edge_y_left():
        return line_y.copy(edge_y_out.at[0], edge_y_in.at[1], hy + 1, jnp.maximum(iy - 1, 0))

    @pl.when(ix < nx - 1)
    def _():
        edge_x().start()

    @pl.when(iy < ny - 1)
    def _():
        edge_y_right().start()

    @pl.when(iy > 0)
    def _():
        edge_y_left().start()

    prior = kx_raw[pl.ds(0, nz, stride=lx), :]
    for x in range(1, lx):
        now = kx_raw[pl.ds(x, nz, stride=lx), :]
        gx[x // SUB, x % SUB] = 0.5 * (prior + now)
        prior = now

    @pl.when(ix > 0)
    def _():
        edge_x().wait_recv()

    gx[0, 0] = 0.5 * (jnp.where(ix > 0, edge_x_in[...], 0.0) + kx_raw[pl.ds(0, nz, stride=lx), :])
    at_p, series, at_l = factor_tree(*factor_cells(lambda t: gx[:, t], coef_x), tree_x)
    at_l = at_l + jnp.where(ix == nx - 1, 0.5 * kx_last, 0.0)
    share_coefs(line_x, (at_p, series, at_l), every_x)

    @pl.when(iy > 0)
    def _():
        edge_y_right().wait_recv()

    @pl.when(iy < ny - 1)
    def _():
        edge_y_left().wait_recv()

    k_prior = jnp.where(iy > 0, edge_y_in[0, 0], 0.0)
    u_prior = jnp.where(iy > 0, edge_y_in[0, 1], 0.0)
    k_last = k_y[ly - 1]
    k_now = k_y[0]
    u_now = u_y[0]
    face = 0.5 * (k_prior + k_now)
    k_y[0] = face
    flux = face * (u_now - u_prior)
    for y in range(ly):
        if y < ly - 1:
            k_next = k_y[y + 1]
            u_next = u_y[y + 1]
        else:
            k_next = jnp.where(iy < ny - 1, edge_y_in[1, 0], 0.0)
            u_next = jnp.where(iy < ny - 1, edge_y_in[1, 1], 0.0)
        face = 0.5 * (k_now + k_next)
        if y < ly - 1:
            k_y[y + 1] = face
        flux_next = face * (u_next - u_now)
        turned[pl.ds(y, groups, stride=ly), :] = u_now + (flux_next - flux)
        k_now, u_now, flux = k_next, u_next, flux_next
    for g in range(groups):
        back = turned[g * ly : (g + 1) * ly].T
        vx[g * per : (g + 1) * per] = back.reshape(per, nz, ly)
    vx_t = vx.reshape(lx // SUB, SUB, nz, ly)
    k_yt = k_y.reshape(ly // SUB, SUB, groups, 128)
    d_p, d_l = down_cells(lambda t: vx_t[:, t], coef_x, kept_x)
    d_p, d_l = down_tree(d_p, d_l, tree_x, tkept_x)
    await_coefs(line_x, every_x)
    line_weights(ix, nx, every_x, weights_x, mine_x)
    u_p, u_l = solve_ports_start(line_x, d_p, d_l, out_x, got_x, mine_x)

    at_p, series, at_l = factor_tree(*factor_cells(lambda t: k_yt[:, t], coef_y), tree_y)
    at_l = at_l + jnp.where(iy == ny - 1, 0.5 * k_last, 0.0)
    share_coefs(line_y, (at_p, series, at_l), every_y)

    u_p, u_l = solve_ports_end(line_x, u_p, u_l, out_x, got_x, weights_x)
    before, nodes = up_tree(u_p, u_l, tree_x, tkept_x)

    def put_x(t, v):
        vx_t[:, t] = v

    up_cells(before, nodes, coef_x, kept_x, put_x)
    for g in range(groups):
        q = vx[g * per : (g + 1) * per] - u_x[g * per : (g + 1) * per]
        turn_in(q.reshape(128, ly), g)
    for y in range(ly):
        u_y[y] = turned_row(y)
    u_yt = u_y.reshape(ly // SUB, SUB, groups, 128)
    d_p, d_l = down_cells(lambda t: u_yt[:, t], coef_y, kept_y)
    d_p, d_l = down_tree(d_p, d_l, tree_y, tkept_y)
    await_coefs(line_y, every_y)
    line_weights(iy, ny, every_y, weights_y, mine_y)
    u_p, u_l = solve_ports_start(line_y, d_p, d_l, out_y, got_y, mine_y)
    u_p, u_l = solve_ports_end(line_y, u_p, u_l, out_y, got_y, weights_y)
    before, nodes = up_tree(u_p, u_l, tree_y, tkept_y)

    def put_y(t, v):
        u_yt[:, t] = v

    up_cells(before, nodes, coef_y, kept_y, put_y)
    for y in range(ly):
        turned[pl.ds(y, groups, stride=ly), :] = u_y[y]
    for g in range(groups):
        w = turned[g * ly : (g + 1) * ly].T.reshape(per, nz, ly)
        o = u_x[g * per : (g + 1) * per] + 2.0 * w
        for i in range(per):
            out_ref[pl.ds(g * per + i, nz, stride=lx), :] = o[i]

    for line, every, out, got in ((line_x, every_x, out_x, got_x), (line_y, every_y, out_y, got_y)):
        line.done_sending(lambda o: every.at[line.me], every, 0)
        line.done_sending(lambda o: out.at[0], got, line.n - 1)

    @pl.when(ix < nx - 1)
    def _():
        edge_x().wait_send()

    @pl.when(iy < ny - 1)
    def _():
        edge_y_right().wait_send()

    @pl.when(iy > 0)
    def _():
        edge_y_left().wait_send()


def solve_ports_start(line, at_p, at_l, out, got, mine):
    n, me = line.n, line.me
    to_right = at_l + mine[0] * at_p
    to_left = at_p + mine[1] * at_l
    out[0] = to_right
    out[1] = to_left
    line.start_all(lambda o: out.at[(me + o) // n], got, n - 1)
    return mine[2] * to_left, mine[3] * to_right


def solve_ports_end(line, u_p, u_l, out, got, weights):
    for o, _, source in line.others():
        line.await_one(o, out.at[0], got, line.n - 1)
        v = got[source]
        u_p = u_p + weights[source, 0] * v
        u_l = u_l + weights[source, 1] * v
    return u_p, u_l


def on_device(nx, ny, state, kappa_x, kappa_y):
    nz, lx, ly = state.shape
    groups = nz * lx // 128
    flat = (nz * lx, ly)
    bx, by = lx // SUB, ly // SUB

    def line_scratch(n, blocks, rows):
        one = (rows, 128)
        return [
            pltpu.VMEM((3, SUB - 1, blocks) + one, F32),
            pltpu.VMEM((SUB - 1, blocks) + one, F32),
            pltpu.VMEM((3, blocks - 1) + one, F32),
            pltpu.VMEM((blocks - 1,) + one, F32),
            pltpu.VMEM((n, 3) + one, F32),
            pltpu.VMEM((n, 2) + one, F32),
            pltpu.VMEM((4,) + one, F32),
            pltpu.VMEM((2,) + one, F32),
            pltpu.VMEM((n,) + one, F32),
        ]

    scratch = (
        [pltpu.VMEM(flat, F32)] * 3
        + [
            pltpu.VMEM((lx, nz, ly), F32),
            pltpu.VMEM((bx, SUB, nz, ly), F32),
            pltpu.VMEM((lx, nz, ly), F32),
            pltpu.VMEM((groups * ly, 128), F32),
            pltpu.VMEM((ly, groups, 128), F32),
            pltpu.VMEM((ly, groups, 128), F32),
        ]
        + line_scratch(nx, bx, nz)
        + line_scratch(ny, by, groups)
        + [
            pltpu.VMEM((nz, ly), F32),
            pltpu.VMEM((nz, ly), F32),
            pltpu.VMEM((2, 2, groups, 128), F32),
            pltpu.VMEM((2, 2, groups, 128), F32),
            pltpu.SemaphoreType.DMA((3,)),
            pltpu.SemaphoreType.DMA((2 * nx - 1,)),
            pltpu.SemaphoreType.DMA((2 * nx - 1,)),
            pltpu.SemaphoreType.DMA((2 * ny,)),
            pltpu.SemaphoreType.DMA((2 * ny,)),
        ]
    )
    out = pl.pallas_call(
        functools.partial(kernel, nx, ny, (nz, lx, ly)),
        out_shape=jax.ShapeDtypeStruct(flat, F32),
        in_specs=[pl.BlockSpec(memory_space=pl.ANY)] * 3,
        out_specs=pl.BlockSpec(memory_space=pltpu.VMEM),
        scratch_shapes=scratch,
        compiler_params=pltpu.CompilerParams(
            collective_id=0, has_side_effects=True, vmem_limit_bytes=32 * 1024 * 1024
        ),
    )(state.reshape(flat), kappa_x.reshape(flat), kappa_y.reshape(flat))
    return out.reshape(state.shape)


def solution(mesh):
    spec = P(None, "gx", "gy")
    return jax.shard_map(
        functools.partial(on_device, mesh.shape["gx"], mesh.shape["gy"]),
        mesh=mesh,
        in_specs=(spec, spec, spec),
        out_specs=spec,
        check_vma=False,
    )
```

```python
import functools

import jax
import jax.numpy as jnp
from jax import lax
from jax.experimental import pallas as pl
from jax.experimental.pallas import tpu as pltpu
from jax.sharding import PartitionSpec as P

MESH = pl.DeviceIdType.MESH
F32 = jnp.float32
SUB = 8


def recip(p):
    r = pl.reciprocal(p, approx=True)
    return r * (2.0 - p * r)


def factor_cells(face, coef):
    s = jnp.ones_like(face(0))
    to_p = face(0)
    at_p = jnp.zeros_like(s)
    for t in range(SUB - 1):
        right = face(t + 1)
        r = recip(s + to_p + right)
        a = right * r
        b = to_p * r
        coef[0, t] = r
        coef[1, t] = a
        coef[2, t] = b
        at_p = at_p + s * b
        s = 1.0 + s * a
        to_p = to_p * a
    return at_p, to_p, s


def halves(v):
    v = v.reshape((v.shape[0] // 2, 2) + v.shape[1:])
    return v[:, 0], v[:, 1]


def factor_tree(at_p, series, at_l, tree):
    level = 0
    at = 0
    while at_p.shape[0] > 1:
        pa, pb = halves(at_p)
        ga, gb = halves(series)
        la, lb = halves(at_l)
        c = la + pb
        r = recip(c + ga + gb)
        a = gb * r
        b = ga * r
        m = r.shape[0]
        tree[0, at : at + m] = r
        tree[1, at : at + m] = a
        tree[2, at : at + m] = b
        at_p = pa + c * b
        at_l = lb + c * a
        series = ga * a
        at += m
        level += 1
    return at_p[0], series[0], at_l[0]


def down_cells(source, coef, kept):
    d = source(0)
    at_p = None
    for t in range(SUB - 1):
        kept[t] = d
        share = coef[2, t] * d
        at_p = share if at_p is None else at_p + share
        d = source(t + 1) + coef[1, t] * d
    return at_p, d


def down_tree(at_p, at_l, tree, kept):
    at = 0
    while at_p.shape[0] > 1:
        pa, pb = halves(at_p)
        la, lb = halves(at_l)
        d = la + pb
        m = d.shape[0]
        kept[at : at + m] = d
        at_p = pa + tree[2, at : at + m] * d
        at_l = lb + tree[1, at : at + m] * d
        at += m
    return at_p[0], at_l[0]


def up_tree(u_p, u_l, tree, kept):
    nodes = u_l[None]
    total = kept.shape[0]
    m = 1
    at = total - 1
    while at >= 0:
        before = u_p[None] if m == 1 else jnp.concatenate([u_p[None], nodes[:-1]], axis=0)
        mid = (
            tree[0, at : at + m] * kept[at : at + m]
            + tree[1, at : at + m] * nodes
            + tree[2, at : at + m] * before
        )
        nodes = jnp.stack([mid, nodes], axis=1).reshape((2 * m,) + nodes.shape[1:])
        m *= 2
        at -= m
    before = jnp.concatenate([u_p[None], nodes[:-1]], axis=0)
    return before, nodes


def up_cells(before, nodes, coef, kept, put):
    u = nodes
    put(SUB - 1, u)
    for t in range(SUB - 2, -1, -1):
        u = coef[0, t] * kept[t] + coef[1, t] * u + coef[2, t] * before
        put(t, u)


def line_ratios(me, n, every, chain, mine):
    zero = jnp.zeros(every.shape[2:], F32)
    ahead = []
    prior = None
    for j in range(n):
        p, g, l = every[j, 0], every[j, 1], every[j, 2]
        if prior is None:
            ahead.append((zero, zero, l + g))
            prior = l + g
        else:
            c = prior + p
            ratio = g * recip(c + g)
            now = l + c * ratio
            ahead.append((ratio, prior, now))
            prior = now
    back = [None] * n
    later = zero
    for j in range(n - 1, -1, -1):
        p, g, l = every[j, 0], every[j, 1], every[j, 2]
        c = later + l
        ratio = g * recip(c + g)
        now = p + c * ratio
        back[j] = (ratio, later, now)
        later = now
    own = [zero] * 6
    for j in range(n):
        here = me == j
        own = [jnp.where(here, v, o) for v, o in zip(ahead[j] + back[j], own)]
        chain[j, 0] = ahead[j][0]
        chain[j, 1] = back[j][0]
    for i, v in enumerate(own):
        mine[i] = v


def line_weights(me, n, chain, mine, weights):
    rho, sf_prior, sf_now, tau, sb_later, sb_now = [mine[i] for i in range(6)]
    zero = jnp.zeros_like(rho)
    inv_l = recip(sf_now + sb_later)
    inv_p = jnp.where(me > 0, recip(sf_prior + sb_now), zero)
    ahead = [None] * n
    w_p, w_l = inv_p, inv_l * rho
    for j in range(n - 1, -1, -1):
        left = me > j
        ahead[j] = (w_p, w_l)
        w_p = jnp.where(left, w_p * chain[j, 0], w_p)
        w_l = jnp.where(left, w_l * chain[j, 0], w_l)
    w_p, w_l = inv_p * tau, inv_l
    for j in range(n):
        left, right = me > j, me < j
        weights[j, 0] = jnp.where(left, ahead[j][0], w_p)
        weights[j, 1] = jnp.where(left, ahead[j][1], w_l)
        w_p = jnp.where(right, w_p * chain[j, 1], w_p)
        w_l = jnp.where(right, w_l * chain[j, 1], w_l)
    return inv_p, inv_l


class Line:
    def __init__(self, axis, n, me, send, recv):
        self.axis, self.n, self.me, self.send, self.recv = axis, n, me, send, recv

    def copy(self, src, dst, slot, target):
        return pltpu.make_async_remote_copy(
            src_ref=src,
            dst_ref=dst,
            send_sem=self.send.at[slot],
            recv_sem=self.recv.at[slot],
            device_id={self.axis: target},
            device_id_type=MESH,
        )

    def others(self):
        for o in range(1, self.n):
            yield o, lax.rem(self.me + o, self.n), lax.rem(self.me + self.n - o, self.n)

    def start_all(self, src_of, buf, base):
        for o, target, _ in self.others():
            self.copy(src_of(o), buf.at[self.me], base + o - 1, target).start()

    def await_one(self, o, src, buf, base):
        source = lax.rem(self.me + self.n - o, self.n)
        self.copy(src, buf.at[source], base + o - 1, source).wait_recv()

    def done_sending(self, src_of, buf, base):
        for o, target, _ in self.others():
            self.copy(src_of(o), buf.at[self.me], base + o - 1, target).wait_send()


def share_coefs(line, mine, every):
    for i, v in enumerate(mine):
        every[line.me, i] = v
    line.start_all(lambda o: every.at[line.me], every, 0)


def await_coefs(line, every):
    for o, _, _ in line.others():
        line.await_one(o, every.at[line.me], every, 0)


def send_values(line, at_p, at_l, out, got, mine):
    me = line.me
    out[0] = at_l + mine[0] * at_p
    out[1] = at_p + mine[3] * at_l
    line.start_all(lambda o: out.at[(me + o) // line.n], got, line.n - 1)


def take_values(line, inverses, out, got, weights):
    u_p = inverses[0] * out[1]
    u_l = inverses[1] * out[0]
    for o, _, source in line.others():
        line.await_one(o, out.at[0], got, line.n - 1)
        v = got[source]
        u_p = u_p + weights[source, 0] * v
        u_l = u_l + weights[source, 1] * v
    return u_p, u_l


def kernel(
    nx, ny, dims,
    u_hbm, kx_hbm, ky_hbm, out_ref,
    u_raw, kx_raw, ky_raw, nat, turned, gx, gy,
    coef_x, kept_x, tree_x, tkept_x, every_x, weights_x, chain_x, mine_x, out_x, got_x,
    coef_y, kept_y, tree_y, tkept_y, every_y, weights_y, chain_y, mine_y, out_y, got_y,
    edge_x_out, edge_x_in, edge_y_out, edge_y_in,
    local_sem, xs, xr, ys, yr,
):
    nz, lx, ly = dims
    lanes = 128
    groups = nz * lx // lanes
    bx, by = lx // SUB, ly // SUB
    ix = lax.axis_index("gx")
    iy = lax.axis_index("gy")
    loads = []
    for i, (src, dst) in enumerate(((ky_hbm, ky_raw), (u_hbm, u_raw), (kx_hbm, kx_raw))):
        cp = pltpu.make_async_copy(src, dst, local_sem.at[i])
        cp.start()
        loads.append(cp)
    line_x = Line("gx", nx, ix, xs, xr)
    line_y = Line("gy", ny, iy, ys, yr)
    barrier = pltpu.get_barrier_semaphore()
    for line in (line_x, line_y):
        for _, target, _ in line.others():
            pl.semaphore_signal(barrier, inc=1, device_id={line.axis: target}, device_id_type=MESH)

    def group(ref, g):
        return ref[g * lanes : (g + 1) * lanes]

    def x_rows(ref, x):
        return ref[pl.ds(x, nz, stride=lx), :]

    def y_rows(y):
        return turned[pl.ds(y, groups, stride=ly), :]

    hx = 2 * (nx - 1)
    hy = 2 * (ny - 1)

    def edge_x():
        return line_x.copy(edge_x_out, edge_x_in, hx, jnp.minimum(ix + 1, nx - 1))

    def edge_y_right():
        return line_y.copy(edge_y_out.at[1], edge_y_in.at[0], hy, jnp.minimum(iy + 1, ny - 1))

    def edge_y_left():
        return line_y.copy(edge_y_out.at[0], edge_y_in.at[1], hy + 1, jnp.maximum(iy - 1, 0))

    row8 = lax.broadcasted_iota(jnp.int32, (8, ly), 0)
    lane8 = lax.broadcasted_iota(jnp.int32, (8, ly), 1)
    pick = jnp.where(((row8 == 0) & (lane8 == 0)) | ((row8 == 1) & (lane8 == ly - 1)), 1.0, 0.0).astype(F32)
    for kind, (load, raw) in enumerate(((loads[0], ky_raw), (loads[1], u_raw))):
        load.wait()
        for g in range(groups):
            edges = lax.dot_general(
                pick, group(raw, g), (((1,), (1,)), ((), ())),
                precision=lax.Precision.HIGHEST, preferred_element_type=F32,
            )
            edge_y_out[0, kind, g : g + 1] = edges[0:1]
            edge_y_out[1, kind, g : g + 1] = edges[1:2]
    loads[2].wait()
    kx_first = x_rows(kx_raw, 0)
    kx_last = x_rows(kx_raw, lx - 1)
    edge_x_out[...] = kx_last
    pl.semaphore_wait(barrier, nx - 1 + ny - 1)

    @pl.when(ix < nx - 1)
    def _():
        edge_x().start()

    @pl.when(iy < ny - 1)
    def _():
        edge_y_right().start()

    @pl.when(iy > 0)
    def _():
        edge_y_left().start()

    prior = kx_first
    for x in range(1, lx):
        now = x_rows(kx_raw, x)
        gx[x // SUB, x % SUB] = 0.5 * (prior + now)
        prior = now
    for g in range(groups):
        turned[g * ly : (g + 1) * ly] = group(ky_raw, g).T
    prior = y_rows(0)
    for y in range(1, ly):
        now = y_rows(y)
        gy[y // SUB, y % SUB] = 0.5 * (prior + now)
        prior = now
    ky_last = prior

    @pl.when(ix > 0)
    def _():
        edge_x().wait_recv()

    gx[0, 0] = 0.5 * (jnp.where(ix > 0, edge_x_in[...], 0.0) + kx_first)
    at_p, series, at_l = factor_tree(*factor_cells(lambda t: gx[:, t], coef_x), tree_x)
    at_l = at_l + jnp.where(ix == nx - 1, 0.5 * kx_last, 0.0)
    share_coefs(line_x, (at_p, series, at_l), every_x)

    @pl.when(iy > 0)
    def _():
        edge_y_right().wait_recv()

    @pl.when(iy < ny - 1)
    def _():
        edge_y_left().wait_recv()

    k0, u0, k1, u1 = edge_y_out[0, 0], edge_y_out[0, 1], edge_y_out[1, 0], edge_y_out[1, 1]
    inner, last = iy > 0, iy < ny - 1
    face_0 = 0.5 * (jnp.where(inner, edge_y_in[0, 0], 0.0) + k0)
    gy[0, 0] = face_0
    face_1 = 0.5 * (jnp.where(last, edge_y_in[1, 0], 0.0) + k1)
    flux_0 = face_0 * (jnp.where(inner, edge_y_in[0, 1], 0.0) - u0)
    flux_1 = face_1 * (jnp.where(last, edge_y_in[1, 1], 0.0) - u1)
    ends = jnp.concatenate([flux_0, flux_1], axis=0).T
    row = lax.broadcasted_iota(jnp.int32, (2 * groups, ly), 0)
    lane = lax.broadcasted_iota(jnp.int32, (2 * groups, ly), 1)
    inside = lax.broadcasted_iota(jnp.int32, (lanes, ly), 1) > 0
    for g in range(groups):
        put = jnp.where(((row == g) & (lane == 0)) | ((row == groups + g) & (lane == ly - 1)), 1.0, 0.0).astype(F32)
        added = lax.dot_general(
            ends, put, (((1,), (0,)), ((), ())), precision=lax.Precision.HIGHEST, preferred_element_type=F32
        )
        u = group(u_raw, g)
        k = group(ky_raw, g)
        flux = jnp.where(inside, 0.5 * (k + pltpu.roll(k, 1, 1)) * (u - pltpu.roll(u, 1, 1)), 0.0)
        nat[g * lanes : (g + 1) * lanes] = (u + added) + (pltpu.roll(flux, ly - 1, 1) - flux)

    def x_cells(t):
        return jnp.stack([x_rows(nat, b * SUB + t) for b in range(bx)], axis=0)

    d_p, d_l = down_cells(x_cells, coef_x, kept_x)
    d_p, d_l = down_tree(d_p, d_l, tree_x, tkept_x)
    await_coefs(line_x, every_x)
    line_ratios(ix, nx, every_x, chain_x, mine_x)
    send_values(line_x, d_p, d_l, out_x, got_x, mine_x)

    inverses = line_weights(ix, nx, chain_x, mine_x, weights_x)
    at_p, series, at_l = factor_tree(*factor_cells(lambda t: gy[:, t], coef_y), tree_y)
    at_l = at_l + jnp.where(iy == ny - 1, 0.5 * ky_last, 0.0)
    share_coefs(line_y, (at_p, series, at_l), every_y)

    u_p, u_l = take_values(line_x, inverses, out_x, got_x, weights_x)
    before, nodes = up_tree(u_p, u_l, tree_x, tkept_x)

    def put_x(t, v):
        for b in range(bx):
            nat[pl.ds(b * SUB + t, nz, stride=lx), :] = v[b]

    up_cells(before, nodes, coef_x, kept_x, put_x)
    for g in range(groups):
        turned[g * ly : (g + 1) * ly] = (group(nat, g) - group(u_raw, g)).T

    def y_cells(t):
        return jnp.stack([y_rows(b * SUB + t) for b in range(by)], axis=0)

    d_p, d_l = down_cells(y_cells, coef_y, kept_y)
    d_p, d_l = down_tree(d_p, d_l, tree_y, tkept_y)
    await_coefs(line_y, every_y)
    line_ratios(iy, ny, every_y, chain_y, mine_y)
    send_values(line_y, d_p, d_l, out_y, got_y, mine_y)
    inverses = line_weights(iy, ny, chain_y, mine_y, weights_y)
    u_p, u_l = take_values(line_y, inverses, out_y, got_y, weights_y)
    before, nodes = up_tree(u_p, u_l, tree_y, tkept_y)

    def put_y(t, v):
        for b in range(by):
            turned[pl.ds(b * SUB + t, groups, stride=ly), :] = v[b]

    up_cells(before, nodes, coef_y, kept_y, put_y)
    for g in range(groups):
        out_ref[g * lanes : (g + 1) * lanes] = group(u_raw, g) + 2.0 * turned[g * ly : (g + 1) * ly].T

    for line, every, out, got in ((line_x, every_x, out_x, got_x), (line_y, every_y, out_y, got_y)):
        line.done_sending(lambda o: every.at[line.me], every, 0)
        line.done_sending(lambda o: out.at[0], got, line.n - 1)

    @pl.when(ix < nx - 1)
    def _():
        edge_x().wait_send()

    @pl.when(iy < ny - 1)
    def _():
        edge_y_right().wait_send()

    @pl.when(iy > 0)
    def _():
        edge_y_left().wait_send()


def on_device(nx, ny, state, kappa_x, kappa_y):
    nz, lx, ly = state.shape
    groups = nz * lx // 128
    flat = (nz * lx, ly)
    bx, by = lx // SUB, ly // SUB

    def line_scratch(n, blocks, rows):
        one = (rows, 128)
        return [
            pltpu.VMEM((3, SUB - 1, blocks) + one, F32),
            pltpu.VMEM((SUB - 1, blocks) + one, F32),
            pltpu.VMEM((3, blocks - 1) + one, F32),
            pltpu.VMEM((blocks - 1,) + one, F32),
            pltpu.VMEM((n, 3) + one, F32),
            pltpu.VMEM((n, 2) + one, F32),
            pltpu.VMEM((n, 2) + one, F32),
            pltpu.VMEM((6,) + one, F32),
            pltpu.VMEM((2,) + one, F32),
            pltpu.VMEM((n,) + one, F32),
        ]

    scratch = (
        [pltpu.VMEM(flat, F32)] * 5
        + [
            pltpu.VMEM((bx, SUB, nz, ly), F32),
            pltpu.VMEM((by, SUB, groups, 128), F32),
        ]
        + line_scratch(nx, bx, nz)
        + line_scratch(ny, by, groups)
        + [
            pltpu.VMEM((nz, ly), F32),
            pltpu.VMEM((nz, ly), F32),
            pltpu.VMEM((2, 2, groups, 128), F32),
            pltpu.VMEM((2, 2, groups, 128), F32),
            pltpu.SemaphoreType.DMA((3,)),
            pltpu.SemaphoreType.DMA((2 * nx - 1,)),
            pltpu.SemaphoreType.DMA((2 * nx - 1,)),
            pltpu.SemaphoreType.DMA((2 * ny,)),
            pltpu.SemaphoreType.DMA((2 * ny,)),
        ]
    )
    out = pl.pallas_call(
        functools.partial(kernel, nx, ny, (nz, lx, ly)),
        out_shape=jax.ShapeDtypeStruct(flat, F32),
        in_specs=[pl.BlockSpec(memory_space=pltpu.HBM)] * 3,
        out_specs=pl.BlockSpec(memory_space=pltpu.VMEM),
        scratch_shapes=scratch,
        compiler_params=pltpu.CompilerParams(
            collective_id=0, has_side_effects=True, vmem_limit_bytes=32 * 1024 * 1024
        ),
    )(*[pltpu.with_memory_space_constraint(v.reshape(flat), pltpu.HBM) for v in (state, kappa_x, kappa_y)])
    return out.reshape(state.shape)


def solution(mesh):
    spec = P(None, "gx", "gy")
    return jax.shard_map(
        functools.partial(on_device, mesh.shape["gx"], mesh.shape["gy"]),
        mesh=mesh,
        in_specs=(spec, spec, spec),
        out_specs=spec,
        check_vma=False,
    )
```

```python
import functools

import jax
import jax.numpy as jnp
from jax import lax
from jax.experimental import pallas as pl
from jax.experimental.pallas import tpu as pltpu
from jax.sharding import PartitionSpec as P

MESH = pl.DeviceIdType.MESH
F32 = jnp.float32
SUB = 8


def recip(p):
    r = pl.reciprocal(p, approx=True)
    return r * (2.0 - p * r)


def factor_cells(face, coef):
    s = jnp.ones_like(face(0))
    to_p = face(0)
    at_p = jnp.zeros_like(s)
    for t in range(SUB - 1):
        right = face(t + 1)
        r = recip(s + to_p + right)
        a = right * r
        b = to_p * r
        coef[0, t] = r
        coef[1, t] = a
        coef[2, t] = b
        at_p = at_p + s * b
        s = 1.0 + s * a
        to_p = to_p * a
    return at_p, to_p, s


def halves(v):
    v = v.reshape((v.shape[0] // 2, 2) + v.shape[1:])
    return v[:, 0], v[:, 1]


def factor_tree(at_p, series, at_l, tree):
    level = 0
    at = 0
    while at_p.shape[0] > 1:
        pa, pb = halves(at_p)
        ga, gb = halves(series)
        la, lb = halves(at_l)
        c = la + pb
        r = recip(c + ga + gb)
        a = gb * r
        b = ga * r
        m = r.shape[0]
        tree[0, at : at + m] = r
        tree[1, at : at + m] = a
        tree[2, at : at + m] = b
        at_p = pa + c * b
        at_l = lb + c * a
        series = ga * a
        at += m
        level += 1
    return at_p[0], series[0], at_l[0]


def down_cells(source, coef, kept):
    d = source(0)
    at_p = None
    for t in range(SUB - 1):
        kept[t] = d
        share = coef[2, t] * d
        at_p = share if at_p is None else at_p + share
        d = source(t + 1) + coef[1, t] * d
    return at_p, d


def down_tree(at_p, at_l, tree, kept):
    at = 0
    while at_p.shape[0] > 1:
        pa, pb = halves(at_p)
        la, lb = halves(at_l)
        d = la + pb
        m = d.shape[0]
        kept[at : at + m] = d
        at_p = pa + tree[2, at : at + m] * d
        at_l = lb + tree[1, at : at + m] * d
        at += m
    return at_p[0], at_l[0]


def up_tree(u_p, u_l, tree, kept):
    nodes = u_l[None]
    total = kept.shape[0]
    m = 1
    at = total - 1
    while at >= 0:
        before = u_p[None] if m == 1 else jnp.concatenate([u_p[None], nodes[:-1]], axis=0)
        mid = (
            tree[0, at : at + m] * kept[at : at + m]
            + tree[1, at : at + m] * nodes
            + tree[2, at : at + m] * before
        )
        nodes = jnp.stack([mid, nodes], axis=1).reshape((2 * m,) + nodes.shape[1:])
        m *= 2
        at -= m
    before = jnp.concatenate([u_p[None], nodes[:-1]], axis=0)
    return before, nodes


def up_cells(before, nodes, coef, kept, put):
    u = nodes
    put(SUB - 1, u)
    for t in range(SUB - 2, -1, -1):
        u = coef[0, t] * kept[t] + coef[1, t] * u + coef[2, t] * before
        put(t, u)


def line_ratios(me, n, every, chain, mine):
    zero = jnp.zeros(every.shape[2:], F32)
    ahead = []
    prior = None
    for j in range(n):
        p, g, l = every[j, 0], every[j, 1], every[j, 2]
        if prior is None:
            ahead.append((zero, zero, l + g))
            prior = l + g
        else:
            c = prior + p
            ratio = g * recip(c + g)
            now = l + c * ratio
            ahead.append((ratio, prior, now))
            prior = now
    back = [None] * n
    later = zero
    for j in range(n - 1, -1, -1):
        p, g, l = every[j, 0], every[j, 1], every[j, 2]
        c = later + l
        ratio = g * recip(c + g)
        now = p + c * ratio
        back[j] = (ratio, later, now)
        later = now
    own = [zero] * 6
    for j in range(n):
        here = me == j
        own = [jnp.where(here, v, o) for v, o in zip(ahead[j] + back[j], own)]
        chain[j, 0] = ahead[j][0]
        chain[j, 1] = back[j][0]
    for i, v in enumerate(own):
        mine[i] = v


def line_weights(me, n, chain, mine, weights):
    rho, sf_prior, sf_now, tau, sb_later, sb_now = [mine[i] for i in range(6)]
    zero = jnp.zeros_like(rho)
    inv_l = recip(sf_now + sb_later)
    inv_p = jnp.where(me > 0, recip(sf_prior + sb_now), zero)
    ahead = [None] * n
    w_p, w_l = inv_p, inv_l * rho
    for j in range(n - 1, -1, -1):
        left = me > j
        ahead[j] = (w_p, w_l)
        w_p = jnp.where(left, w_p * chain[j, 0], w_p)
        w_l = jnp.where(left, w_l * chain[j, 0], w_l)
    w_p, w_l = inv_p * tau, inv_l
    for j in range(n):
        left, right = me > j, me < j
        weights[j, 0] = jnp.where(left, ahead[j][0], w_p)
        weights[j, 1] = jnp.where(left, ahead[j][1], w_l)
        w_p = jnp.where(right, w_p * chain[j, 1], w_p)
        w_l = jnp.where(right, w_l * chain[j, 1], w_l)
    return inv_p, inv_l


class Line:
    def __init__(self, axis, n, me, send, recv):
        self.axis, self.n, self.me, self.send, self.recv = axis, n, me, send, recv

    def copy(self, src, dst, slot, target):
        return pltpu.make_async_remote_copy(
            src_ref=src,
            dst_ref=dst,
            send_sem=self.send.at[slot],
            recv_sem=self.recv.at[slot],
            device_id={self.axis: target},
            device_id_type=MESH,
        )

    def others(self):
        for o in range(1, self.n):
            yield o, lax.rem(self.me + o, self.n), lax.rem(self.me + self.n - o, self.n)

    def start_all(self, src_of, buf, base):
        for o, target, _ in self.others():
            self.copy(src_of(o), buf.at[self.me], base + o - 1, target).start()

    def await_one(self, o, src, buf, base):
        source = lax.rem(self.me + self.n - o, self.n)
        self.copy(src, buf.at[source], base + o - 1, source).wait_recv()

    def done_sending(self, src_of, buf, base):
        for o, target, _ in self.others():
            self.copy(src_of(o), buf.at[self.me], base + o - 1, target).wait_send()


def share_coefs(line, mine, every):
    for i, v in enumerate(mine):
        every[line.me, i] = v
    line.start_all(lambda o: every.at[line.me], every, 0)


def await_coefs(line, every):
    for o, _, _ in line.others():
        line.await_one(o, every.at[line.me], every, 0)


def send_values(line, at_p, at_l, out, got, mine):
    me = line.me
    out[0] = at_l + mine[0] * at_p
    out[1] = at_p + mine[3] * at_l
    line.start_all(lambda o: out.at[(me + o) // line.n], got, line.n - 1)


def take_values(line, inverses, out, got, weights):
    u_p = inverses[0] * out[1]
    u_l = inverses[1] * out[0]
    for o, _, source in line.others():
        line.await_one(o, out.at[0], got, line.n - 1)
        v = got[source]
        u_p = u_p + weights[source, 0] * v
        u_l = u_l + weights[source, 1] * v
    return u_p, u_l


def kernel(
    nx, ny, dims,
    u_hbm, kx_hbm, ky_hbm, out_ref,
    u_raw, kx_raw, ky_raw, nat, turned, gx, gy,
    coef_x, kept_x, tree_x, tkept_x, every_x, weights_x, chain_x, mine_x, out_x, got_x,
    coef_y, kept_y, tree_y, tkept_y, every_y, weights_y, chain_y, mine_y, out_y, got_y,
    edge_x_in, edge_y_out, edge_y_in, ends,
    local_sem, xs, xr, ys, yr,
):
    nz, lx, ly = dims
    lanes = 128
    groups = nz * lx // lanes
    bx, by = lx // SUB, ly // SUB
    ix = lax.axis_index("gx")
    iy = lax.axis_index("gy")
    loads = []
    for i, (src, dst) in enumerate(((ky_hbm, ky_raw), (u_hbm, u_raw), (kx_hbm, kx_raw))):
        cp = pltpu.make_async_copy(src, dst, local_sem.at[i])
        cp.start()
        loads.append(cp)
    line_x = Line("gx", nx, ix, xs, xr)
    line_y = Line("gy", ny, iy, ys, yr)
    barrier = pltpu.get_barrier_semaphore()
    for line in (line_x, line_y):
        for _, target, _ in line.others():
            pl.semaphore_signal(barrier, inc=1, device_id={line.axis: target}, device_id_type=MESH)

    def group(ref, g):
        return ref[g * lanes : (g + 1) * lanes]

    def x_rows(ref, x):
        return ref[pl.ds(x, nz, stride=lx), :]

    def y_rows(y):
        return turned[pl.ds(y, groups, stride=ly), :]

    hx = 2 * (nx - 1)
    hy = 2 * (ny - 1)

    def edge_x():
        return line_x.copy(kx_hbm.reshape(nz, lx, ly).at[:, lx - 1, :], edge_x_in, hx, jnp.minimum(ix + 1, nx - 1))

    def edge_y_right():
        return line_y.copy(edge_y_out.at[1], edge_y_in.at[0], hy, jnp.minimum(iy + 1, ny - 1))

    def edge_y_left():
        return line_y.copy(edge_y_out.at[0], edge_y_in.at[1], hy + 1, jnp.maximum(iy - 1, 0))

    pl.semaphore_wait(barrier, nx - 1 + ny - 1)

    @pl.when(ix < nx - 1)
    def _():
        edge_x().start()

    lane = lax.broadcasted_iota(jnp.int32, (lanes, ly), 1)
    packed = None
    for kind, (load, raw) in enumerate(((loads[0], ky_raw), (loads[1], u_raw))):
        load.wait()
        for g in range(groups):
            at = 2 * (kind * groups + g)
            moved = pltpu.roll(group(raw, g), at + 1, 1)
            packed = moved if packed is None else jnp.where(lane >= at, moved, packed)
    ends[...] = packed.T
    for kind in range(2):
        for side in range(2):
            edge_y_out[side, kind] = ends[pl.ds(2 * kind * groups + 1 - side, groups, stride=2), :]

    @pl.when(iy < ny - 1)
    def _():
        edge_y_right().start()

    @pl.when(iy > 0)
    def _():
        edge_y_left().start()

    loads[2].wait()
    kx_first = x_rows(kx_raw, 0)
    kx_last = x_rows(kx_raw, lx - 1)
    prior = kx_first
    for x in range(1, lx):
        now = x_rows(kx_raw, x)
        gx[x // SUB, x % SUB] = 0.5 * (prior + now)
        prior = now
    @pl.when(ix > 0)
    def _():
        edge_x().wait_recv()

    gx[0, 0] = 0.5 * (jnp.where(ix > 0, edge_x_in[...], 0.0) + kx_first)
    at_p, series, at_l = factor_tree(*factor_cells(lambda t: gx[:, t], coef_x), tree_x)
    at_l = at_l + jnp.where(ix == nx - 1, 0.5 * kx_last, 0.0)
    share_coefs(line_x, (at_p, series, at_l), every_x)

    @pl.when(iy > 0)
    def _():
        edge_y_right().wait_recv()

    @pl.when(iy < ny - 1)
    def _():
        edge_y_left().wait_recv()

    k0, u0, k1, u1 = edge_y_out[0, 0], edge_y_out[0, 1], edge_y_out[1, 0], edge_y_out[1, 1]
    inner, last = iy > 0, iy < ny - 1
    face_0 = 0.5 * (jnp.where(inner, edge_y_in[0, 0], 0.0) + k0)
    gy[0, 0] = face_0
    face_1 = 0.5 * (jnp.where(last, edge_y_in[1, 0], 0.0) + k1)
    flux_0 = face_0 * (jnp.where(inner, edge_y_in[0, 1], 0.0) - u0)
    flux_1 = face_1 * (jnp.where(last, edge_y_in[1, 1], 0.0) - u1)
    ends[pl.ds(0, groups, stride=2), :] = flux_1
    ends[pl.ds(1, groups, stride=2), :] = -flux_0
    fluxes = ends[...].T
    for g in range(groups):
        outer = pltpu.roll(fluxes, (ly - 2 * g - 1) % ly, 1)
        u = group(u_raw, g)
        k = group(ky_raw, g)
        flux = 0.5 * (k + pltpu.roll(k, 1, 1)) * (u - pltpu.roll(u, 1, 1))
        flux = jnp.where(lane > 0, flux, outer)
        later = jnp.where(lane < ly - 1, pltpu.roll(flux, ly - 1, 1), outer)
        nat[g * lanes : (g + 1) * lanes] = u + (later - flux)

    await_coefs(line_x, every_x)
    def x_cells(t):
        return jnp.stack([x_rows(nat, b * SUB + t) for b in range(bx)], axis=0)

    d_p, d_l = down_cells(x_cells, coef_x, kept_x)
    d_p, d_l = down_tree(d_p, d_l, tree_x, tkept_x)
    line_ratios(ix, nx, every_x, chain_x, mine_x)
    send_values(line_x, d_p, d_l, out_x, got_x, mine_x)

    inverses = line_weights(ix, nx, chain_x, mine_x, weights_x)
    for g in range(groups):
        turned[g * ly : (g + 1) * ly] = group(ky_raw, g).T
    prior = y_rows(0)
    for y in range(1, ly):
        now = y_rows(y)
        gy[y // SUB, y % SUB] = 0.5 * (prior + now)
        prior = now
    ky_last = prior
    at_p, series, at_l = factor_tree(*factor_cells(lambda t: gy[:, t], coef_y), tree_y)
    at_l = at_l + jnp.where(iy == ny - 1, 0.5 * ky_last, 0.0)
    share_coefs(line_y, (at_p, series, at_l), every_y)

    u_p, u_l = take_values(line_x, inverses, out_x, got_x, weights_x)
    before, nodes = up_tree(u_p, u_l, tree_x, tkept_x)

    def put_x(t, v):
        for b in range(bx):
            nat[pl.ds(b * SUB + t, nz, stride=lx), :] = v[b]

    up_cells(before, nodes, coef_x, kept_x, put_x)
    for g in range(groups):
        turned[g * ly : (g + 1) * ly] = (group(nat, g) - group(u_raw, g)).T

    def y_cells(t):
        return jnp.stack([y_rows(b * SUB + t) for b in range(by)], axis=0)

    await_coefs(line_y, every_y)
    d_p, d_l = down_cells(y_cells, coef_y, kept_y)
    d_p, d_l = down_tree(d_p, d_l, tree_y, tkept_y)
    line_ratios(iy, ny, every_y, chain_y, mine_y)
    send_values(line_y, d_p, d_l, out_y, got_y, mine_y)
    inverses = line_weights(iy, ny, chain_y, mine_y, weights_y)
    line_x.done_sending(lambda o: every_x.at[ix], every_x, 0)
    line_x.done_sending(lambda o: out_x.at[0], got_x, nx - 1)
    line_y.done_sending(lambda o: every_y.at[iy], every_y, 0)

    @pl.when(ix < nx - 1)
    def _():
        edge_x().wait_send()

    @pl.when(iy < ny - 1)
    def _():
        edge_y_right().wait_send()

    @pl.when(iy > 0)
    def _():
        edge_y_left().wait_send()

    u_p, u_l = take_values(line_y, inverses, out_y, got_y, weights_y)
    before, nodes = up_tree(u_p, u_l, tree_y, tkept_y)

    def put_y(t, v):
        for b in range(by):
            turned[pl.ds(b * SUB + t, groups, stride=ly), :] = v[b]

    up_cells(before, nodes, coef_y, kept_y, put_y)
    for g in range(groups):
        out_ref[g * lanes : (g + 1) * lanes] = group(u_raw, g) + 2.0 * turned[g * ly : (g + 1) * ly].T

    line_y.done_sending(lambda o: out_y.at[0], got_y, ny - 1)


def on_device(nx, ny, state, kappa_x, kappa_y):
    nz, lx, ly = state.shape
    groups = nz * lx // 128
    flat = (nz * lx, ly)
    bx, by = lx // SUB, ly // SUB

    def line_scratch(n, blocks, rows):
        one = (rows, 128)
        return [
            pltpu.VMEM((3, SUB - 1, blocks) + one, F32),
            pltpu.VMEM((SUB - 1, blocks) + one, F32),
            pltpu.VMEM((3, blocks - 1) + one, F32),
            pltpu.VMEM((blocks - 1,) + one, F32),
            pltpu.VMEM((n, 3) + one, F32),
            pltpu.VMEM((n, 2) + one, F32),
            pltpu.VMEM((n, 2) + one, F32),
            pltpu.VMEM((6,) + one, F32),
            pltpu.VMEM((2,) + one, F32),
            pltpu.VMEM((n,) + one, F32),
        ]

    scratch = (
        [pltpu.VMEM(flat, F32)] * 5
        + [
            pltpu.VMEM((bx, SUB, nz, ly), F32),
            pltpu.VMEM((by, SUB, groups, 128), F32),
        ]
        + line_scratch(nx, bx, nz)
        + line_scratch(ny, by, groups)
        + [
            pltpu.VMEM((nz, ly), F32),
            pltpu.VMEM((2, 2, groups, 128), F32),
            pltpu.VMEM((2, 2, groups, 128), F32),
            pltpu.VMEM((128, 128), F32),
            pltpu.SemaphoreType.DMA((3,)),
            pltpu.SemaphoreType.DMA((2 * nx - 1,)),
            pltpu.SemaphoreType.DMA((2 * nx - 1,)),
            pltpu.SemaphoreType.DMA((2 * ny,)),
            pltpu.SemaphoreType.DMA((2 * ny,)),
        ]
    )
    out = pl.pallas_call(
        functools.partial(kernel, nx, ny, (nz, lx, ly)),
        out_shape=jax.ShapeDtypeStruct(flat, F32),
        in_specs=[pl.BlockSpec(memory_space=pltpu.HBM)] * 3,
        out_specs=pl.BlockSpec(memory_space=pltpu.VMEM),
        scratch_shapes=scratch,
        compiler_params=pltpu.CompilerParams(
            collective_id=0, has_side_effects=True, vmem_limit_bytes=32 * 1024 * 1024
        ),
    )(*[pltpu.with_memory_space_constraint(v.reshape(flat), pltpu.HBM) for v in (state, kappa_x, kappa_y)])
    return out.reshape(state.shape)


def solution(mesh):
    spec = P(None, "gx", "gy")
    return jax.shard_map(
        functools.partial(on_device, mesh.shape["gx"], mesh.shape["gy"]),
        mesh=mesh,
        in_specs=(spec, spec, spec),
        out_specs=spec,
        check_vma=False,
    )
```

```python
import functools

import jax
import jax.numpy as jnp
from jax import lax
from jax.experimental import pallas as pl
from jax.experimental.pallas import tpu as pltpu
from jax.sharding import PartitionSpec as P

MESH = pl.DeviceIdType.MESH
F32 = jnp.float32
SUB = 8


def recip(p):
    r = pl.reciprocal(p, approx=True)
    return r * (2.0 - p * r)


def factor_cells(face, coef):
    s = jnp.ones_like(face(0))
    to_p = face(0)
    at_p = jnp.zeros_like(s)
    for t in range(SUB - 1):
        right = face(t + 1)
        r = recip(s + to_p + right)
        a = right * r
        b = to_p * r
        coef[0, t] = r
        coef[1, t] = a
        coef[2, t] = b
        at_p = at_p + s * b
        s = 1.0 + s * a
        to_p = to_p * a
    return at_p, to_p, s


def halves(v):
    v = v.reshape((v.shape[0] // 2, 2) + v.shape[1:])
    return v[:, 0], v[:, 1]


def factor_tree(at_p, series, at_l, tree):
    level = 0
    at = 0
    while at_p.shape[0] > 1:
        pa, pb = halves(at_p)
        ga, gb = halves(series)
        la, lb = halves(at_l)
        c = la + pb
        r = recip(c + ga + gb)
        a = gb * r
        b = ga * r
        m = r.shape[0]
        tree[0, at : at + m] = r
        tree[1, at : at + m] = a
        tree[2, at : at + m] = b
        at_p = pa + c * b
        at_l = lb + c * a
        series = ga * a
        at += m
        level += 1
    return at_p[0], series[0], at_l[0]


def down_cells(source, coef, kept):
    d = source(0)
    at_p = None
    for t in range(SUB - 1):
        kept[t] = d
        share = coef[2, t] * d
        at_p = share if at_p is None else at_p + share
        d = source(t + 1) + coef[1, t] * d
    return at_p, d


def down_tree(at_p, at_l, tree, kept):
    at = 0
    while at_p.shape[0] > 1:
        pa, pb = halves(at_p)
        la, lb = halves(at_l)
        d = la + pb
        m = d.shape[0]
        kept[at : at + m] = d
        at_p = pa + tree[2, at : at + m] * d
        at_l = lb + tree[1, at : at + m] * d
        at += m
    return at_p[0], at_l[0]


def up_tree(u_p, u_l, tree, kept):
    nodes = u_l[None]
    total = kept.shape[0]
    m = 1
    at = total - 1
    while at >= 0:
        before = u_p[None] if m == 1 else jnp.concatenate([u_p[None], nodes[:-1]], axis=0)
        mid = (
            tree[0, at : at + m] * kept[at : at + m]
            + tree[1, at : at + m] * nodes
            + tree[2, at : at + m] * before
        )
        nodes = jnp.stack([mid, nodes], axis=1).reshape((2 * m,) + nodes.shape[1:])
        m *= 2
        at -= m
    before = jnp.concatenate([u_p[None], nodes[:-1]], axis=0)
    return before, nodes


def up_cells(before, nodes, coef, kept, put):
    u = nodes
    put(SUB - 1, u)
    for t in range(SUB - 2, -1, -1):
        u = coef[0, t] * kept[t] + coef[1, t] * u + coef[2, t] * before
        put(t, u)


def line_ratios(me, n, every, chain, mine):
    zero = jnp.zeros(every.shape[2:], F32)
    ahead = []
    prior = None
    for j in range(n):
        p, g, l = every[j, 0], every[j, 1], every[j, 2]
        if prior is None:
            ahead.append((zero, zero, l + g))
            prior = l + g
        else:
            c = prior + p
            ratio = g * recip(c + g)
            now = l + c * ratio
            ahead.append((ratio, prior, now))
            prior = now
    back = [None] * n
    later = zero
    for j in range(n - 1, -1, -1):
        p, g, l = every[j, 0], every[j, 1], every[j, 2]
        c = later + l
        ratio = g * recip(c + g)
        now = p + c * ratio
        back[j] = (ratio, later, now)
        later = now
    own = [zero] * 6
    for j in range(n):
        here = me == j
        own = [jnp.where(here, v, o) for v, o in zip(ahead[j] + back[j], own)]
        chain[j, 0] = ahead[j][0]
        chain[j, 1] = back[j][0]
    for i, v in enumerate(own):
        mine[i] = v


def line_weights(me, n, chain, mine, weights):
    rho, sf_prior, sf_now, tau, sb_later, sb_now = [mine[i] for i in range(6)]
    zero = jnp.zeros_like(rho)
    inv_l = recip(sf_now + sb_later)
    inv_p = jnp.where(me > 0, recip(sf_prior + sb_now), zero)
    ahead = [None] * n
    w_p, w_l = inv_p, inv_l * rho
    for j in range(n - 1, -1, -1):
        left = me > j
        ahead[j] = (w_p, w_l)
        w_p = jnp.where(left, w_p * chain[j, 0], w_p)
        w_l = jnp.where(left, w_l * chain[j, 0], w_l)
    w_p, w_l = inv_p * tau, inv_l
    for j in range(n):
        left, right = me > j, me < j
        weights[j, 0] = jnp.where(left, ahead[j][0], w_p)
        weights[j, 1] = jnp.where(left, ahead[j][1], w_l)
        w_p = jnp.where(right, w_p * chain[j, 1], w_p)
        w_l = jnp.where(right, w_l * chain[j, 1], w_l)
    return inv_p, inv_l


class Line:
    def __init__(self, axis, n, me, send, recv):
        self.axis, self.n, self.me, self.send, self.recv = axis, n, me, send, recv

    def copy(self, src, dst, slot, target):
        return pltpu.make_async_remote_copy(
            src_ref=src,
            dst_ref=dst,
            send_sem=self.send.at[slot],
            recv_sem=self.recv.at[slot],
            device_id={self.axis: target},
            device_id_type=MESH,
        )

    def others(self):
        for o in range(1, self.n):
            yield o, lax.rem(self.me + o, self.n), lax.rem(self.me + self.n - o, self.n)

    def start_all(self, src_of, buf, base):
        for o, target, _ in self.others():
            self.copy(src_of(o), buf.at[self.me], base + o - 1, target).start()

    def await_one(self, o, src, buf, base):
        source = lax.rem(self.me + self.n - o, self.n)
        self.copy(src, buf.at[source], base + o - 1, source).wait_recv()

    def done_sending(self, src_of, buf, base):
        for o, target, _ in self.others():
            self.copy(src_of(o), buf.at[self.me], base + o - 1, target).wait_send()


def share_coefs(line, mine, every):
    for i, v in enumerate(mine):
        every[line.me, i] = v
    line.start_all(lambda o: every.at[line.me], every, 0)


def await_coefs(line, every):
    for o, _, _ in line.others():
        line.await_one(o, every.at[line.me], every, 0)


def send_values(line, at_p, at_l, out, got, mine):
    me = line.me
    out[0] = at_l + mine[0] * at_p
    out[1] = at_p + mine[3] * at_l
    line.start_all(lambda o: out.at[(me + o) // line.n], got, line.n - 1)


def take_values(line, inverses, out, got, weights):
    u_p = inverses[0] * out[1]
    u_l = inverses[1] * out[0]
    for o, _, source in line.others():
        line.await_one(o, out.at[0], got, line.n - 1)
        v = got[source]
        u_p = u_p + weights[source, 0] * v
        u_l = u_l + weights[source, 1] * v
    return u_p, u_l


def kernel(
    nx, ny, dims,
    u_hbm, kx_hbm, ky_hbm, out_ref,
    u_raw, kx_raw, ky_raw, nat, turned, gx, gy,
    coef_x, kept_x, tree_x, tkept_x, every_x, weights_x, chain_x, mine_x, out_x, got_x,
    coef_y, kept_y, tree_y, tkept_y, every_y, weights_y, chain_y, mine_y, out_y, got_y,
    edge_x_in, edge_y_out, edge_y_in, ends, ports,
    local_sem, xs, xr, ys, yr,
):
    nz, lx, ly = dims
    lanes = 128
    groups = nz * lx // lanes
    bx, by = lx // SUB, ly // SUB
    ix = lax.axis_index("gx")
    iy = lax.axis_index("gy")
    loads = []
    for i, (src, dst) in enumerate(((ky_hbm, ky_raw), (u_hbm, u_raw), (kx_hbm, kx_raw))):
        parts = [
            pltpu.make_async_copy(src.at[:, :, t, :], dst.at[:, t], local_sem.at[i, t]) for t in range(SUB)
        ]
        for part in parts:
            part.start()
        loads.append(parts)
    line_x = Line("gx", nx, ix, xs, xr)
    line_y = Line("gy", ny, iy, ys, yr)
    barrier = pltpu.get_barrier_semaphore()
    for line in (line_x, line_y):
        for _, target, _ in line.others():
            pl.semaphore_signal(barrier, inc=1, device_id={line.axis: target}, device_id_type=MESH)

    planes = lanes // lx

    def arrived(parts):
        for part in parts:
            part.wait()

    def group(ref, g):
        return ref[g * planes : (g + 1) * planes].reshape(lanes, ly)

    def by_block(v):
        ports[...] = v.reshape(nz * bx, ly)
        return jnp.stack([ports[pl.ds(b, nz, stride=bx), :] for b in range(bx)], axis=0)

    def by_plane(v):
        for b in range(bx):
            ports[pl.ds(b, nz, stride=bx), :] = v[b]
        return ports[...].reshape(nz, bx, ly)

    def y_rows(y):
        return turned[pl.ds(y, groups, stride=ly), :]

    hx = 2 * (nx - 1)
    hy = 2 * (ny - 1)

    def edge_x():
        return line_x.copy(kx_hbm.at[:, bx - 1, SUB - 1, :], edge_x_in.at[:, 0, :], hx, jnp.minimum(ix + 1, nx - 1))

    def edge_y_right():
        return line_y.copy(edge_y_out.at[1], edge_y_in.at[0], hy, jnp.minimum(iy + 1, ny - 1))

    def edge_y_left():
        return line_y.copy(edge_y_out.at[0], edge_y_in.at[1], hy + 1, jnp.maximum(iy - 1, 0))

    pl.semaphore_wait(barrier, nx - 1 + ny - 1)

    @pl.when(ix < nx - 1)
    def _():
        edge_x().start()

    lane = lax.broadcasted_iota(jnp.int32, (lanes, ly), 1)
    packed = None
    for kind, (load, raw) in enumerate(((loads[0], ky_raw), (loads[1], u_raw))):
        arrived(load)
        for g in range(groups):
            at = 2 * (kind * groups + g)
            moved = pltpu.roll(group(raw, g), at + 1, 1)
            packed = moved if packed is None else jnp.where(lane >= at, moved, packed)
    ends[...] = packed.T
    for kind in range(2):
        for side in range(2):
            edge_y_out[side, kind] = ends[pl.ds(2 * kind * groups + 1 - side, groups, stride=2), :]

    @pl.when(iy < ny - 1)
    def _():
        edge_y_right().start()

    @pl.when(iy > 0)
    def _():
        edge_y_left().start()

    for g in range(groups):
        turned[g * ly : (g + 1) * ly] = group(ky_raw, g).T
    prior = y_rows(0)
    for y in range(1, ly):
        now = y_rows(y)
        gy[y // SUB, y % SUB] = 0.5 * (prior + now)
        prior = now
    ky_last = prior

    arrived(loads[2])
    for t in range(1, SUB):
        gx[:, t] = 0.5 * (kx_raw[:, t - 1] + kx_raw[:, t])
    kx_ends = kx_raw[:, SUB - 1]
    kx_last = by_block(kx_ends)[bx - 1]

    @pl.when(ix > 0)
    def _():
        edge_x().wait_recv()

    block = lax.broadcasted_iota(jnp.int32, (nz, bx, ly), 1)
    prior = jnp.where(block > 0, pltpu.roll(kx_ends, 1, 1), jnp.where(ix > 0, edge_x_in[...], 0.0))
    gx[:, 0] = 0.5 * (prior + kx_raw[:, 0])
    at_p, series, at_l = factor_tree(*[by_block(v) for v in factor_cells(lambda t: gx[:, t], coef_x)], tree_x)
    at_l = at_l + jnp.where(ix == nx - 1, 0.5 * kx_last, 0.0)
    share_coefs(line_x, (at_p, series, at_l), every_x)

    @pl.when(iy > 0)
    def _():
        edge_y_right().wait_recv()

    @pl.when(iy < ny - 1)
    def _():
        edge_y_left().wait_recv()

    k0, u0, k1, u1 = edge_y_out[0, 0], edge_y_out[0, 1], edge_y_out[1, 0], edge_y_out[1, 1]
    inner, last = iy > 0, iy < ny - 1
    face_0 = 0.5 * (jnp.where(inner, edge_y_in[0, 0], 0.0) + k0)
    gy[0, 0] = face_0
    face_1 = 0.5 * (jnp.where(last, edge_y_in[1, 0], 0.0) + k1)
    flux_0 = face_0 * (jnp.where(inner, edge_y_in[0, 1], 0.0) - u0)
    flux_1 = face_1 * (jnp.where(last, edge_y_in[1, 1], 0.0) - u1)
    ends[pl.ds(0, groups, stride=2), :] = flux_1
    ends[pl.ds(1, groups, stride=2), :] = -flux_0
    fluxes = ends[...].T
    for g in range(groups):
        outer = pltpu.roll(fluxes, (ly - 2 * g - 1) % ly, 1)
        u = group(u_raw, g)
        k = group(ky_raw, g)
        flux = 0.5 * (k + pltpu.roll(k, 1, 1)) * (u - pltpu.roll(u, 1, 1))
        flux = jnp.where(lane > 0, flux, outer)
        later = jnp.where(lane < ly - 1, pltpu.roll(flux, ly - 1, 1), outer)
        nat[g * planes : (g + 1) * planes] = (u + (later - flux)).reshape(planes, SUB, bx, ly)

    await_coefs(line_x, every_x)
    d_p, d_l = down_cells(lambda t: nat[:, t], coef_x, kept_x)
    d_p, d_l = down_tree(by_block(d_p), by_block(d_l), tree_x, tkept_x)
    line_ratios(ix, nx, every_x, chain_x, mine_x)
    send_values(line_x, d_p, d_l, out_x, got_x, mine_x)

    inverses = line_weights(ix, nx, chain_x, mine_x, weights_x)
    at_p, series, at_l = factor_tree(*factor_cells(lambda t: gy[:, t], coef_y), tree_y)
    at_l = at_l + jnp.where(iy == ny - 1, 0.5 * ky_last, 0.0)
    share_coefs(line_y, (at_p, series, at_l), every_y)

    u_p, u_l = take_values(line_x, inverses, out_x, got_x, weights_x)
    before, nodes = up_tree(u_p, u_l, tree_x, tkept_x)

    def put_x(t, v):
        nat[:, t] = v

    up_cells(by_plane(before), by_plane(nodes), coef_x, kept_x, put_x)
    for g in range(groups):
        turned[g * ly : (g + 1) * ly] = (group(nat, g) - group(u_raw, g)).T

    def y_cells(t):
        return jnp.stack([y_rows(b * SUB + t) for b in range(by)], axis=0)

    await_coefs(line_y, every_y)
    d_p, d_l = down_cells(y_cells, coef_y, kept_y)
    d_p, d_l = down_tree(d_p, d_l, tree_y, tkept_y)
    line_ratios(iy, ny, every_y, chain_y, mine_y)
    send_values(line_y, d_p, d_l, out_y, got_y, mine_y)
    inverses = line_weights(iy, ny, chain_y, mine_y, weights_y)
    line_x.done_sending(lambda o: every_x.at[ix], every_x, 0)
    line_x.done_sending(lambda o: out_x.at[0], got_x, nx - 1)
    line_y.done_sending(lambda o: every_y.at[iy], every_y, 0)

    @pl.when(ix < nx - 1)
    def _():
        edge_x().wait_send()

    @pl.when(iy < ny - 1)
    def _():
        edge_y_right().wait_send()

    @pl.when(iy > 0)
    def _():
        edge_y_left().wait_send()

    u_p, u_l = take_values(line_y, inverses, out_y, got_y, weights_y)
    before, nodes = up_tree(u_p, u_l, tree_y, tkept_y)

    def put_y(t, v):
        for b in range(by):
            turned[pl.ds(b * SUB + t, groups, stride=ly), :] = v[b]

    up_cells(before, nodes, coef_y, kept_y, put_y)
    for g in range(groups):
        o = group(u_raw, g) + 2.0 * turned[g * ly : (g + 1) * ly].T
        for p in range(planes):
            for t in range(SUB):
                at = p * lx + t * bx
                out_ref[pl.ds(g * lanes + p * lx + t, bx, stride=SUB), :] = o[at : at + bx]

    line_y.done_sending(lambda o: out_y.at[0], got_y, ny - 1)


def on_device(nx, ny, state, kappa_x, kappa_y):
    nz, lx, ly = state.shape
    groups = nz * lx // 128
    flat = (nz * lx, ly)
    bx, by = lx // SUB, ly // SUB

    def line_scratch(n, blocks, rows, cells):
        one = (rows, 128)
        return [
            pltpu.VMEM((3, SUB - 1) + cells, F32),
            pltpu.VMEM((SUB - 1,) + cells, F32),
            pltpu.VMEM((3, blocks - 1) + one, F32),
            pltpu.VMEM((blocks - 1,) + one, F32),
            pltpu.VMEM((n, 3) + one, F32),
            pltpu.VMEM((n, 2) + one, F32),
            pltpu.VMEM((n, 2) + one, F32),
            pltpu.VMEM((6,) + one, F32),
            pltpu.VMEM((2,) + one, F32),
            pltpu.VMEM((n,) + one, F32),
        ]

    scratch = (
        [pltpu.VMEM((nz, SUB, bx, ly), F32)] * 4
        + [
            pltpu.VMEM(flat, F32),
            pltpu.VMEM((nz, SUB, bx, ly), F32),
            pltpu.VMEM((by, SUB, groups, 128), F32),
        ]
        + line_scratch(nx, bx, nz, (nz, bx, ly))
        + line_scratch(ny, by, groups, (by, groups, 128))
        + [
            pltpu.VMEM((nz, bx, ly), F32),
            pltpu.VMEM((2, 2, groups, 128), F32),
            pltpu.VMEM((2, 2, groups, 128), F32),
            pltpu.VMEM((128, 128), F32),
            pltpu.VMEM((nz * bx, ly), F32),
            pltpu.SemaphoreType.DMA((3, SUB)),
            pltpu.SemaphoreType.DMA((2 * nx - 1,)),
            pltpu.SemaphoreType.DMA((2 * nx - 1,)),
            pltpu.SemaphoreType.DMA((2 * ny,)),
            pltpu.SemaphoreType.DMA((2 * ny,)),
        ]
    )
    out = pl.pallas_call(
        functools.partial(kernel, nx, ny, (nz, lx, ly)),
        out_shape=jax.ShapeDtypeStruct(flat, F32),
        in_specs=[pl.BlockSpec(memory_space=pltpu.HBM)] * 3,
        out_specs=pl.BlockSpec(memory_space=pltpu.VMEM),
        scratch_shapes=scratch,
        compiler_params=pltpu.CompilerParams(
            collective_id=0, has_side_effects=True, vmem_limit_bytes=32 * 1024 * 1024
        ),
    )(*[pltpu.with_memory_space_constraint(v.reshape(nz, bx, SUB, ly), pltpu.HBM) for v in (state, kappa_x, kappa_y)])
    return out.reshape(state.shape)


def solution(mesh):
    spec = P(None, "gx", "gy")
    return jax.shard_map(
        functools.partial(on_device, mesh.shape["gx"], mesh.shape["gy"]),
        mesh=mesh,
        in_specs=(spec, spec, spec),
        out_specs=spec,
        check_vma=False,
    )
```

```python
import functools

import jax
import jax.numpy as jnp
from jax import lax
from jax.experimental import pallas as pl
from jax.experimental.pallas import tpu as pltpu
from jax.sharding import PartitionSpec as P

MESH = pl.DeviceIdType.MESH
F32 = jnp.float32
SUB = 8


def recip(p):
    r = pl.reciprocal(p, approx=True)
    return r * (2.0 - p * r)


def loop(count, body):
    lax.fori_loop(0, count, lambda i, c: (body(i), c)[1], 0)


def factor_cells(face, coef, chunk, ports):
    to_p = face(0)
    s = jnp.ones_like(to_p)
    at_p = jnp.zeros_like(s)
    for t in range(SUB - 1):
        right = face(t + 1)
        r = recip(s + to_p + right)
        a = right * r
        b = to_p * r
        coef[0, t, chunk] = r
        coef[1, t, chunk] = a
        coef[2, t, chunk] = b
        at_p = at_p + s * b
        s = 1.0 + s * a
        to_p = to_p * a
    ports[0, chunk] = at_p
    ports[1, chunk] = to_p
    ports[2, chunk] = s


def halves(v):
    v = v.reshape((v.shape[0] // 2, 2) + v.shape[1:])
    return v[:, 0], v[:, 1]


def factor_tree(at_p, series, at_l, tree):
    level = 0
    at = 0
    while at_p.shape[0] > 1:
        pa, pb = halves(at_p)
        ga, gb = halves(series)
        la, lb = halves(at_l)
        c = la + pb
        r = recip(c + ga + gb)
        a = gb * r
        b = ga * r
        m = r.shape[0]
        tree[0, at : at + m] = r
        tree[1, at : at + m] = a
        tree[2, at : at + m] = b
        at_p = pa + c * b
        at_l = lb + c * a
        series = ga * a
        at += m
        level += 1
    return at_p[0], series[0], at_l[0]


def down_cells(source, coef, kept, chunk, ports):
    d = source(0)
    at_p = None
    for t in range(SUB - 1):
        kept[t, chunk] = d
        share = coef[2, t, chunk] * d
        at_p = share if at_p is None else at_p + share
        d = source(t + 1) + coef[1, t, chunk] * d
    ports[0, chunk] = at_p
    ports[1, chunk] = d


def down_tree(at_p, at_l, tree, kept):
    at = 0
    while at_p.shape[0] > 1:
        pa, pb = halves(at_p)
        la, lb = halves(at_l)
        d = la + pb
        m = d.shape[0]
        kept[at : at + m] = d
        at_p = pa + tree[2, at : at + m] * d
        at_l = lb + tree[1, at : at + m] * d
        at += m
    return at_p[0], at_l[0]


def up_tree(u_p, u_l, tree, kept):
    nodes = u_l[None]
    total = kept.shape[0]
    m = 1
    at = total - 1
    while at >= 0:
        before = u_p[None] if m == 1 else jnp.concatenate([u_p[None], nodes[:-1]], axis=0)
        mid = (
            tree[0, at : at + m] * kept[at : at + m]
            + tree[1, at : at + m] * nodes
            + tree[2, at : at + m] * before
        )
        nodes = jnp.stack([mid, nodes], axis=1).reshape((2 * m,) + nodes.shape[1:])
        m *= 2
        at -= m
    before = jnp.concatenate([u_p[None], nodes[:-1]], axis=0)
    return before, nodes


def up_cells(coef, kept, put, chunk, ports):
    before = ports[0, chunk]
    u = ports[1, chunk]
    put(SUB - 1, u)
    for t in range(SUB - 2, -1, -1):
        u = coef[0, t, chunk] * kept[t, chunk] + coef[1, t, chunk] * u + coef[2, t, chunk] * before
        put(t, u)


def line_ratios(me, n, every, chain, mine):
    zero = jnp.zeros(every.shape[2:], F32)
    ahead = []
    prior = None
    for j in range(n):
        p, g, l = every[j, 0], every[j, 1], every[j, 2]
        if prior is None:
            ahead.append((zero, zero, l + g))
            prior = l + g
        else:
            c = prior + p
            ratio = g * recip(c + g)
            now = l + c * ratio
            ahead.append((ratio, prior, now))
            prior = now
    back = [None] * n
    later = zero
    for j in range(n - 1, -1, -1):
        p, g, l = every[j, 0], every[j, 1], every[j, 2]
        c = later + l
        ratio = g * recip(c + g)
        now = p + c * ratio
        back[j] = (ratio, later, now)
        later = now
    own = [zero] * 6
    for j in range(n):
        here = me == j
        own = [jnp.where(here, v, o) for v, o in zip(ahead[j] + back[j], own)]
        chain[j, 0] = ahead[j][0]
        chain[j, 1] = back[j][0]
    for i, v in enumerate(own):
        mine[i] = v


def line_weights(me, n, chain, mine, weights):
    rho, sf_prior, sf_now, tau, sb_later, sb_now = [mine[i] for i in range(6)]
    zero = jnp.zeros_like(rho)
    inv_l = recip(sf_now + sb_later)
    inv_p = jnp.where(me > 0, recip(sf_prior + sb_now), zero)
    ahead = [None] * n
    w_p, w_l = inv_p, inv_l * rho
    for j in range(n - 1, -1, -1):
        left = me > j
        ahead[j] = (w_p, w_l)
        w_p = jnp.where(left, w_p * chain[j, 0], w_p)
        w_l = jnp.where(left, w_l * chain[j, 0], w_l)
    w_p, w_l = inv_p * tau, inv_l
    for j in range(n):
        left, right = me > j, me < j
        weights[j, 0] = jnp.where(left, ahead[j][0], w_p)
        weights[j, 1] = jnp.where(left, ahead[j][1], w_l)
        w_p = jnp.where(right, w_p * chain[j, 1], w_p)
        w_l = jnp.where(right, w_l * chain[j, 1], w_l)
    return inv_p, inv_l


class Line:
    def __init__(self, axis, n, me, send, recv):
        self.axis, self.n, self.me, self.send, self.recv = axis, n, me, send, recv

    def copy(self, src, dst, slot, target):
        return pltpu.make_async_remote_copy(
            src_ref=src,
            dst_ref=dst,
            send_sem=self.send.at[slot],
            recv_sem=self.recv.at[slot],
            device_id={self.axis: target},
            device_id_type=MESH,
        )

    def others(self):
        for o in range(1, self.n):
            yield o, lax.rem(self.me + o, self.n), lax.rem(self.me + self.n - o, self.n)

    def start_all(self, src_of, buf, base):
        for o, target, _ in self.others():
            self.copy(src_of(o), buf.at[self.me], base + o - 1, target).start()

    def await_one(self, o, src, buf, base):
        source = lax.rem(self.me + self.n - o, self.n)
        self.copy(src, buf.at[source], base + o - 1, source).wait_recv()

    def done_sending(self, src_of, buf, base):
        for o, target, _ in self.others():
            self.copy(src_of(o), buf.at[self.me], base + o - 1, target).wait_send()


def share_coefs(line, mine, every):
    for i, v in enumerate(mine):
        every[line.me, i] = v
    line.start_all(lambda o: every.at[line.me], every, 0)


def await_coefs(line, every):
    for o, _, _ in line.others():
        line.await_one(o, every.at[line.me], every, 0)


def send_values(line, at_p, at_l, out, got, mine):
    me = line.me
    out[0] = at_l + mine[0] * at_p
    out[1] = at_p + mine[3] * at_l
    line.start_all(lambda o: out.at[(me + o) // line.n], got, line.n - 1)


def take_values(line, inverses, out, got, weights):
    u_p = inverses[0] * out[1]
    u_l = inverses[1] * out[0]
    for o, _, source in line.others():
        line.await_one(o, out.at[0], got, line.n - 1)
        v = got[source]
        u_p = u_p + weights[source, 0] * v
        u_l = u_l + weights[source, 1] * v
    return u_p, u_l


def kernel(
    nx, ny, dims,
    u_hbm, kx_hbm, ky_hbm, out_ref,
    u_raw, kx_raw, ky_raw, nat, turned, k_before, ports_x, ports_y,
    coef_x, kept_x, tree_x, tkept_x, every_x, weights_x, chain_x, mine_x, out_x, got_x,
    coef_y, kept_y, tree_y, tkept_y, every_y, weights_y, chain_y, mine_y, out_y, got_y,
    edge_x_in, edge_y_out, edge_y_in, ends,
    local_sem, xs, xr, ys, yr,
):
    nz, lx, ly = dims
    lanes = 128
    groups = nz * lx // lanes
    bx, by = lx // SUB, ly // SUB
    ix = lax.axis_index("gx")
    iy = lax.axis_index("gy")
    loads = []
    for i, (src, dst) in enumerate(((ky_hbm, ky_raw), (u_hbm, u_raw), (kx_hbm, kx_raw))):
        parts = [
            pltpu.make_async_copy(src.at[:, :, t, :], dst.at[:, t], local_sem.at[i, t]) for t in range(SUB)
        ]
        for part in parts:
            part.start()
        loads.append(parts)
    line_x = Line("gx", nx, ix, xs, xr)
    line_y = Line("gy", ny, iy, ys, yr)
    barrier = pltpu.get_barrier_semaphore()
    for line in (line_x, line_y):
        for _, target, _ in line.others():
            pl.semaphore_signal(barrier, inc=1, device_id={line.axis: target}, device_id_type=MESH)

    planes = lanes // lx

    def arrived(parts):
        for part in parts:
            part.wait()

    def group(ref, g):
        return ref[pl.ds(g * planes, planes)].reshape(lanes, ly)

    def by_block(i):
        rows = ports_x.at[i].reshape(nz * bx, ly)
        return jnp.stack([rows[pl.ds(b, nz, stride=bx), :] for b in range(bx)], axis=0)

    def by_plane(i, v):
        rows = ports_x.at[i].reshape(nz * bx, ly)
        for b in range(bx):
            rows[pl.ds(b, nz, stride=bx), :] = v[b]

    def chunks(total, parts):
        size = total // parts
        return lambda c: pl.ds(c * size, size)

    x2, x4 = chunks(nz, 2), chunks(nz, 4)
    y2, y4 = chunks(by, 2), chunks(by, 4)

    def y_cells(c, parts, t):
        size = by // parts
        return jnp.stack(
            [turned[pl.ds((c * size + b) * SUB + t, groups, stride=ly), :] for b in range(size)], axis=0
        )

    def y_rows(y):
        return turned[pl.ds(y, groups, stride=ly), :]

    hx = 2 * (nx - 1)
    hy = 2 * (ny - 1)

    def edge_x():
        return line_x.copy(kx_hbm.at[:, bx - 1, SUB - 1, :], edge_x_in.at[:, 0, :], hx, jnp.minimum(ix + 1, nx - 1))

    def edge_y_right():
        return line_y.copy(edge_y_out.at[1], edge_y_in.at[0], hy, jnp.minimum(iy + 1, ny - 1))

    def edge_y_left():
        return line_y.copy(edge_y_out.at[0], edge_y_in.at[1], hy + 1, jnp.maximum(iy - 1, 0))

    pl.semaphore_wait(barrier, nx - 1 + ny - 1)

    @pl.when(ix < nx - 1)
    def _():
        edge_x().start()

    lane = lax.broadcasted_iota(jnp.int32, (lanes, ly), 1)
    ends[...] = jnp.zeros_like(ends)
    for kind, (load, raw) in enumerate(((loads[0], ky_raw), (loads[1], u_raw))):
        arrived(load)

        def pack(g, packed):
            at = 2 * (kind * groups + g)
            return jnp.where(lane >= at, pltpu.roll(group(raw, g), at + 1, 1), packed)

        packed = lax.fori_loop(0, groups, pack, ends[...])
        ends[...] = packed
    ends[...] = ends[...].T
    for kind in range(2):
        for side in range(2):
            edge_y_out[side, kind] = ends[pl.ds(2 * kind * groups + 1 - side, groups, stride=2), :]

    @pl.when(iy < ny - 1)
    def _():
        edge_y_right().start()

    @pl.when(iy > 0)
    def _():
        edge_y_left().start()

    def turn_k(g):
        turned[pl.ds(pl.multiple_of(g * ly, ly), ly), :] = group(ky_raw, g).T

    loop(groups, turn_k)
    ky_last = y_rows(ly - 1)
    for b in range(1, by):
        k_before[b] = y_rows(b * SUB - 1)

    arrived(loads[2])
    @pl.when(ix > 0)
    def _():
        edge_x().wait_recv()

    block = lax.broadcasted_iota(jnp.int32, (nz // 2, bx, ly), 1)

    def factor_x(c):
        k = [kx_raw[x2(c), t] for t in range(SUB)]
        prior = jnp.where(block > 0, pltpu.roll(k[SUB - 1], 1, 1), jnp.where(ix > 0, edge_x_in[x2(c)], 0.0))
        factor_cells(lambda t: 0.5 * ((k[t - 1] if t else prior) + k[t]), coef_x, x2(c), ports_x)
        ports_x[3, x2(c)] = k[SUB - 1]

    loop(2, factor_x)
    at_p, series, at_l = factor_tree(by_block(0), by_block(1), by_block(2), tree_x)
    kx_last = ports_x.at[3].reshape(nz * bx, ly)[pl.ds(bx - 1, nz, stride=bx), :]
    at_l = at_l + jnp.where(ix == nx - 1, 0.5 * kx_last, 0.0)
    share_coefs(line_x, (at_p, series, at_l), every_x)

    @pl.when(iy > 0)
    def _():
        edge_y_right().wait_recv()

    @pl.when(iy < ny - 1)
    def _():
        edge_y_left().wait_recv()

    k0, u0, k1, u1 = edge_y_out[0, 0], edge_y_out[0, 1], edge_y_out[1, 0], edge_y_out[1, 1]
    inner, last = iy > 0, iy < ny - 1
    face_0 = 0.5 * (jnp.where(inner, edge_y_in[0, 0], 0.0) + k0)
    k_before[0] = jnp.where(inner, edge_y_in[0, 0], 0.0)
    face_1 = 0.5 * (jnp.where(last, edge_y_in[1, 0], 0.0) + k1)
    flux_0 = face_0 * (jnp.where(inner, edge_y_in[0, 1], 0.0) - u0)
    flux_1 = face_1 * (jnp.where(last, edge_y_in[1, 1], 0.0) - u1)
    ends[pl.ds(0, groups, stride=2), :] = flux_1
    ends[pl.ds(1, groups, stride=2), :] = -flux_0
    fluxes = ends[...].T

    def sources(g):
        outer = pltpu.roll(fluxes, ly - 2 * g - 1, 1)
        u = group(u_raw, g)
        k = group(ky_raw, g)
        flux = 0.5 * (k + pltpu.roll(k, 1, 1)) * (u - pltpu.roll(u, 1, 1))
        flux = jnp.where(lane > 0, flux, outer)
        later = jnp.where(lane < ly - 1, pltpu.roll(flux, ly - 1, 1), outer)
        nat[pl.ds(g * planes, planes)] = (u + (later - flux)).reshape(planes, SUB, bx, ly)

    loop(groups, sources)
    await_coefs(line_x, every_x)
    loop(4, lambda c: down_cells(lambda t: nat[x4(c), t], coef_x, kept_x, x4(c), ports_x))
    d_p, d_l = down_tree(by_block(0), by_block(1), tree_x, tkept_x)
    line_ratios(ix, nx, every_x, chain_x, mine_x)
    send_values(line_x, d_p, d_l, out_x, got_x, mine_x)

    inverses = line_weights(ix, nx, chain_x, mine_x, weights_x)

    def factor_y(c):
        def face(t):
            prior = y_cells(c, 2, t - 1) if t else k_before[y2(c)]
            return 0.5 * (prior + y_cells(c, 2, t))

        factor_cells(face, coef_y, y2(c), ports_y)

    loop(2, factor_y)
    at_p, series, at_l = factor_tree(ports_y[0], ports_y[1], ports_y[2], tree_y)
    at_l = at_l + jnp.where(iy == ny - 1, 0.5 * ky_last, 0.0)
    share_coefs(line_y, (at_p, series, at_l), every_y)

    u_p, u_l = take_values(line_x, inverses, out_x, got_x, weights_x)
    before, nodes = up_tree(u_p, u_l, tree_x, tkept_x)

    by_plane(0, before)
    by_plane(1, nodes)

    def up_x(c):
        def put(t, v):
            nat[x4(c), t] = v

        up_cells(coef_x, kept_x, put, x4(c), ports_x)

    loop(4, up_x)

    def turn_q(g):
        turned[pl.ds(pl.multiple_of(g * ly, ly), ly), :] = (group(nat, g) - group(u_raw, g)).T

    loop(groups, turn_q)
    await_coefs(line_y, every_y)
    loop(4, lambda c: down_cells(lambda t: y_cells(c, 4, t), coef_y, kept_y, y4(c), ports_y))
    d_p, d_l = down_tree(ports_y[0], ports_y[1], tree_y, tkept_y)
    line_ratios(iy, ny, every_y, chain_y, mine_y)
    send_values(line_y, d_p, d_l, out_y, got_y, mine_y)
    inverses = line_weights(iy, ny, chain_y, mine_y, weights_y)
    line_x.done_sending(lambda o: every_x.at[ix], every_x, 0)
    line_x.done_sending(lambda o: out_x.at[0], got_x, nx - 1)
    line_y.done_sending(lambda o: every_y.at[iy], every_y, 0)

    @pl.when(ix < nx - 1)
    def _():
        edge_x().wait_send()

    @pl.when(iy < ny - 1)
    def _():
        edge_y_right().wait_send()

    @pl.when(iy > 0)
    def _():
        edge_y_left().wait_send()

    u_p, u_l = take_values(line_y, inverses, out_y, got_y, weights_y)
    before, nodes = up_tree(u_p, u_l, tree_y, tkept_y)

    ports_y[0] = before
    ports_y[1] = nodes

    def up_y(c):
        def put(t, v):
            size = by // 4
            for b in range(size):
                turned[pl.ds((c * size + b) * SUB + t, groups, stride=ly), :] = v[b]

        up_cells(coef_y, kept_y, put, y4(c), ports_y)

    loop(4, up_y)

    def finish(g):
        w = turned[pl.ds(pl.multiple_of(g * ly, ly), ly), :].T
        o = group(u_raw, g) + 2.0 * w
        for p in range(planes):
            for t in range(SUB):
                at = p * lx + t * bx
                out_ref[pl.ds(g * lanes + p * lx + t, bx, stride=SUB), :] = o[at : at + bx]

    loop(groups, finish)
    line_y.done_sending(lambda o: out_y.at[0], got_y, ny - 1)


def on_device(nx, ny, state, kappa_x, kappa_y):
    nz, lx, ly = state.shape
    groups = nz * lx // 128
    flat = (nz * lx, ly)
    bx, by = lx // SUB, ly // SUB

    def line_scratch(n, blocks, rows, cells):
        one = (rows, 128)
        return [
            pltpu.VMEM((3, SUB - 1) + cells, F32),
            pltpu.VMEM((SUB - 1,) + cells, F32),
            pltpu.VMEM((3, blocks - 1) + one, F32),
            pltpu.VMEM((blocks - 1,) + one, F32),
            pltpu.VMEM((n, 3) + one, F32),
            pltpu.VMEM((n, 2) + one, F32),
            pltpu.VMEM((n, 2) + one, F32),
            pltpu.VMEM((6,) + one, F32),
            pltpu.VMEM((2,) + one, F32),
            pltpu.VMEM((n,) + one, F32),
        ]

    scratch = (
        [pltpu.VMEM((nz, SUB, bx, ly), F32)] * 4
        + [
            pltpu.VMEM(flat, F32),
            pltpu.VMEM((by, groups, 128), F32),
            pltpu.VMEM((4, nz, bx, ly), F32),
            pltpu.VMEM((3, by, groups, 128), F32),
        ]
        + line_scratch(nx, bx, nz, (nz, bx, ly))
        + line_scratch(ny, by, groups, (by, groups, 128))
        + [
            pltpu.VMEM((nz, bx, ly), F32),
            pltpu.VMEM((2, 2, groups, 128), F32),
            pltpu.VMEM((2, 2, groups, 128), F32),
            pltpu.VMEM((128, 128), F32),
            pltpu.SemaphoreType.DMA((3, SUB)),
            pltpu.SemaphoreType.DMA((2 * nx - 1,)),
            pltpu.SemaphoreType.DMA((2 * nx - 1,)),
            pltpu.SemaphoreType.DMA((2 * ny,)),
            pltpu.SemaphoreType.DMA((2 * ny,)),
        ]
    )
    out = pl.pallas_call(
        functools.partial(kernel, nx, ny, (nz, lx, ly)),
        out_shape=jax.ShapeDtypeStruct(flat, F32),
        in_specs=[pl.BlockSpec(memory_space=pltpu.HBM)] * 3,
        out_specs=pl.BlockSpec(memory_space=pltpu.VMEM),
        scratch_shapes=scratch,
        compiler_params=pltpu.CompilerParams(
            collective_id=0, has_side_effects=True, vmem_limit_bytes=32 * 1024 * 1024
        ),
    )(*[pltpu.with_memory_space_constraint(v.reshape(nz, bx, SUB, ly), pltpu.HBM) for v in (state, kappa_x, kappa_y)])
    return out.reshape(state.shape)


def solution(mesh):
    spec = P(None, "gx", "gy")
    return jax.shard_map(
        functools.partial(on_device, mesh.shape["gx"], mesh.shape["gy"]),
        mesh=mesh,
        in_specs=(spec, spec, spec),
        out_specs=spec,
        check_vma=False,
    )
```

```python
import functools

import jax
import jax.numpy as jnp
from jax import lax
from jax.experimental import pallas as pl
from jax.experimental.pallas import tpu as pltpu
from jax.sharding import PartitionSpec as P

MESH = pl.DeviceIdType.MESH
F32 = jnp.float32
SUB = 8


def recip(p):
    r = pl.reciprocal(p, approx=True)
    return r * (2.0 - p * r)


def factor_cells(face, coef):
    s = jnp.ones_like(face(0))
    to_p = face(0)
    at_p = jnp.zeros_like(s)
    for t in range(SUB - 1):
        right = face(t + 1)
        r = recip(s + to_p + right)
        a = right * r
        b = to_p * r
        coef[0, t] = r
        coef[1, t] = a
        coef[2, t] = b
        at_p = at_p + s * b
        s = 1.0 + s * a
        to_p = to_p * a
    return at_p, to_p, s


def halves(v):
    v = v.reshape((v.shape[0] // 2, 2) + v.shape[1:])
    return v[:, 0], v[:, 1]


def factor_tree(at_p, series, at_l, tree):
    level = 0
    at = 0
    while at_p.shape[0] > 1:
        pa, pb = halves(at_p)
        ga, gb = halves(series)
        la, lb = halves(at_l)
        c = la + pb
        r = recip(c + ga + gb)
        a = gb * r
        b = ga * r
        m = r.shape[0]
        tree[0, at : at + m] = r
        tree[1, at : at + m] = a
        tree[2, at : at + m] = b
        at_p = pa + c * b
        at_l = lb + c * a
        series = ga * a
        at += m
        level += 1
    return at_p[0], series[0], at_l[0]


def down_cells(source, coef, kept):
    d = source(0)
    at_p = None
    for t in range(SUB - 1):
        kept[t] = d
        share = coef[2, t] * d
        at_p = share if at_p is None else at_p + share
        d = source(t + 1) + coef[1, t] * d
    return at_p, d


def down_tree(at_p, at_l, tree, kept):
    at = 0
    while at_p.shape[0] > 1:
        pa, pb = halves(at_p)
        la, lb = halves(at_l)
        d = la + pb
        m = d.shape[0]
        kept[at : at + m] = d
        at_p = pa + tree[2, at : at + m] * d
        at_l = lb + tree[1, at : at + m] * d
        at += m
    return at_p[0], at_l[0]


def up_tree(u_p, u_l, tree, kept):
    nodes = u_l[None]
    total = kept.shape[0]
    m = 1
    at = total - 1
    while at >= 0:
        before = u_p[None] if m == 1 else jnp.concatenate([u_p[None], nodes[:-1]], axis=0)
        mid = (
            tree[0, at : at + m] * kept[at : at + m]
            + tree[1, at : at + m] * nodes
            + tree[2, at : at + m] * before
        )
        nodes = jnp.stack([mid, nodes], axis=1).reshape((2 * m,) + nodes.shape[1:])
        m *= 2
        at -= m
    before = jnp.concatenate([u_p[None], nodes[:-1]], axis=0)
    return before, nodes


def up_cells(before, nodes, coef, kept, put):
    u = nodes
    put(SUB - 1, u)
    for t in range(SUB - 2, -1, -1):
        u = coef[0, t] * kept[t] + coef[1, t] * u + coef[2, t] * before
        put(t, u)


def line_ratios(me, n, every, chain, mine):
    zero = jnp.zeros(every.shape[2:], F32)
    ahead = []
    prior = None
    for j in range(n):
        p, g, l = every[j, 0], every[j, 1], every[j, 2]
        if prior is None:
            ahead.append((zero, zero, l + g))
            prior = l + g
        else:
            c = prior + p
            ratio = g * recip(c + g)
            now = l + c * ratio
            ahead.append((ratio, prior, now))
            prior = now
    back = [None] * n
    later = zero
    for j in range(n - 1, -1, -1):
        p, g, l = every[j, 0], every[j, 1], every[j, 2]
        c = later + l
        ratio = g * recip(c + g)
        now = p + c * ratio
        back[j] = (ratio, later, now)
        later = now
    own = [zero] * 6
    for j in range(n):
        here = me == j
        own = [jnp.where(here, v, o) for v, o in zip(ahead[j] + back[j], own)]
        chain[j, 0] = ahead[j][0]
        chain[j, 1] = back[j][0]
    for i, v in enumerate(own):
        mine[i] = v


def line_weights(me, n, chain, mine, weights):
    rho, sf_prior, sf_now, tau, sb_later, sb_now = [mine[i] for i in range(6)]
    zero = jnp.zeros_like(rho)
    inv_l = recip(sf_now + sb_later)
    inv_p = jnp.where(me > 0, recip(sf_prior + sb_now), zero)
    ahead = [None] * n
    w_p, w_l = inv_p, inv_l * rho
    for j in range(n - 1, -1, -1):
        left = me > j
        ahead[j] = (w_p, w_l)
        w_p = jnp.where(left, w_p * chain[j, 0], w_p)
        w_l = jnp.where(left, w_l * chain[j, 0], w_l)
    w_p, w_l = inv_p * tau, inv_l
    for j in range(n):
        left, right = me > j, me < j
        weights[j, 0] = jnp.where(left, ahead[j][0], w_p)
        weights[j, 1] = jnp.where(left, ahead[j][1], w_l)
        w_p = jnp.where(right, w_p * chain[j, 1], w_p)
        w_l = jnp.where(right, w_l * chain[j, 1], w_l)
    return inv_p, inv_l


class Line:
    def __init__(self, axis, n, me, send, recv):
        self.axis, self.n, self.me, self.send, self.recv = axis, n, me, send, recv

    def copy(self, src, dst, slot, target):
        return pltpu.make_async_remote_copy(
            src_ref=src,
            dst_ref=dst,
            send_sem=self.send.at[slot],
            recv_sem=self.recv.at[slot],
            device_id={self.axis: target},
            device_id_type=MESH,
        )

    def others(self):
        for o in range(1, self.n):
            yield o, lax.rem(self.me + o, self.n), lax.rem(self.me + self.n - o, self.n)

    def start_all(self, src_of, buf, base):
        for o, target, _ in self.others():
            self.copy(src_of(o), buf.at[self.me], base + o - 1, target).start()

    def await_one(self, o, src, buf, base):
        source = lax.rem(self.me + self.n - o, self.n)
        self.copy(src, buf.at[source], base + o - 1, source).wait_recv()

    def done_sending(self, src_of, buf, base):
        for o, target, _ in self.others():
            self.copy(src_of(o), buf.at[self.me], base + o - 1, target).wait_send()


def share_coefs(line, mine, every):
    for i, v in enumerate(mine):
        every[line.me, i] = v
    line.start_all(lambda o: every.at[line.me], every, 0)


def await_coefs(line, every):
    for o, _, _ in line.others():
        line.await_one(o, every.at[line.me], every, 0)


def send_values(line, at_p, at_l, out, got, mine):
    me = line.me
    out[0] = at_l + mine[0] * at_p
    out[1] = at_p + mine[3] * at_l
    line.start_all(lambda o: out.at[(me + o) // line.n], got, line.n - 1)


def take_values(line, inverses, out, got, weights):
    u_p = inverses[0] * out[1]
    u_l = inverses[1] * out[0]
    for o, _, source in line.others():
        line.await_one(o, out.at[0], got, line.n - 1)
        v = got[source]
        u_p = u_p + weights[source, 0] * v
        u_l = u_l + weights[source, 1] * v
    return u_p, u_l


def kernel(
    nx, ny, dims,
    u_hbm, kx_hbm, ky_hbm, out_ref,
    u_raw, kx_raw, ky_raw, nat, turned, gx, gy,
    coef_x, kept_x, tree_x, tkept_x, every_x, weights_x, chain_x, mine_x, out_x, got_x,
    coef_y, kept_y, tree_y, tkept_y, every_y, weights_y, chain_y, mine_y, out_y, got_y,
    edge_x_in, edge_y_out, edge_y_in, ends,
    local_sem, xs, xr, ys, yr,
):
    nz, lx, ly = dims
    lanes = 128
    groups = nz * lx // lanes
    bx, by = lx // SUB, ly // SUB
    ix = lax.axis_index("gx")
    iy = lax.axis_index("gy")
    loads = []
    for i, (src, dst) in enumerate(((ky_hbm, ky_raw), (u_hbm, u_raw), (kx_hbm, kx_raw))):
        cp = pltpu.make_async_copy(src, dst, local_sem.at[i])
        cp.start()
        loads.append(cp)
    line_x = Line("gx", nx, ix, xs, xr)
    line_y = Line("gy", ny, iy, ys, yr)
    barrier = pltpu.get_barrier_semaphore()
    for line in (line_x, line_y):
        for _, target, _ in line.others():
            pl.semaphore_signal(barrier, inc=1, device_id={line.axis: target}, device_id_type=MESH)

    def group(ref, g):
        return ref[g * lanes : (g + 1) * lanes]

    def x_rows(ref, x):
        return ref[pl.ds(x, nz, stride=lx), :]

    def y_rows(y):
        return turned[pl.ds(y, groups, stride=ly), :]

    hx = 2 * (nx - 1)
    hy = 2 * (ny - 1)

    def edge_x():
        return line_x.copy(kx_hbm.reshape(nz, lx, ly).at[:, lx - 1, :], edge_x_in, hx, jnp.minimum(ix + 1, nx - 1))

    def edge_y_right():
        return line_y.copy(edge_y_out.at[1], edge_y_in.at[0], hy, jnp.minimum(iy + 1, ny - 1))

    def edge_y_left():
        return line_y.copy(edge_y_out.at[0], edge_y_in.at[1], hy + 1, jnp.maximum(iy - 1, 0))

    pl.semaphore_wait(barrier, nx - 1 + ny - 1)

    @pl.when(ix < nx - 1)
    def _():
        edge_x().start()

    lane = lax.broadcasted_iota(jnp.int32, (lanes, ly), 1)
    packed = None
    for kind, (load, raw) in enumerate(((loads[0], ky_raw), (loads[1], u_raw))):
        load.wait()
        for g in range(groups):
            at = 2 * (kind * groups + g)
            moved = pltpu.roll(group(raw, g), at + 1, 1)
            packed = moved if packed is None else jnp.where(lane >= at, moved, packed)
    ends[...] = packed.T
    for kind in range(2):
        for side in range(2):
            edge_y_out[side, kind] = ends[pl.ds(2 * kind * groups + 1 - side, groups, stride=2), :]

    @pl.when(iy < ny - 1)
    def _():
        edge_y_right().start()

    @pl.when(iy > 0)
    def _():
        edge_y_left().start()

    for g in range(groups):
        turned[g * ly : (g + 1) * ly] = group(ky_raw, g).T
    prior = y_rows(0)
    for y in range(1, ly):
        now = y_rows(y)
        gy[y // SUB, y % SUB] = 0.5 * (prior + now)
        prior = now
    ky_last = prior

    loads[2].wait()
    kx_first = x_rows(kx_raw, 0)
    kx_last = x_rows(kx_raw, lx - 1)
    prior = kx_first
    for x in range(1, lx):
        now = x_rows(kx_raw, x)
        gx[x // SUB, x % SUB] = 0.5 * (prior + now)
        prior = now

    @pl.when(ix > 0)
    def _():
        edge_x().wait_recv()

    gx[0, 0] = 0.5 * (jnp.where(ix > 0, edge_x_in[...], 0.0) + kx_first)
    at_p, series, at_l = factor_tree(*factor_cells(lambda t: gx[:, t], coef_x), tree_x)
    at_l = at_l + jnp.where(ix == nx - 1, 0.5 * kx_last, 0.0)
    share_coefs(line_x, (at_p, series, at_l), every_x)

    @pl.when(iy > 0)
    def _():
        edge_y_right().wait_recv()

    @pl.when(iy < ny - 1)
    def _():
        edge_y_left().wait_recv()

    k0, u0, k1, u1 = edge_y_out[0, 0], edge_y_out[0, 1], edge_y_out[1, 0], edge_y_out[1, 1]
    inner, last = iy > 0, iy < ny - 1
    face_0 = 0.5 * (jnp.where(inner, edge_y_in[0, 0], 0.0) + k0)
    gy[0, 0] = face_0
    face_1 = 0.5 * (jnp.where(last, edge_y_in[1, 0], 0.0) + k1)
    flux_0 = face_0 * (jnp.where(inner, edge_y_in[0, 1], 0.0) - u0)
    flux_1 = face_1 * (jnp.where(last, edge_y_in[1, 1], 0.0) - u1)
    ends[pl.ds(0, groups, stride=2), :] = flux_1
    ends[pl.ds(1, groups, stride=2), :] = -flux_0
    fluxes = ends[...].T
    for g in range(groups):
        outer = pltpu.roll(fluxes, (ly - 2 * g - 1) % ly, 1)
        u = group(u_raw, g)
        k = group(ky_raw, g)
        flux = 0.5 * (k + pltpu.roll(k, 1, 1)) * (u - pltpu.roll(u, 1, 1))
        flux = jnp.where(lane > 0, flux, outer)
        later = jnp.where(lane < ly - 1, pltpu.roll(flux, ly - 1, 1), outer)
        nat[g * lanes : (g + 1) * lanes] = u + (later - flux)

    def x_cells(t):
        return jnp.stack([x_rows(nat, b * SUB + t) for b in range(bx)], axis=0)

    d_p, d_l = down_cells(x_cells, coef_x, kept_x)
    d_p, d_l = down_tree(d_p, d_l, tree_x, tkept_x)
    await_coefs(line_x, every_x)
    line_ratios(ix, nx, every_x, chain_x, mine_x)
    send_values(line_x, d_p, d_l, out_x, got_x, mine_x)

    inverses = line_weights(ix, nx, chain_x, mine_x, weights_x)
    at_p, series, at_l = factor_tree(*factor_cells(lambda t: gy[:, t], coef_y), tree_y)
    at_l = at_l + jnp.where(iy == ny - 1, 0.5 * ky_last, 0.0)
    share_coefs(line_y, (at_p, series, at_l), every_y)

    u_p, u_l = take_values(line_x, inverses, out_x, got_x, weights_x)
    before, nodes = up_tree(u_p, u_l, tree_x, tkept_x)

    def put_x(t, v):
        for b in range(bx):
            nat[pl.ds(b * SUB + t, nz, stride=lx), :] = v[b]

    up_cells(before, nodes, coef_x, kept_x, put_x)
    for g in range(groups):
        turned[g * ly : (g + 1) * ly] = (group(nat, g) - group(u_raw, g)).T

    def y_cells(t):
        return jnp.stack([y_rows(b * SUB + t) for b in range(by)], axis=0)

    await_coefs(line_y, every_y)
    d_p, d_l = down_cells(y_cells, coef_y, kept_y)
    d_p, d_l = down_tree(d_p, d_l, tree_y, tkept_y)
    line_ratios(iy, ny, every_y, chain_y, mine_y)
    send_values(line_y, d_p, d_l, out_y, got_y, mine_y)
    inverses = line_weights(iy, ny, chain_y, mine_y, weights_y)
    line_x.done_sending(lambda o: every_x.at[ix], every_x, 0)
    line_x.done_sending(lambda o: out_x.at[0], got_x, nx - 1)
    line_y.done_sending(lambda o: every_y.at[iy], every_y, 0)

    @pl.when(ix < nx - 1)
    def _():
        edge_x().wait_send()

    @pl.when(iy < ny - 1)
    def _():
        edge_y_right().wait_send()

    @pl.when(iy > 0)
    def _():
        edge_y_left().wait_send()

    u_p, u_l = take_values(line_y, inverses, out_y, got_y, weights_y)
    before, nodes = up_tree(u_p, u_l, tree_y, tkept_y)

    def put_y(t, v):
        for b in range(by):
            turned[pl.ds(b * SUB + t, groups, stride=ly), :] = v[b]

    up_cells(before, nodes, coef_y, kept_y, put_y)
    for g in range(groups):
        out_ref[g * lanes : (g + 1) * lanes] = group(u_raw, g) + 2.0 * turned[g * ly : (g + 1) * ly].T

    line_y.done_sending(lambda o: out_y.at[0], got_y, ny - 1)


def on_device(nx, ny, state, kappa_x, kappa_y):
    nz, lx, ly = state.shape
    groups = nz * lx // 128
    flat = (nz * lx, ly)
    bx, by = lx // SUB, ly // SUB

    def line_scratch(n, blocks, rows):
        one = (rows, 128)
        return [
            pltpu.VMEM((3, SUB - 1, blocks) + one, F32),
            pltpu.VMEM((SUB - 1, blocks) + one, F32),
            pltpu.VMEM((3, blocks - 1) + one, F32),
            pltpu.VMEM((blocks - 1,) + one, F32),
            pltpu.VMEM((n, 3) + one, F32),
            pltpu.VMEM((n, 2) + one, F32),
            pltpu.VMEM((n, 2) + one, F32),
            pltpu.VMEM((6,) + one, F32),
            pltpu.VMEM((2,) + one, F32),
            pltpu.VMEM((n,) + one, F32),
        ]

    scratch = (
        [pltpu.VMEM(flat, F32)] * 5
        + [
            pltpu.VMEM((bx, SUB, nz, ly), F32),
            pltpu.VMEM((by, SUB, groups, 128), F32),
        ]
        + line_scratch(nx, bx, nz)
        + line_scratch(ny, by, groups)
        + [
            pltpu.VMEM((nz, ly), F32),
            pltpu.VMEM((2, 2, groups, 128), F32),
            pltpu.VMEM((2, 2, groups, 128), F32),
            pltpu.VMEM((128, 128), F32),
            pltpu.SemaphoreType.DMA((3,)),
            pltpu.SemaphoreType.DMA((2 * nx - 1,)),
            pltpu.SemaphoreType.DMA((2 * nx - 1,)),
            pltpu.SemaphoreType.DMA((2 * ny,)),
            pltpu.SemaphoreType.DMA((2 * ny,)),
        ]
    )
    out = pl.pallas_call(
        functools.partial(kernel, nx, ny, (nz, lx, ly)),
        out_shape=jax.ShapeDtypeStruct(flat, F32),
        in_specs=[pl.BlockSpec(memory_space=pltpu.HBM)] * 3,
        out_specs=pl.BlockSpec(memory_space=pltpu.VMEM),
        scratch_shapes=scratch,
        compiler_params=pltpu.CompilerParams(
            collective_id=0, has_side_effects=True, vmem_limit_bytes=32 * 1024 * 1024
        ),
    )(*[pltpu.with_memory_space_constraint(v.reshape(flat), pltpu.HBM) for v in (state, kappa_x, kappa_y)])
    return out.reshape(state.shape)


def solution(mesh):
    spec = P(None, "gx", "gy")
    return jax.shard_map(
        functools.partial(on_device, mesh.shape["gx"], mesh.shape["gy"]),
        mesh=mesh,
        in_specs=(spec, spec, spec),
        out_specs=spec,
        check_vma=False,
    )
```

```python
import functools

import jax
import jax.numpy as jnp
from jax import lax
from jax.experimental import pallas as pl
from jax.experimental.pallas import tpu as pltpu
from jax.sharding import PartitionSpec as P

MESH = pl.DeviceIdType.MESH
F32 = jnp.float32
SUB = 8


def recip(p):
    r = pl.reciprocal(p, approx=True)
    return r * (2.0 - p * r)


def factor_cells(face, coef):
    s = jnp.ones_like(face(0))
    to_p = face(0)
    at_p = jnp.zeros_like(s)
    for t in range(SUB - 1):
        right = face(t + 1)
        r = recip(s + to_p + right)
        a = right * r
        b = to_p * r
        coef[0, t] = r
        coef[1, t] = a
        coef[2, t] = b
        at_p = at_p + s * b
        s = 1.0 + s * a
        to_p = to_p * a
    return at_p, to_p, s


def halves(v):
    v = v.reshape((v.shape[0] // 2, 2) + v.shape[1:])
    return v[:, 0], v[:, 1]


def factor_tree(at_p, series, at_l, tree):
    level = 0
    at = 0
    while at_p.shape[0] > 1:
        pa, pb = halves(at_p)
        ga, gb = halves(series)
        la, lb = halves(at_l)
        c = la + pb
        r = recip(c + ga + gb)
        a = gb * r
        b = ga * r
        m = r.shape[0]
        tree[0, at : at + m] = r
        tree[1, at : at + m] = a
        tree[2, at : at + m] = b
        at_p = pa + c * b
        at_l = lb + c * a
        series = ga * a
        at += m
        level += 1
    return at_p[0], series[0], at_l[0]


def down_cells(source, coef, kept):
    d = source(0)
    at_p = None
    for t in range(SUB - 1):
        kept[t] = d
        share = coef[2, t] * d
        at_p = share if at_p is None else at_p + share
        d = source(t + 1) + coef[1, t] * d
    return at_p, d


def down_tree(at_p, at_l, tree, kept):
    at = 0
    while at_p.shape[0] > 1:
        pa, pb = halves(at_p)
        la, lb = halves(at_l)
        d = la + pb
        m = d.shape[0]
        kept[at : at + m] = d
        at_p = pa + tree[2, at : at + m] * d
        at_l = lb + tree[1, at : at + m] * d
        at += m
    return at_p[0], at_l[0]


def up_tree(u_p, u_l, tree, kept):
    nodes = u_l[None]
    total = kept.shape[0]
    m = 1
    at = total - 1
    while at >= 0:
        before = u_p[None] if m == 1 else jnp.concatenate([u_p[None], nodes[:-1]], axis=0)
        mid = (
            tree[0, at : at + m] * kept[at : at + m]
            + tree[1, at : at + m] * nodes
            + tree[2, at : at + m] * before
        )
        nodes = jnp.stack([mid, nodes], axis=1).reshape((2 * m,) + nodes.shape[1:])
        m *= 2
        at -= m
    before = jnp.concatenate([u_p[None], nodes[:-1]], axis=0)
    return before, nodes


def up_cells(before, nodes, coef, kept, put):
    u = nodes
    put(SUB - 1, u)
    for t in range(SUB - 2, -1, -1):
        u = coef[0, t] * kept[t] + coef[1, t] * u + coef[2, t] * before
        put(t, u)


def line_ratios(me, n, every, chain, mine):
    zero = jnp.zeros(every.shape[2:], F32)
    ahead = []
    prior = None
    for j in range(n):
        p, g, l = every[j, 0], every[j, 1], every[j, 2]
        if prior is None:
            ahead.append((zero, zero, l + g))
            prior = l + g
        else:
            c = prior + p
            ratio = g * recip(c + g)
            now = l + c * ratio
            ahead.append((ratio, prior, now))
            prior = now
    back = [None] * n
    later = zero
    for j in range(n - 1, -1, -1):
        p, g, l = every[j, 0], every[j, 1], every[j, 2]
        c = later + l
        ratio = g * recip(c + g)
        now = p + c * ratio
        back[j] = (ratio, later, now)
        later = now
    own = [zero] * 6
    for j in range(n):
        here = me == j
        own = [jnp.where(here, v, o) for v, o in zip(ahead[j] + back[j], own)]
        chain[j, 0] = ahead[j][0]
        chain[j, 1] = back[j][0]
    for i, v in enumerate(own):
        mine[i] = v


def line_weights(me, n, chain, mine, weights):
    rho, sf_prior, sf_now, tau, sb_later, sb_now = [mine[i] for i in range(6)]
    zero = jnp.zeros_like(rho)
    inv_l = recip(sf_now + sb_later)
    inv_p = jnp.where(me > 0, recip(sf_prior + sb_now), zero)
    ahead = [None] * n
    w_p, w_l = inv_p, inv_l * rho
    for j in range(n - 1, -1, -1):
        left = me > j
        ahead[j] = (w_p, w_l)
        w_p = jnp.where(left, w_p * chain[j, 0], w_p)
        w_l = jnp.where(left, w_l * chain[j, 0], w_l)
    w_p, w_l = inv_p * tau, inv_l
    for j in range(n):
        left, right = me > j, me < j
        weights[j, 0] = jnp.where(left, ahead[j][0], w_p)
        weights[j, 1] = jnp.where(left, ahead[j][1], w_l)
        w_p = jnp.where(right, w_p * chain[j, 1], w_p)
        w_l = jnp.where(right, w_l * chain[j, 1], w_l)
    return inv_p, inv_l


class Line:
    def __init__(self, axis, n, me, send, recv):
        self.axis, self.n, self.me, self.send, self.recv = axis, n, me, send, recv

    def copy(self, src, dst, slot, target):
        return pltpu.make_async_remote_copy(
            src_ref=src,
            dst_ref=dst,
            send_sem=self.send.at[slot],
            recv_sem=self.recv.at[slot],
            device_id={self.axis: target},
            device_id_type=MESH,
        )

    def others(self):
        for o in range(1, self.n):
            yield o, lax.rem(self.me + o, self.n), lax.rem(self.me + self.n - o, self.n)

    def start_all(self, src_of, buf, base):
        for o, target, _ in self.others():
            self.copy(src_of(o), buf.at[self.me], base + o - 1, target).start()

    def await_one(self, o, src, buf, base):
        source = lax.rem(self.me + self.n - o, self.n)
        self.copy(src, buf.at[source], base + o - 1, source).wait_recv()

    def done_sending(self, src_of, buf, base):
        for o, target, _ in self.others():
            self.copy(src_of(o), buf.at[self.me], base + o - 1, target).wait_send()


def share_coefs(line, mine, every):
    for i, v in enumerate(mine):
        every[line.me, i] = v
    line.start_all(lambda o: every.at[line.me], every, 0)


def await_coefs(line, every):
    for o, _, _ in line.others():
        line.await_one(o, every.at[line.me], every, 0)


def send_values(line, at_p, at_l, out, got, mine):
    me = line.me
    out[0] = at_l + mine[0] * at_p
    out[1] = at_p + mine[3] * at_l
    line.start_all(lambda o: out.at[(me + o) // line.n], got, line.n - 1)


def take_values(line, inverses, out, got, weights):
    u_p = inverses[0] * out[1]
    u_l = inverses[1] * out[0]
    for o, _, source in line.others():
        line.await_one(o, out.at[0], got, line.n - 1)
        v = got[source]
        u_p = u_p + weights[source, 0] * v
        u_l = u_l + weights[source, 1] * v
    return u_p, u_l


def kernel(
    nx, ny, dims,
    u_hbm, kx_hbm, ky_hbm, out_ref,
    u_raw, kx_raw, ky_raw, nat, turned, gx, gy,
    coef_x, kept_x, tree_x, tkept_x, every_x, weights_x, chain_x, mine_x, out_x, got_x,
    coef_y, kept_y, tree_y, tkept_y, every_y, weights_y, chain_y, mine_y, out_y, got_y,
    edge_x_in, edge_y_out, edge_y_in, ends,
    local_sem, xs, xr, ys, yr,
):
    nz, lx, ly = dims
    lanes = 128
    groups = nz * lx // lanes
    bx, by = lx // SUB, ly // SUB
    ix = lax.axis_index("gx")
    iy = lax.axis_index("gy")
    loads = []
    for i, (src, dst) in enumerate(((ky_hbm, ky_raw), (u_hbm, u_raw), (kx_hbm, kx_raw))):
        cp = pltpu.make_async_copy(src, dst, local_sem.at[i])
        cp.start()
        loads.append(cp)
    line_x = Line("gx", nx, ix, xs, xr)
    line_y = Line("gy", ny, iy, ys, yr)
    barrier = pltpu.get_barrier_semaphore()
    for line in (line_x, line_y):
        for _, target, _ in line.others():
            pl.semaphore_signal(barrier, inc=1, device_id={line.axis: target}, device_id_type=MESH)

    def group(ref, g):
        return ref[g * lanes : (g + 1) * lanes]

    def x_rows(ref, x):
        return ref[pl.ds(x, nz, stride=lx), :]

    def y_rows(y):
        return turned[pl.ds(y, groups, stride=ly), :]

    hx = 2 * (nx - 1)
    hy = 2 * (ny - 1)

    def edge_x():
        return line_x.copy(kx_hbm.reshape(nz, lx, ly).at[:, lx - 1, :], edge_x_in, hx, jnp.minimum(ix + 1, nx - 1))

    def edge_y_right():
        return line_y.copy(edge_y_out.at[1], edge_y_in.at[0], hy, jnp.minimum(iy + 1, ny - 1))

    def edge_y_left():
        return line_y.copy(edge_y_out.at[0], edge_y_in.at[1], hy + 1, jnp.maximum(iy - 1, 0))

    pl.semaphore_wait(barrier, nx - 1 + ny - 1)

    @pl.when(ix < nx - 1)
    def _():
        edge_x().start()

    lane = lax.broadcasted_iota(jnp.int32, (lanes, ly), 1)
    packed = None
    for kind, (load, raw) in enumerate(((loads[0], ky_raw), (loads[1], u_raw))):
        load.wait()
        for g in range(groups):
            at = 2 * (kind * groups + g)
            moved = pltpu.roll(group(raw, g), at + 1, 1)
            packed = moved if packed is None else jnp.where(lane >= at, moved, packed)
    ends[...] = packed.T
    for kind in range(2):
        for side in range(2):
            edge_y_out[side, kind] = ends[pl.ds(2 * kind * groups + 1 - side, groups, stride=2), :]

    @pl.when(iy < ny - 1)
    def _():
        edge_y_right().start()

    @pl.when(iy > 0)
    def _():
        edge_y_left().start()

    loads[2].wait()
    kx_first = x_rows(kx_raw, 0)
    kx_last = x_rows(kx_raw, lx - 1)
    prior = kx_first
    for x in range(1, lx):
        now = x_rows(kx_raw, x)
        gx[x // SUB, x % SUB] = 0.5 * (prior + now)
        prior = now

    @pl.when(ix > 0)
    def _():
        edge_x().wait_recv()

    gx[0, 0] = 0.5 * (jnp.where(ix > 0, edge_x_in[...], 0.0) + kx_first)
    at_p, series, at_l = factor_tree(*factor_cells(lambda t: gx[:, t], coef_x), tree_x)
    at_l = at_l + jnp.where(ix == nx - 1, 0.5 * kx_last, 0.0)
    share_coefs(line_x, (at_p, series, at_l), every_x)

    for g in range(groups):
        turned[g * ly : (g + 1) * ly] = group(ky_raw, g).T
    prior = y_rows(0)
    for y in range(1, ly):
        now = y_rows(y)
        gy[y // SUB, y % SUB] = 0.5 * (prior + now)
        prior = now
    ky_last = prior

    @pl.when(iy > 0)
    def _():
        edge_y_right().wait_recv()

    @pl.when(iy < ny - 1)
    def _():
        edge_y_left().wait_recv()

    k0, u0, k1, u1 = edge_y_out[0, 0], edge_y_out[0, 1], edge_y_out[1, 0], edge_y_out[1, 1]
    inner, last = iy > 0, iy < ny - 1
    face_0 = 0.5 * (jnp.where(inner, edge_y_in[0, 0], 0.0) + k0)
    gy[0, 0] = face_0
    face_1 = 0.5 * (jnp.where(last, edge_y_in[1, 0], 0.0) + k1)
    flux_0 = face_0 * (jnp.where(inner, edge_y_in[0, 1], 0.0) - u0)
    flux_1 = face_1 * (jnp.where(last, edge_y_in[1, 1], 0.0) - u1)
    at_p, series, at_l = factor_tree(*factor_cells(lambda t: gy[:, t], coef_y), tree_y)
    at_l = at_l + jnp.where(iy == ny - 1, 0.5 * ky_last, 0.0)
    share_coefs(line_y, (at_p, series, at_l), every_y)


    ends[pl.ds(0, groups, stride=2), :] = flux_1
    ends[pl.ds(1, groups, stride=2), :] = -flux_0
    fluxes = ends[...].T
    for g in range(groups):
        outer = pltpu.roll(fluxes, (ly - 2 * g - 1) % ly, 1)
        u = group(u_raw, g)
        k = group(ky_raw, g)
        flux = 0.5 * (k + pltpu.roll(k, 1, 1)) * (u - pltpu.roll(u, 1, 1))
        flux = jnp.where(lane > 0, flux, outer)
        later = jnp.where(lane < ly - 1, pltpu.roll(flux, ly - 1, 1), outer)
        nat[g * lanes : (g + 1) * lanes] = u + (later - flux)

    def x_cells(t):
        return jnp.stack([x_rows(nat, b * SUB + t) for b in range(bx)], axis=0)

    d_p, d_l = down_cells(x_cells, coef_x, kept_x)
    d_p, d_l = down_tree(d_p, d_l, tree_x, tkept_x)
    await_coefs(line_x, every_x)
    line_ratios(ix, nx, every_x, chain_x, mine_x)
    send_values(line_x, d_p, d_l, out_x, got_x, mine_x)

    inverses = line_weights(ix, nx, chain_x, mine_x, weights_x)
    await_coefs(line_y, every_y)
    line_ratios(iy, ny, every_y, chain_y, mine_y)
    inverses_y = line_weights(iy, ny, chain_y, mine_y, weights_y)
    u_p, u_l = take_values(line_x, inverses, out_x, got_x, weights_x)
    before, nodes = up_tree(u_p, u_l, tree_x, tkept_x)

    def put_x(t, v):
        for b in range(bx):
            nat[pl.ds(b * SUB + t, nz, stride=lx), :] = v[b]

    up_cells(before, nodes, coef_x, kept_x, put_x)
    for g in range(groups):
        turned[g * ly : (g + 1) * ly] = (group(nat, g) - group(u_raw, g)).T

    def y_cells(t):
        return jnp.stack([y_rows(b * SUB + t) for b in range(by)], axis=0)

    d_p, d_l = down_cells(y_cells, coef_y, kept_y)
    d_p, d_l = down_tree(d_p, d_l, tree_y, tkept_y)
    send_values(line_y, d_p, d_l, out_y, got_y, mine_y)
    line_x.done_sending(lambda o: every_x.at[ix], every_x, 0)
    line_x.done_sending(lambda o: out_x.at[0], got_x, nx - 1)
    line_y.done_sending(lambda o: every_y.at[iy], every_y, 0)

    @pl.when(ix < nx - 1)
    def _():
        edge_x().wait_send()

    @pl.when(iy < ny - 1)
    def _():
        edge_y_right().wait_send()

    @pl.when(iy > 0)
    def _():
        edge_y_left().wait_send()

    u_p, u_l = take_values(line_y, inverses_y, out_y, got_y, weights_y)
    before, nodes = up_tree(u_p, u_l, tree_y, tkept_y)

    def put_y(t, v):
        for b in range(by):
            turned[pl.ds(b * SUB + t, groups, stride=ly), :] = v[b]

    up_cells(before, nodes, coef_y, kept_y, put_y)
    for g in range(groups):
        out_ref[g * lanes : (g + 1) * lanes] = group(u_raw, g) + 2.0 * turned[g * ly : (g + 1) * ly].T

    line_y.done_sending(lambda o: out_y.at[0], got_y, ny - 1)


def on_device(nx, ny, state, kappa_x, kappa_y):
    nz, lx, ly = state.shape
    groups = nz * lx // 128
    flat = (nz * lx, ly)
    bx, by = lx // SUB, ly // SUB

    def line_scratch(n, blocks, rows):
        one = (rows, 128)
        return [
            pltpu.VMEM((3, SUB - 1, blocks) + one, F32),
            pltpu.VMEM((SUB - 1, blocks) + one, F32),
            pltpu.VMEM((3, blocks - 1) + one, F32),
            pltpu.VMEM((blocks - 1,) + one, F32),
            pltpu.VMEM((n, 3) + one, F32),
            pltpu.VMEM((n, 2) + one, F32),
            pltpu.VMEM((n, 2) + one, F32),
            pltpu.VMEM((6,) + one, F32),
            pltpu.VMEM((2,) + one, F32),
            pltpu.VMEM((n,) + one, F32),
        ]

    scratch = (
        [pltpu.VMEM(flat, F32)] * 5
        + [
            pltpu.VMEM((bx, SUB, nz, ly), F32),
            pltpu.VMEM((by, SUB, groups, 128), F32),
        ]
        + line_scratch(nx, bx, nz)
        + line_scratch(ny, by, groups)
        + [
            pltpu.VMEM((nz, ly), F32),
            pltpu.VMEM((2, 2, groups, 128), F32),
            pltpu.VMEM((2, 2, groups, 128), F32),
            pltpu.VMEM((128, 128), F32),
            pltpu.SemaphoreType.DMA((3,)),
            pltpu.SemaphoreType.DMA((2 * nx - 1,)),
            pltpu.SemaphoreType.DMA((2 * nx - 1,)),
            pltpu.SemaphoreType.DMA((2 * ny,)),
            pltpu.SemaphoreType.DMA((2 * ny,)),
        ]
    )
    out = pl.pallas_call(
        functools.partial(kernel, nx, ny, (nz, lx, ly)),
        out_shape=jax.ShapeDtypeStruct(flat, F32),
        in_specs=[pl.BlockSpec(memory_space=pltpu.HBM)] * 3,
        out_specs=pl.BlockSpec(memory_space=pltpu.VMEM),
        scratch_shapes=scratch,
        compiler_params=pltpu.CompilerParams(
            collective_id=0, has_side_effects=True, vmem_limit_bytes=32 * 1024 * 1024
        ),
    )(*[pltpu.with_memory_space_constraint(v.reshape(flat), pltpu.HBM) for v in (state, kappa_x, kappa_y)])
    return out.reshape(state.shape)


def solution(mesh):
    spec = P(None, "gx", "gy")
    return jax.shard_map(
        functools.partial(on_device, mesh.shape["gx"], mesh.shape["gy"]),
        mesh=mesh,
        in_specs=(spec, spec, spec),
        out_specs=spec,
        check_vma=False,
    )
```

```python
import functools

import jax
import jax.numpy as jnp
from jax import lax
from jax.experimental import pallas as pl
from jax.experimental.pallas import tpu as pltpu
from jax.sharding import PartitionSpec as P

MESH = pl.DeviceIdType.MESH
F32 = jnp.float32
SUB = 8
PARTS = 4


def recip(p):
    r = pl.reciprocal(p, approx=True)
    return r * (2.0 - p * r)


def factor_cells(row, before_first, coef, blocks):
    ports = []
    for part in range(2):
        half = range(part * blocks // 2, (part + 1) * blocks // 2)

        def cells(t):
            return jnp.stack([row(b * SUB + t) if b * SUB + t >= 0 else before_first for b in half], axis=0)

        now = cells(0)
        to_p = 0.5 * (cells(-1) + now)
        s = jnp.ones_like(to_p)
        at_p = jnp.zeros_like(s)
        for t in range(SUB - 1):
            later = cells(t + 1)
            right = 0.5 * (now + later)
            now = later
            r = recip(s + to_p + right)
            a = right * r
            b = to_p * r
            coef[0, t, half.start : half.stop] = r
            coef[1, t, half.start : half.stop] = a
            coef[2, t, half.start : half.stop] = b
            at_p = at_p + s * b
            s = 1.0 + s * a
            to_p = to_p * a
        ports.append((at_p, to_p, s))
    return [jnp.concatenate(both, axis=0) for both in zip(*ports)]


def halves(v):
    v = v.reshape((v.shape[0] // 2, 2) + v.shape[1:])
    return v[:, 0], v[:, 1]


def factor_tree(at_p, series, at_l, tree):
    level = 0
    at = 0
    while at_p.shape[0] > 1:
        pa, pb = halves(at_p)
        ga, gb = halves(series)
        la, lb = halves(at_l)
        c = la + pb
        r = recip(c + ga + gb)
        a = gb * r
        b = ga * r
        m = r.shape[0]
        tree[0, at : at + m] = r
        tree[1, at : at + m] = a
        tree[2, at : at + m] = b
        at_p = pa + c * b
        at_l = lb + c * a
        series = ga * a
        at += m
        level += 1
    return at_p[0], series[0], at_l[0]


def down_cells(source, coef, kept):
    d = source(0)
    at_p = None
    for t in range(SUB - 1):
        kept[t] = d
        share = coef[2, t] * d
        at_p = share if at_p is None else at_p + share
        d = source(t + 1) + coef[1, t] * d
    return at_p, d


def down_tree(at_p, at_l, tree, kept):
    at = 0
    while at_p.shape[0] > 1:
        pa, pb = halves(at_p)
        la, lb = halves(at_l)
        d = la + pb
        m = d.shape[0]
        kept[at : at + m] = d
        at_p = pa + tree[2, at : at + m] * d
        at_l = lb + tree[1, at : at + m] * d
        at += m
    return at_p[0], at_l[0]


def up_tree(u_p, u_l, tree, kept):
    nodes = u_l[None]
    total = kept.shape[0]
    m = 1
    at = total - 1
    while at >= 0:
        before = u_p[None] if m == 1 else jnp.concatenate([u_p[None], nodes[:-1]], axis=0)
        mid = (
            tree[0, at : at + m] * kept[at : at + m]
            + tree[1, at : at + m] * nodes
            + tree[2, at : at + m] * before
        )
        nodes = jnp.stack([mid, nodes], axis=1).reshape((2 * m,) + nodes.shape[1:])
        m *= 2
        at -= m
    before = jnp.concatenate([u_p[None], nodes[:-1]], axis=0)
    return before, nodes


def up_cells(before, nodes, coef, kept, put):
    u = nodes
    put(SUB - 1, u)
    for t in range(SUB - 2, -1, -1):
        u = coef[0, t] * kept[t] + coef[1, t] * u + coef[2, t] * before
        put(t, u)


def line_ratios(me, n, every, chain, mine):
    zero = jnp.zeros(every.shape[2:], F32)
    ahead = []
    prior = None
    for j in range(n):
        p, g, l = every[j, 0], every[j, 1], every[j, 2]
        if prior is None:
            ahead.append((zero, zero, l + g))
            prior = l + g
        else:
            c = prior + p
            ratio = g * recip(c + g)
            now = l + c * ratio
            ahead.append((ratio, prior, now))
            prior = now
    back = [None] * n
    later = zero
    for j in range(n - 1, -1, -1):
        p, g, l = every[j, 0], every[j, 1], every[j, 2]
        c = later + l
        ratio = g * recip(c + g)
        now = p + c * ratio
        back[j] = (ratio, later, now)
        later = now
    own = [zero] * 6
    for j in range(n):
        here = me == j
        own = [jnp.where(here, v, o) for v, o in zip(ahead[j] + back[j], own)]
        chain[j, 0] = ahead[j][0]
        chain[j, 1] = back[j][0]
    for i, v in enumerate(own):
        mine[i] = v


def line_weights(me, n, chain, mine, weights):
    rho, sf_prior, sf_now, tau, sb_later, sb_now = [mine[i] for i in range(6)]
    zero = jnp.zeros_like(rho)
    inv_l = recip(sf_now + sb_later)
    inv_p = jnp.where(me > 0, recip(sf_prior + sb_now), zero)
    ahead = [None] * n
    w_p, w_l = inv_p, inv_l * rho
    for j in range(n - 1, -1, -1):
        left = me > j
        ahead[j] = (w_p, w_l)
        w_p = jnp.where(left, w_p * chain[j, 0], w_p)
        w_l = jnp.where(left, w_l * chain[j, 0], w_l)
    w_p, w_l = inv_p * tau, inv_l
    for j in range(n):
        left, right = me > j, me < j
        weights[j, 0] = jnp.where(left, ahead[j][0], w_p)
        weights[j, 1] = jnp.where(left, ahead[j][1], w_l)
        w_p = jnp.where(right, w_p * chain[j, 1], w_p)
        w_l = jnp.where(right, w_l * chain[j, 1], w_l)
    return inv_p, inv_l


class Line:
    def __init__(self, axis, n, me, send, recv):
        self.axis, self.n, self.me, self.send, self.recv = axis, n, me, send, recv

    def copy(self, src, dst, slot, target):
        return pltpu.make_async_remote_copy(
            src_ref=src,
            dst_ref=dst,
            send_sem=self.send.at[slot],
            recv_sem=self.recv.at[slot],
            device_id={self.axis: target},
            device_id_type=MESH,
        )

    def others(self):
        for o in sorted(range(1, self.n), key=lambda o: abs(2 * o - self.n)):
            yield o, lax.rem(self.me + o, self.n), lax.rem(self.me + self.n - o, self.n)

    def start_all(self, src_of, buf, base):
        for o, target, _ in self.others():
            self.copy(src_of(o), buf.at[self.me], base + o - 1, target).start()

    def await_one(self, o, src, buf, base):
        source = lax.rem(self.me + self.n - o, self.n)
        self.copy(src, buf.at[source], base + o - 1, source).wait_recv()

    def done_sending(self, src_of, buf, base):
        for o, target, _ in self.others():
            self.copy(src_of(o), buf.at[self.me], base + o - 1, target).wait_send()


def share_coefs(line, mine, every):
    for i, v in enumerate(mine):
        every[line.me, i] = v
    line.start_all(lambda o: every.at[line.me], every, 0)


def await_coefs(line, every):
    for o, _, _ in line.others():
        line.await_one(o, every.at[line.me], every, 0)


def send_values(line, at_p, at_l, out, got, mine):
    me = line.me
    out[0] = at_l + mine[0] * at_p
    out[1] = at_p + mine[3] * at_l
    line.start_all(lambda o: out.at[(me + o) // line.n], got, line.n - 1)


def take_values(line, inverses, out, got, weights):
    u_p = inverses[0] * out[1]
    u_l = inverses[1] * out[0]
    for o, _, source in reversed(list(line.others())):
        line.await_one(o, out.at[0], got, line.n - 1)
        v = got[source]
        u_p = u_p + weights[source, 0] * v
        u_l = u_l + weights[source, 1] * v
    return u_p, u_l


def kernel(
    nx, ny, dims,
    u_hbm, kx_hbm, ky_hbm, out_ref,
    u_raw, kx_raw, ky_raw, nat, turned,
    coef_x, kept_x, tree_x, tkept_x, every_x, weights_x, chain_x, mine_x, out_x, got_x,
    coef_y, kept_y, tree_y, tkept_y, every_y, weights_y, chain_y, mine_y, out_y, got_y,
    edge_x_in, edge_y_out, edge_y_in, ends,
    local_sem, xs, xr, ys, yr,
):
    nz, lx, ly = dims
    lanes = 128
    groups = nz * lx // lanes
    bx, by = lx // SUB, ly // SUB
    ix = lax.axis_index("gx")
    iy = lax.axis_index("gy")
    loads = []
    for i, (src, dst) in enumerate(((ky_hbm, ky_raw), (u_hbm, u_raw), (kx_hbm, kx_raw))):
        size = nz * lx // PARTS
        parts = [
            pltpu.make_async_copy(src.at[pl.ds(p * size, size)], dst.at[pl.ds(p * size, size)], local_sem.at[i, p])
            for p in range(PARTS)
        ]
        for part in parts:
            part.start()
        loads.append(parts)
    line_x = Line("gx", nx, ix, xs, xr)
    line_y = Line("gy", ny, iy, ys, yr)
    barrier = pltpu.get_barrier_semaphore()
    for line in (line_x, line_y):
        for _, target, _ in line.others():
            pl.semaphore_signal(barrier, inc=1, device_id={line.axis: target}, device_id_type=MESH)

    def group(ref, g):
        return ref[g * lanes : (g + 1) * lanes]

    def x_rows(ref, x):
        return ref[pl.ds(x, nz, stride=lx), :]

    def y_rows(y):
        return turned[pl.ds(y, groups, stride=ly), :]

    hx = 2 * (nx - 1)
    hy = 2 * (ny - 1)

    def edge_x():
        return line_x.copy(kx_hbm.reshape(nz, lx, ly).at[:, lx - 1, :], edge_x_in, hx, jnp.minimum(ix + 1, nx - 1))

    def edge_y_right():
        return line_y.copy(edge_y_out.at[1], edge_y_in.at[0], hy, jnp.minimum(iy + 1, ny - 1))

    def edge_y_left():
        return line_y.copy(edge_y_out.at[0], edge_y_in.at[1], hy + 1, jnp.maximum(iy - 1, 0))

    pl.semaphore_wait(barrier, nx - 1 + ny - 1)

    @pl.when(ix < nx - 1)
    def _():
        edge_x().start()

    lane = lax.broadcasted_iota(jnp.int32, (lanes, ly), 1)
    packed = None
    for kind, (load, raw) in enumerate(((loads[0], ky_raw), (loads[1], u_raw))):
        for part in load:
            part.wait()
        for g in range(groups):
            at = 2 * (kind * groups + g)
            moved = pltpu.roll(group(raw, g), at + 1, 1)
            packed = moved if packed is None else jnp.where(lane >= at, moved, packed)
    ends[...] = packed.T
    for kind in range(2):
        for side in range(2):
            edge_y_out[side, kind] = ends[pl.ds(2 * kind * groups + 1 - side, groups, stride=2), :]

    @pl.when(iy < ny - 1)
    def _():
        edge_y_right().start()

    @pl.when(iy > 0)
    def _():
        edge_y_left().start()

    for part in loads[2]:
        part.wait()
    kx_last = x_rows(kx_raw, lx - 1)
    @pl.when(ix > 0)
    def _():
        edge_x().wait_recv()

    before_x = jnp.where(ix > 0, edge_x_in[...], 0.0)
    at_p, series, at_l = factor_tree(*factor_cells(lambda x: x_rows(kx_raw, x), before_x, coef_x, bx), tree_x)
    at_l = at_l + jnp.where(ix == nx - 1, 0.5 * kx_last, 0.0)
    share_coefs(line_x, (at_p, series, at_l), every_x)

    for g in range(groups):
        turned[g * ly : (g + 1) * ly] = group(ky_raw, g).T
    ky_last = y_rows(ly - 1)

    @pl.when(iy > 0)
    def _():
        edge_y_right().wait_recv()

    @pl.when(iy < ny - 1)
    def _():
        edge_y_left().wait_recv()

    k0, u0, k1, u1 = edge_y_out[0, 0], edge_y_out[0, 1], edge_y_out[1, 0], edge_y_out[1, 1]
    inner, last = iy > 0, iy < ny - 1
    before_y = jnp.where(inner, edge_y_in[0, 0], 0.0)
    face_0 = 0.5 * (before_y + k0)
    face_1 = 0.5 * (jnp.where(last, edge_y_in[1, 0], 0.0) + k1)
    flux_0 = face_0 * (jnp.where(inner, edge_y_in[0, 1], 0.0) - u0)
    flux_1 = face_1 * (jnp.where(last, edge_y_in[1, 1], 0.0) - u1)
    at_p, series, at_l = factor_tree(*factor_cells(y_rows, before_y, coef_y, by), tree_y)
    at_l = at_l + jnp.where(iy == ny - 1, 0.5 * ky_last, 0.0)
    share_coefs(line_y, (at_p, series, at_l), every_y)


    ends[pl.ds(0, groups, stride=2), :] = flux_1
    ends[pl.ds(1, groups, stride=2), :] = -flux_0
    fluxes = ends[...].T
    for g in range(groups):
        outer = pltpu.roll(fluxes, (ly - 2 * g - 1) % ly, 1)
        u = group(u_raw, g)
        k = group(ky_raw, g)
        flux = 0.5 * (k + pltpu.roll(k, 1, 1)) * (u - pltpu.roll(u, 1, 1))
        flux = jnp.where(lane > 0, flux, outer)
        later = jnp.where(lane < ly - 1, pltpu.roll(flux, ly - 1, 1), outer)
        nat[g * lanes : (g + 1) * lanes] = u + (later - flux)

    def x_cells(t):
        return jnp.stack([x_rows(nat, b * SUB + t) for b in range(bx)], axis=0)

    d_p, d_l = down_cells(x_cells, coef_x, kept_x)
    d_p, d_l = down_tree(d_p, d_l, tree_x, tkept_x)
    await_coefs(line_x, every_x)
    line_ratios(ix, nx, every_x, chain_x, mine_x)
    send_values(line_x, d_p, d_l, out_x, got_x, mine_x)

    inverses = line_weights(ix, nx, chain_x, mine_x, weights_x)
    await_coefs(line_y, every_y)
    line_ratios(iy, ny, every_y, chain_y, mine_y)
    inverses_y = line_weights(iy, ny, chain_y, mine_y, weights_y)
    u_p, u_l = take_values(line_x, inverses, out_x, got_x, weights_x)
    before, nodes = up_tree(u_p, u_l, tree_x, tkept_x)

    def put_x(t, v):
        for b in range(bx):
            nat[pl.ds(b * SUB + t, nz, stride=lx), :] = v[b]

    up_cells(before, nodes, coef_x, kept_x, put_x)
    for g in range(groups):
        turned[g * ly : (g + 1) * ly] = (group(nat, g) - group(u_raw, g)).T

    def y_cells(t):
        return jnp.stack([y_rows(b * SUB + t) for b in range(by)], axis=0)

    d_p, d_l = down_cells(y_cells, coef_y, kept_y)
    d_p, d_l = down_tree(d_p, d_l, tree_y, tkept_y)
    send_values(line_y, d_p, d_l, out_y, got_y, mine_y)
    line_x.done_sending(lambda o: every_x.at[ix], every_x, 0)
    line_x.done_sending(lambda o: out_x.at[0], got_x, nx - 1)
    line_y.done_sending(lambda o: every_y.at[iy], every_y, 0)

    @pl.when(ix < nx - 1)
    def _():
        edge_x().wait_send()

    @pl.when(iy < ny - 1)
    def _():
        edge_y_right().wait_send()

    @pl.when(iy > 0)
    def _():
        edge_y_left().wait_send()

    u_p, u_l = take_values(line_y, inverses_y, out_y, got_y, weights_y)
    before, nodes = up_tree(u_p, u_l, tree_y, tkept_y)

    def put_y(t, v):
        for b in range(by):
            turned[pl.ds(b * SUB + t, groups, stride=ly), :] = v[b]

    up_cells(before, nodes, coef_y, kept_y, put_y)
    for g in range(groups):
        out_ref[g * lanes : (g + 1) * lanes] = group(u_raw, g) + 2.0 * turned[g * ly : (g + 1) * ly].T

    line_y.done_sending(lambda o: out_y.at[0], got_y, ny - 1)


def on_device(nx, ny, state, kappa_x, kappa_y):
    nz, lx, ly = state.shape
    groups = nz * lx // 128
    flat = (nz * lx, ly)
    bx, by = lx // SUB, ly // SUB

    def line_scratch(n, blocks, rows):
        one = (rows, 128)
        return [
            pltpu.VMEM((3, SUB - 1, blocks) + one, F32),
            pltpu.VMEM((SUB - 1, blocks) + one, F32),
            pltpu.VMEM((3, blocks - 1) + one, F32),
            pltpu.VMEM((blocks - 1,) + one, F32),
            pltpu.VMEM((n, 3) + one, F32),
            pltpu.VMEM((n, 2) + one, F32),
            pltpu.VMEM((n, 2) + one, F32),
            pltpu.VMEM((6,) + one, F32),
            pltpu.VMEM((2,) + one, F32),
            pltpu.VMEM((n,) + one, F32),
        ]

    scratch = (
        [pltpu.VMEM(flat, F32)] * 5
        + line_scratch(nx, bx, nz)
        + line_scratch(ny, by, groups)
        + [
            pltpu.VMEM((nz, ly), F32),
            pltpu.VMEM((2, 2, groups, 128), F32),
            pltpu.VMEM((2, 2, groups, 128), F32),
            pltpu.VMEM((128, 128), F32),
            pltpu.SemaphoreType.DMA((3, PARTS)),
            pltpu.SemaphoreType.DMA((2 * nx - 1,)),
            pltpu.SemaphoreType.DMA((2 * nx - 1,)),
            pltpu.SemaphoreType.DMA((2 * ny,)),
            pltpu.SemaphoreType.DMA((2 * ny,)),
        ]
    )
    out = pl.pallas_call(
        functools.partial(kernel, nx, ny, (nz, lx, ly)),
        out_shape=jax.ShapeDtypeStruct(flat, F32),
        in_specs=[pl.BlockSpec(memory_space=pltpu.HBM)] * 3,
        out_specs=pl.BlockSpec(memory_space=pltpu.VMEM),
        scratch_shapes=scratch,
        compiler_params=pltpu.CompilerParams(
            collective_id=0, has_side_effects=True, vmem_limit_bytes=32 * 1024 * 1024
        ),
    )(*[pltpu.with_memory_space_constraint(v.reshape(flat), pltpu.HBM) for v in (state, kappa_x, kappa_y)])
    return out.reshape(state.shape)


def solution(mesh):
    spec = P(None, "gx", "gy")
    return jax.shard_map(
        functools.partial(on_device, mesh.shape["gx"], mesh.shape["gy"]),
        mesh=mesh,
        in_specs=(spec, spec, spec),
        out_specs=spec,
        check_vma=False,
    )
```

```python
import functools

import jax
import jax.numpy as jnp
from jax import lax
from jax.experimental import pallas as pl
from jax.experimental.pallas import tpu as pltpu
from jax.sharding import PartitionSpec as P

MESH = pl.DeviceIdType.MESH
F32 = jnp.float32
SUB = 8


def recip(p):
    r = pl.reciprocal(p, approx=True)
    return r * (2.0 - p * r)


def factor_cells(face, coef):
    s = jnp.ones_like(face(0))
    to_p = face(0)
    at_p = jnp.zeros_like(s)
    for t in range(SUB - 1):
        right = face(t + 1)
        r = recip(s + to_p + right)
        a = right * r
        b = to_p * r
        coef[0, t] = r
        coef[1, t] = a
        coef[2, t] = b
        at_p = at_p + s * b
        s = 1.0 + s * a
        to_p = to_p * a
    return at_p, to_p, s


def halves(v):
    v = v.reshape((v.shape[0] // 2, 2) + v.shape[1:])
    return v[:, 0], v[:, 1]


def factor_tree(at_p, series, at_l, tree):
    level = 0
    at = 0
    while at_p.shape[0] > 1:
        pa, pb = halves(at_p)
        ga, gb = halves(series)
        la, lb = halves(at_l)
        c = la + pb
        r = recip(c + ga + gb)
        a = gb * r
        b = ga * r
        m = r.shape[0]
        tree[0, at : at + m] = r
        tree[1, at : at + m] = a
        tree[2, at : at + m] = b
        at_p = pa + c * b
        at_l = lb + c * a
        series = ga * a
        at += m
        level += 1
    return at_p[0], series[0], at_l[0]


def down_cells(source, coef, kept):
    d = source(0)
    at_p = None
    for t in range(SUB - 1):
        kept[t] = d
        share = coef[2, t] * d
        at_p = share if at_p is None else at_p + share
        d = source(t + 1) + coef[1, t] * d
    return at_p, d


def down_tree(at_p, at_l, tree, kept):
    at = 0
    while at_p.shape[0] > 1:
        pa, pb = halves(at_p)
        la, lb = halves(at_l)
        d = la + pb
        m = d.shape[0]
        kept[at : at + m] = d
        at_p = pa + tree[2, at : at + m] * d
        at_l = lb + tree[1, at : at + m] * d
        at += m
    return at_p[0], at_l[0]


def up_tree(u_p, u_l, tree, kept):
    nodes = u_l[None]
    total = kept.shape[0]
    m = 1
    at = total - 1
    while at >= 0:
        before = u_p[None] if m == 1 else jnp.concatenate([u_p[None], nodes[:-1]], axis=0)
        mid = (
            tree[0, at : at + m] * kept[at : at + m]
            + tree[1, at : at + m] * nodes
            + tree[2, at : at + m] * before
        )
        nodes = jnp.stack([mid, nodes], axis=1).reshape((2 * m,) + nodes.shape[1:])
        m *= 2
        at -= m
    before = jnp.concatenate([u_p[None], nodes[:-1]], axis=0)
    return before, nodes


def up_cells(before, nodes, coef, kept, put):
    u = nodes
    put(SUB - 1, u)
    for t in range(SUB - 2, -1, -1):
        u = coef[0, t] * kept[t] + coef[1, t] * u + coef[2, t] * before
        put(t, u)


def line_ratios(me, n, every, chain, mine):
    zero = jnp.zeros(every.shape[2:], F32)
    ahead = []
    prior = None
    for j in range(n):
        p, g, l = every[j, 0], every[j, 1], every[j, 2]
        if prior is None:
            ahead.append((zero, zero, l + g))
            prior = l + g
        else:
            c = prior + p
            ratio = g * recip(c + g)
            now = l + c * ratio
            ahead.append((ratio, prior, now))
            prior = now
    back = [None] * n
    later = zero
    for j in range(n - 1, -1, -1):
        p, g, l = every[j, 0], every[j, 1], every[j, 2]
        c = later + l
        ratio = g * recip(c + g)
        now = p + c * ratio
        back[j] = (ratio, later, now)
        later = now
    own = [zero] * 6
    for j in range(n):
        here = me == j
        own = [jnp.where(here, v, o) for v, o in zip(ahead[j] + back[j], own)]
        chain[j, 0] = ahead[j][0]
        chain[j, 1] = back[j][0]
    for i, v in enumerate(own):
        mine[i] = v


def line_weights(me, n, chain, mine, weights):
    rho, sf_prior, sf_now, tau, sb_later, sb_now = [mine[i] for i in range(6)]
    zero = jnp.zeros_like(rho)
    inv_l = recip(sf_now + sb_later)
    inv_p = jnp.where(me > 0, recip(sf_prior + sb_now), zero)
    ahead = [None] * n
    w_p, w_l = inv_p, inv_l * rho
    for j in range(n - 1, -1, -1):
        left = me > j
        ahead[j] = (w_p, w_l)
        w_p = jnp.where(left, w_p * chain[j, 0], w_p)
        w_l = jnp.where(left, w_l * chain[j, 0], w_l)
    w_p, w_l = inv_p * tau, inv_l
    for j in range(n):
        left, right = me > j, me < j
        weights[j, 0] = jnp.where(left, ahead[j][0], w_p)
        weights[j, 1] = jnp.where(left, ahead[j][1], w_l)
        w_p = jnp.where(right, w_p * chain[j, 1], w_p)
        w_l = jnp.where(right, w_l * chain[j, 1], w_l)
    return inv_p, inv_l


class Line:
    def __init__(self, axis, n, me, send, recv):
        self.axis, self.n, self.me, self.send, self.recv = axis, n, me, send, recv

    def copy(self, src, dst, slot, target):
        return pltpu.make_async_remote_copy(
            src_ref=src,
            dst_ref=dst,
            send_sem=self.send.at[slot],
            recv_sem=self.recv.at[slot],
            device_id={self.axis: target},
            device_id_type=MESH,
        )

    def others(self):
        for o in range(1, self.n):
            yield o, lax.rem(self.me + o, self.n), lax.rem(self.me + self.n - o, self.n)

    def start_all(self, src_of, buf, base):
        for o, target, _ in self.others():
            self.copy(src_of(o), buf.at[self.me], base + o - 1, target).start()

    def await_one(self, o, src, buf, base):
        source = lax.rem(self.me + self.n - o, self.n)
        self.copy(src, buf.at[source], base + o - 1, source).wait_recv()

    def done_sending(self, src_of, buf, base):
        for o, target, _ in self.others():
            self.copy(src_of(o), buf.at[self.me], base + o - 1, target).wait_send()


def share_coefs(line, mine, every):
    for i, v in enumerate(mine):
        every[line.me, i] = v
    line.start_all(lambda o: every.at[line.me], every, 0)


def await_coefs(line, every):
    for o, _, _ in line.others():
        line.await_one(o, every.at[line.me], every, 0)


def send_values(line, at_p, at_l, out, got, mine):
    me = line.me
    out[0] = at_l + mine[0] * at_p
    out[1] = at_p + mine[3] * at_l
    line.start_all(lambda o: out.at[(me + o) // line.n], got, line.n - 1)


def take_values(line, inverses, out, got, weights):
    u_p = inverses[0] * out[1]
    u_l = inverses[1] * out[0]
    for o, _, source in line.others():
        line.await_one(o, out.at[0], got, line.n - 1)
        v = got[source]
        u_p = u_p + weights[source, 0] * v
        u_l = u_l + weights[source, 1] * v
    return u_p, u_l


def kernel(
    nx, ny, dims,
    u_hbm, kx_hbm, ky_hbm, out_ref,
    u_raw, kx_raw, ky_raw, nat, turned, gx, gy,
    coef_x, kept_x, tree_x, tkept_x, every_x, weights_x, chain_x, mine_x, out_x, got_x,
    coef_y, kept_y, tree_y, tkept_y, every_y, weights_y, chain_y, mine_y, out_y, got_y,
    edge_x_out, edge_x_in, edge_y_out, edge_y_in,
    local_sem, xs, xr, ys, yr,
):
    nz, lx, ly = dims
    lanes = 128
    groups = nz * lx // lanes
    bx, by = lx // SUB, ly // SUB
    ix = lax.axis_index("gx")
    iy = lax.axis_index("gy")
    loads = []
    for i, (src, dst) in enumerate(((ky_hbm, ky_raw), (u_hbm, u_raw), (kx_hbm, kx_raw))):
        cp = pltpu.make_async_copy(src, dst, local_sem.at[i])
        cp.start()
        loads.append(cp)
    line_x = Line("gx", nx, ix, xs, xr)
    line_y = Line("gy", ny, iy, ys, yr)
    barrier = pltpu.get_barrier_semaphore()
    for line in (line_x, line_y):
        for _, target, _ in line.others():
            pl.semaphore_signal(barrier, inc=1, device_id={line.axis: target}, device_id_type=MESH)

    def group(ref, g):
        return ref[g * lanes : (g + 1) * lanes]

    def x_rows(ref, x):
        return ref[pl.ds(x, nz, stride=lx), :]

    def y_rows(y):
        return turned[pl.ds(y, groups, stride=ly), :]

    hx = 2 * (nx - 1)
    hy = 2 * (ny - 1)

    def edge_x():
        return line_x.copy(edge_x_out, edge_x_in, hx, jnp.minimum(ix + 1, nx - 1))

    def edge_y_right():
        return line_y.copy(edge_y_out.at[1], edge_y_in.at[0], hy, jnp.minimum(iy + 1, ny - 1))

    def edge_y_left():
        return line_y.copy(edge_y_out.at[0], edge_y_in.at[1], hy + 1, jnp.maximum(iy - 1, 0))

    row8 = lax.broadcasted_iota(jnp.int32, (8, ly), 0)
    lane8 = lax.broadcasted_iota(jnp.int32, (8, ly), 1)
    pick = jnp.where(((row8 == 0) & (lane8 == 0)) | ((row8 == 1) & (lane8 == ly - 1)), 1.0, 0.0).astype(F32)
    for kind, (load, raw) in enumerate(((loads[0], ky_raw), (loads[1], u_raw))):
        load.wait()
        for g in range(groups):
            edges = lax.dot_general(
                pick, group(raw, g), (((1,), (1,)), ((), ())),
                precision=lax.Precision.HIGHEST, preferred_element_type=F32,
            )
            edge_y_out[0, kind, g : g + 1] = edges[0:1]
            edge_y_out[1, kind, g : g + 1] = edges[1:2]
    loads[2].wait()
    kx_first = x_rows(kx_raw, 0)
    kx_last = x_rows(kx_raw, lx - 1)
    edge_x_out[...] = kx_last
    pl.semaphore_wait(barrier, nx - 1 + ny - 1)

    @pl.when(ix < nx - 1)
    def _():
        edge_x().start()

    @pl.when(iy < ny - 1)
    def _():
        edge_y_right().start()

    @pl.when(iy > 0)
    def _():
        edge_y_left().start()

    prior = kx_first
    for x in range(1, lx):
        now = x_rows(kx_raw, x)
        gx[x // SUB, x % SUB] = 0.5 * (prior + now)
        prior = now
    @pl.when(ix > 0)
    def _():
        edge_x().wait_recv()

    gx[0, 0] = 0.5 * (jnp.where(ix > 0, edge_x_in[...], 0.0) + kx_first)
    at_p, series, at_l = factor_tree(*factor_cells(lambda t: gx[:, t], coef_x), tree_x)
    at_l = at_l + jnp.where(ix == nx - 1, 0.5 * kx_last, 0.0)
    share_coefs(line_x, (at_p, series, at_l), every_x)

    for g in range(groups):
        turned[g * ly : (g + 1) * ly] = group(ky_raw, g).T
    prior = y_rows(0)
    for y in range(1, ly):
        now = y_rows(y)
        gy[y // SUB, y % SUB] = 0.5 * (prior + now)
        prior = now
    ky_last = prior

    @pl.when(iy > 0)
    def _():
        edge_y_right().wait_recv()

    @pl.when(iy < ny - 1)
    def _():
        edge_y_left().wait_recv()

    k0, u0, k1, u1 = edge_y_out[0, 0], edge_y_out[0, 1], edge_y_out[1, 0], edge_y_out[1, 1]
    inner, last = iy > 0, iy < ny - 1
    face_0 = 0.5 * (jnp.where(inner, edge_y_in[0, 0], 0.0) + k0)
    gy[0, 0] = face_0
    face_1 = 0.5 * (jnp.where(last, edge_y_in[1, 0], 0.0) + k1)
    flux_0 = face_0 * (jnp.where(inner, edge_y_in[0, 1], 0.0) - u0)
    flux_1 = face_1 * (jnp.where(last, edge_y_in[1, 1], 0.0) - u1)
    at_p, series, at_l = factor_tree(*factor_cells(lambda t: gy[:, t], coef_y), tree_y)
    at_l = at_l + jnp.where(iy == ny - 1, 0.5 * ky_last, 0.0)
    share_coefs(line_y, (at_p, series, at_l), every_y)


    ends = jnp.concatenate([flux_0, flux_1], axis=0).T
    row = lax.broadcasted_iota(jnp.int32, (2 * groups, ly), 0)
    lane = lax.broadcasted_iota(jnp.int32, (2 * groups, ly), 1)
    inside = lax.broadcasted_iota(jnp.int32, (lanes, ly), 1) > 0
    for g in range(groups):
        put = jnp.where(((row == g) & (lane == 0)) | ((row == groups + g) & (lane == ly - 1)), 1.0, 0.0).astype(F32)
        added = lax.dot_general(
            ends, put, (((1,), (0,)), ((), ())), precision=lax.Precision.HIGHEST, preferred_element_type=F32
        )
        u = group(u_raw, g)
        k = group(ky_raw, g)
        flux = jnp.where(inside, 0.5 * (k + pltpu.roll(k, 1, 1)) * (u - pltpu.roll(u, 1, 1)), 0.0)
        nat[g * lanes : (g + 1) * lanes] = (u + added) + (pltpu.roll(flux, ly - 1, 1) - flux)

    def x_cells(t):
        return jnp.stack([x_rows(nat, b * SUB + t) for b in range(bx)], axis=0)

    d_p, d_l = down_cells(x_cells, coef_x, kept_x)
    d_p, d_l = down_tree(d_p, d_l, tree_x, tkept_x)
    await_coefs(line_x, every_x)
    line_ratios(ix, nx, every_x, chain_x, mine_x)
    send_values(line_x, d_p, d_l, out_x, got_x, mine_x)

    inverses = line_weights(ix, nx, chain_x, mine_x, weights_x)
    await_coefs(line_y, every_y)
    line_ratios(iy, ny, every_y, chain_y, mine_y)
    inverses_y = line_weights(iy, ny, chain_y, mine_y, weights_y)
    u_p, u_l = take_values(line_x, inverses, out_x, got_x, weights_x)
    before, nodes = up_tree(u_p, u_l, tree_x, tkept_x)

    def put_x(t, v):
        for b in range(bx):
            nat[pl.ds(b * SUB + t, nz, stride=lx), :] = v[b]

    up_cells(before, nodes, coef_x, kept_x, put_x)
    for g in range(groups):
        turned[g * ly : (g + 1) * ly] = (group(nat, g) - group(u_raw, g)).T

    def y_cells(t):
        return jnp.stack([y_rows(b * SUB + t) for b in range(by)], axis=0)

    d_p, d_l = down_cells(y_cells, coef_y, kept_y)
    d_p, d_l = down_tree(d_p, d_l, tree_y, tkept_y)
    send_values(line_y, d_p, d_l, out_y, got_y, mine_y)
    line_x.done_sending(lambda o: every_x.at[ix], every_x, 0)
    line_x.done_sending(lambda o: out_x.at[0], got_x, nx - 1)
    line_y.done_sending(lambda o: every_y.at[iy], every_y, 0)

    @pl.when(ix < nx - 1)
    def _():
        edge_x().wait_send()

    @pl.when(iy < ny - 1)
    def _():
        edge_y_right().wait_send()

    @pl.when(iy > 0)
    def _():
        edge_y_left().wait_send()

    u_p, u_l = take_values(line_y, inverses_y, out_y, got_y, weights_y)
    before, nodes = up_tree(u_p, u_l, tree_y, tkept_y)

    def put_y(t, v):
        for b in range(by):
            turned[pl.ds(b * SUB + t, groups, stride=ly), :] = v[b]

    up_cells(before, nodes, coef_y, kept_y, put_y)
    for g in range(groups):
        out_ref[g * lanes : (g + 1) * lanes] = group(u_raw, g) + 2.0 * turned[g * ly : (g + 1) * ly].T

    line_y.done_sending(lambda o: out_y.at[0], got_y, ny - 1)


def on_device(nx, ny, state, kappa_x, kappa_y):
    nz, lx, ly = state.shape
    groups = nz * lx // 128
    flat = (nz * lx, ly)
    bx, by = lx // SUB, ly // SUB

    def line_scratch(n, blocks, rows):
        one = (rows, 128)
        return [
            pltpu.VMEM((3, SUB - 1, blocks) + one, F32),
            pltpu.VMEM((SUB - 1, blocks) + one, F32),
            pltpu.VMEM((3, blocks - 1) + one, F32),
            pltpu.VMEM((blocks - 1,) + one, F32),
            pltpu.VMEM((n, 3) + one, F32),
            pltpu.VMEM((n, 2) + one, F32),
            pltpu.VMEM((n, 2) + one, F32),
            pltpu.VMEM((6,) + one, F32),
            pltpu.VMEM((2,) + one, F32),
            pltpu.VMEM((n,) + one, F32),
        ]

    scratch = (
        [pltpu.VMEM(flat, F32)] * 5
        + [
            pltpu.VMEM((bx, SUB, nz, ly), F32),
            pltpu.VMEM((by, SUB, groups, 128), F32),
        ]
        + line_scratch(nx, bx, nz)
        + line_scratch(ny, by, groups)
        + [
            pltpu.VMEM((nz, ly), F32),
            pltpu.VMEM((nz, ly), F32),
            pltpu.VMEM((2, 2, groups, 128), F32),
            pltpu.VMEM((2, 2, groups, 128), F32),
            pltpu.SemaphoreType.DMA((3,)),
            pltpu.SemaphoreType.DMA((2 * nx - 1,)),
            pltpu.SemaphoreType.DMA((2 * nx - 1,)),
            pltpu.SemaphoreType.DMA((2 * ny,)),
            pltpu.SemaphoreType.DMA((2 * ny,)),
        ]
    )
    out = pl.pallas_call(
        functools.partial(kernel, nx, ny, (nz, lx, ly)),
        out_shape=jax.ShapeDtypeStruct(flat, F32),
        in_specs=[pl.BlockSpec(memory_space=pltpu.HBM)] * 3,
        out_specs=pl.BlockSpec(memory_space=pltpu.VMEM),
        scratch_shapes=scratch,
        compiler_params=pltpu.CompilerParams(
            collective_id=0, has_side_effects=True, vmem_limit_bytes=32 * 1024 * 1024
        ),
    )(*[pltpu.with_memory_space_constraint(v.reshape(flat), pltpu.HBM) for v in (state, kappa_x, kappa_y)])
    return out.reshape(state.shape)


def solution(mesh):
    spec = P(None, "gx", "gy")
    return jax.shard_map(
        functools.partial(on_device, mesh.shape["gx"], mesh.shape["gy"]),
        mesh=mesh,
        in_specs=(spec, spec, spec),
        out_specs=spec,
        check_vma=False,
    )
```

```python
import functools

import jax
import jax.numpy as jnp
from jax import lax
from jax.experimental import pallas as pl
from jax.experimental.pallas import tpu as pltpu
from jax.sharding import PartitionSpec as P

MESH = pl.DeviceIdType.MESH
F32 = jnp.float32
SUB = 8


def recip(p):
    r = pl.reciprocal(p, approx=True)
    return r * (2.0 - p * r)


def two_parts(v, axis):
    high = v.astype(jnp.bfloat16)
    low = (v - high.astype(F32)).astype(jnp.bfloat16)
    return jnp.concatenate([high, low], axis=axis)


def factor_cells(face, coef):
    s = jnp.ones_like(face(0))
    to_p = face(0)
    at_p = jnp.zeros_like(s)
    for t in range(SUB - 1):
        right = face(t + 1)
        r = recip(s + to_p + right)
        a = right * r
        b = to_p * r
        coef[0, t] = r
        coef[1, t] = a
        coef[2, t] = b
        at_p = at_p + s * b
        s = 1.0 + s * a
        to_p = to_p * a
    return at_p, to_p, s


def halves(v):
    v = v.reshape((v.shape[0] // 2, 2) + v.shape[1:])
    return v[:, 0], v[:, 1]


def factor_tree(at_p, series, at_l, tree):
    level = 0
    at = 0
    while at_p.shape[0] > 1:
        pa, pb = halves(at_p)
        ga, gb = halves(series)
        la, lb = halves(at_l)
        c = la + pb
        r = recip(c + ga + gb)
        a = gb * r
        b = ga * r
        m = r.shape[0]
        tree[0, at : at + m] = r
        tree[1, at : at + m] = a
        tree[2, at : at + m] = b
        at_p = pa + c * b
        at_l = lb + c * a
        series = ga * a
        at += m
        level += 1
    return at_p[0], series[0], at_l[0]


def down_cells(source, coef, kept):
    d = source(0)
    at_p = None
    for t in range(SUB - 1):
        kept[t] = d
        share = coef[2, t] * d
        at_p = share if at_p is None else at_p + share
        d = source(t + 1) + coef[1, t] * d
    return at_p, d


def down_tree(at_p, at_l, tree, kept):
    at = 0
    while at_p.shape[0] > 1:
        pa, pb = halves(at_p)
        la, lb = halves(at_l)
        d = la + pb
        m = d.shape[0]
        kept[at : at + m] = d
        at_p = pa + tree[2, at : at + m] * d
        at_l = lb + tree[1, at : at + m] * d
        at += m
    return at_p[0], at_l[0]


def up_tree(u_p, u_l, tree, kept):
    nodes = u_l[None]
    total = kept.shape[0]
    m = 1
    at = total - 1
    while at >= 0:
        before = u_p[None] if m == 1 else jnp.concatenate([u_p[None], nodes[:-1]], axis=0)
        mid = (
            tree[0, at : at + m] * kept[at : at + m]
            + tree[1, at : at + m] * nodes
            + tree[2, at : at + m] * before
        )
        nodes = jnp.stack([mid, nodes], axis=1).reshape((2 * m,) + nodes.shape[1:])
        m *= 2
        at -= m
    before = jnp.concatenate([u_p[None], nodes[:-1]], axis=0)
    return before, nodes


def up_cells(before, nodes, coef, kept, put):
    u = nodes
    put(SUB - 1, u)
    for t in range(SUB - 2, -1, -1):
        u = coef[0, t] * kept[t] + coef[1, t] * u + coef[2, t] * before
        put(t, u)


def line_ratios(me, n, every, chain, mine):
    zero = jnp.zeros(every.shape[2:], F32)
    ahead = []
    prior = None
    for j in range(n):
        p, g, l = every[j, 0], every[j, 1], every[j, 2]
        if prior is None:
            ahead.append((zero, zero, l + g))
            prior = l + g
        else:
            c = prior + p
            ratio = g * recip(c + g)
            now = l + c * ratio
            ahead.append((ratio, prior, now))
            prior = now
    back = [None] * n
    later = zero
    for j in range(n - 1, -1, -1):
        p, g, l = every[j, 0], every[j, 1], every[j, 2]
        c = later + l
        ratio = g * recip(c + g)
        now = p + c * ratio
        back[j] = (ratio, later, now)
        later = now
    own = [zero] * 6
    for j in range(n):
        here = me == j
        own = [jnp.where(here, v, o) for v, o in zip(ahead[j] + back[j], own)]
        chain[j, 0] = ahead[j][0]
        chain[j, 1] = back[j][0]
    for i, v in enumerate(own):
        mine[i] = v


def line_weights(me, n, chain, mine, weights):
    rho, sf_prior, sf_now, tau, sb_later, sb_now = [mine[i] for i in range(6)]
    zero = jnp.zeros_like(rho)
    inv_l = recip(sf_now + sb_later)
    inv_p = jnp.where(me > 0, recip(sf_prior + sb_now), zero)
    ahead = [None] * n
    w_p, w_l = inv_p, inv_l * rho
    for j in range(n - 1, -1, -1):
        left = me > j
        ahead[j] = (w_p, w_l)
        w_p = jnp.where(left, w_p * chain[j, 0], w_p)
        w_l = jnp.where(left, w_l * chain[j, 0], w_l)
    w_p, w_l = inv_p * tau, inv_l
    for j in range(n):
        left, right = me > j, me < j
        weights[j, 0] = jnp.where(left, ahead[j][0], w_p)
        weights[j, 1] = jnp.where(left, ahead[j][1], w_l)
        w_p = jnp.where(right, w_p * chain[j, 1], w_p)
        w_l = jnp.where(right, w_l * chain[j, 1], w_l)
    return inv_p, inv_l


class Line:
    def __init__(self, axis, n, me, send, recv):
        self.axis, self.n, self.me, self.send, self.recv = axis, n, me, send, recv

    def copy(self, src, dst, slot, target):
        return pltpu.make_async_remote_copy(
            src_ref=src,
            dst_ref=dst,
            send_sem=self.send.at[slot],
            recv_sem=self.recv.at[slot],
            device_id={self.axis: target},
            device_id_type=MESH,
        )

    def others(self):
        for o in range(1, self.n):
            yield o, lax.rem(self.me + o, self.n), lax.rem(self.me + self.n - o, self.n)

    def start_all(self, src_of, buf, base):
        for o, target, _ in self.others():
            self.copy(src_of(o), buf.at[self.me], base + o - 1, target).start()

    def await_one(self, o, src, buf, base):
        source = lax.rem(self.me + self.n - o, self.n)
        self.copy(src, buf.at[source], base + o - 1, source).wait_recv()

    def done_sending(self, src_of, buf, base):
        for o, target, _ in self.others():
            self.copy(src_of(o), buf.at[self.me], base + o - 1, target).wait_send()


def share_coefs(line, mine, every):
    for i, v in enumerate(mine):
        every[line.me, i] = v
    line.start_all(lambda o: every.at[line.me], every, 0)


def await_coefs(line, every):
    for o, _, _ in line.others():
        line.await_one(o, every.at[line.me], every, 0)


def send_values(line, at_p, at_l, out, got, mine):
    me = line.me
    out[0] = at_l + mine[0] * at_p
    out[1] = at_p + mine[3] * at_l
    line.start_all(lambda o: out.at[(me + o) // line.n], got, line.n - 1)


def take_values(line, inverses, out, got, weights):
    u_p = inverses[0] * out[1]
    u_l = inverses[1] * out[0]
    for o, _, source in line.others():
        line.await_one(o, out.at[0], got, line.n - 1)
        v = got[source]
        u_p = u_p + weights[source, 0] * v
        u_l = u_l + weights[source, 1] * v
    return u_p, u_l


def kernel(
    nx, ny, dims,
    u_hbm, kx_hbm, ky_hbm, out_ref,
    u_raw, kx_raw, ky_raw, nat, turned, gx, gy,
    coef_x, kept_x, tree_x, tkept_x, every_x, weights_x, chain_x, mine_x, out_x, got_x,
    coef_y, kept_y, tree_y, tkept_y, every_y, weights_y, chain_y, mine_y, out_y, got_y,
    edge_x_out, edge_x_in, edge_y_out, edge_y_in,
    local_sem, xs, xr, ys, yr,
):
    nz, lx, ly = dims
    lanes = 128
    groups = nz * lx // lanes
    bx, by = lx // SUB, ly // SUB
    ix = lax.axis_index("gx")
    iy = lax.axis_index("gy")
    line_x = Line("gx", nx, ix, xs, xr)
    line_y = Line("gy", ny, iy, ys, yr)
    barrier = pltpu.get_barrier_semaphore()
    for line in (line_x, line_y):
        for _, target, _ in line.others():
            pl.semaphore_signal(barrier, inc=1, device_id={line.axis: target}, device_id_type=MESH)
    loads = []
    for i, (src, dst) in enumerate(((ky_hbm, ky_raw), (u_hbm, u_raw), (kx_hbm, kx_raw))):
        cp = pltpu.make_async_copy(src, dst, local_sem.at[i])
        cp.start()
        loads.append(cp)

    def group(ref, g):
        return ref[g * lanes : (g + 1) * lanes]

    def x_rows(ref, x):
        return ref[pl.ds(x, nz, stride=lx), :]

    def y_rows(y):
        return turned[pl.ds(y, groups, stride=ly), :]

    hx = 2 * (nx - 1)
    hy = 2 * (ny - 1)

    def edge_x():
        return line_x.copy(edge_x_out, edge_x_in, hx, jnp.minimum(ix + 1, nx - 1))

    def edge_y_right():
        return line_y.copy(edge_y_out.at[1], edge_y_in.at[0], hy, jnp.minimum(iy + 1, ny - 1))

    def edge_y_left():
        return line_y.copy(edge_y_out.at[0], edge_y_in.at[1], hy + 1, jnp.maximum(iy - 1, 0))

    row16 = lax.broadcasted_iota(jnp.int32, (16, ly), 0)
    lane16 = lax.broadcasted_iota(jnp.int32, (16, ly), 1)
    pick = jnp.where(((row16 == 0) & (lane16 == 0)) | ((row16 == 1) & (lane16 == ly - 1)), 1.0, 0.0)
    pick = jnp.concatenate([pick, pick], axis=1).astype(jnp.bfloat16)
    for kind, (load, raw) in enumerate(((loads[0], ky_raw), (loads[1], u_raw))):
        load.wait()
        for g in range(groups):
            edges = lax.dot_general(
                pick, two_parts(group(raw, g), 1), (((1,), (1,)), ((), ())), preferred_element_type=F32
            )
            edge_y_out[0, kind, g : g + 1] = edges[0:1]
            edge_y_out[1, kind, g : g + 1] = edges[1:2]
    loads[2].wait()
    kx_first = x_rows(kx_raw, 0)
    kx_last = x_rows(kx_raw, lx - 1)
    edge_x_out[...] = kx_last
    pl.semaphore_wait(barrier, nx - 1 + ny - 1)

    @pl.when(ix < nx - 1)
    def _():
        edge_x().start()

    @pl.when(iy < ny - 1)
    def _():
        edge_y_right().start()

    @pl.when(iy > 0)
    def _():
        edge_y_left().start()

    prior = kx_first
    for x in range(1, lx):
        now = x_rows(kx_raw, x)
        gx[x // SUB, x % SUB] = 0.5 * (prior + now)
        prior = now
    @pl.when(ix > 0)
    def _():
        edge_x().wait_recv()

    gx[0, 0] = 0.5 * (jnp.where(ix > 0, edge_x_in[...], 0.0) + kx_first)
    at_p, series, at_l = factor_tree(*factor_cells(lambda t: gx[:, t], coef_x), tree_x)
    at_l = at_l + jnp.where(ix == nx - 1, 0.5 * kx_last, 0.0)
    share_coefs(line_x, (at_p, series, at_l), every_x)

    for g in range(groups):
        turned[g * ly : (g + 1) * ly] = group(ky_raw, g).T
    prior = y_rows(0)
    for y in range(1, ly):
        now = y_rows(y)
        gy[y // SUB, y % SUB] = 0.5 * (prior + now)
        prior = now
    ky_last = prior

    @pl.when(iy > 0)
    def _():
        edge_y_right().wait_recv()

    @pl.when(iy < ny - 1)
    def _():
        edge_y_left().wait_recv()

    k0, u0, k1, u1 = edge_y_out[0, 0], edge_y_out[0, 1], edge_y_out[1, 0], edge_y_out[1, 1]
    inner, last = iy > 0, iy < ny - 1
    face_0 = 0.5 * (jnp.where(inner, edge_y_in[0, 0], 0.0) + k0)
    gy[0, 0] = face_0
    face_1 = 0.5 * (jnp.where(last, edge_y_in[1, 0], 0.0) + k1)
    flux_0 = face_0 * (jnp.where(inner, edge_y_in[0, 1], 0.0) - u0)
    flux_1 = face_1 * (jnp.where(last, edge_y_in[1, 1], 0.0) - u1)
    at_p, series, at_l = factor_tree(*factor_cells(lambda t: gy[:, t], coef_y), tree_y)
    at_l = at_l + jnp.where(iy == ny - 1, 0.5 * ky_last, 0.0)
    share_coefs(line_y, (at_p, series, at_l), every_y)


    ends = two_parts(jnp.concatenate([flux_0, flux_1], axis=0).T, 1)
    row = lax.broadcasted_iota(jnp.int32, (2 * groups, ly), 0)
    lane = lax.broadcasted_iota(jnp.int32, (2 * groups, ly), 1)
    inside = lax.broadcasted_iota(jnp.int32, (lanes, ly), 1) > 0
    for g in range(groups):
        put = jnp.where(((row == g) & (lane == 0)) | ((row == groups + g) & (lane == ly - 1)), 1.0, 0.0)
        put = jnp.concatenate([put, put], axis=0).astype(jnp.bfloat16)
        added = lax.dot_general(ends, put, (((1,), (0,)), ((), ())), preferred_element_type=F32)
        u = group(u_raw, g)
        k = group(ky_raw, g)
        flux = jnp.where(inside, 0.5 * (k + pltpu.roll(k, 1, 1)) * (u - pltpu.roll(u, 1, 1)), 0.0)
        nat[g * lanes : (g + 1) * lanes] = (u + added) + (pltpu.roll(flux, ly - 1, 1) - flux)

    def x_cells(t):
        return jnp.stack([x_rows(nat, b * SUB + t) for b in range(bx)], axis=0)

    d_p, d_l = down_cells(x_cells, coef_x, kept_x)
    d_p, d_l = down_tree(d_p, d_l, tree_x, tkept_x)
    await_coefs(line_x, every_x)
    line_ratios(ix, nx, every_x, chain_x, mine_x)
    send_values(line_x, d_p, d_l, out_x, got_x, mine_x)

    inverses = line_weights(ix, nx, chain_x, mine_x, weights_x)
    await_coefs(line_y, every_y)
    line_ratios(iy, ny, every_y, chain_y, mine_y)
    inverses_y = line_weights(iy, ny, chain_y, mine_y, weights_y)
    u_p, u_l = take_values(line_x, inverses, out_x, got_x, weights_x)
    before, nodes = up_tree(u_p, u_l, tree_x, tkept_x)

    def put_x(t, v):
        for b in range(bx):
            nat[pl.ds(b * SUB + t, nz, stride=lx), :] = v[b]

    up_cells(before, nodes, coef_x, kept_x, put_x)
    for g in range(groups):
        turned[g * ly : (g + 1) * ly] = (group(nat, g) - group(u_raw, g)).T

    def y_cells(t):
        return jnp.stack([y_rows(b * SUB + t) for b in range(by)], axis=0)

    d_p, d_l = down_cells(y_cells, coef_y, kept_y)
    d_p, d_l = down_tree(d_p, d_l, tree_y, tkept_y)
    send_values(line_y, d_p, d_l, out_y, got_y, mine_y)
    line_x.done_sending(lambda o: every_x.at[ix], every_x, 0)
    line_x.done_sending(lambda o: out_x.at[0], got_x, nx - 1)
    line_y.done_sending(lambda o: every_y.at[iy], every_y, 0)

    @pl.when(ix < nx - 1)
    def _():
        edge_x().wait_send()

    @pl.when(iy < ny - 1)
    def _():
        edge_y_right().wait_send()

    @pl.when(iy > 0)
    def _():
        edge_y_left().wait_send()

    u_p, u_l = take_values(line_y, inverses_y, out_y, got_y, weights_y)
    before, nodes = up_tree(u_p, u_l, tree_y, tkept_y)

    def put_y(t, v):
        for b in range(by):
            turned[pl.ds(b * SUB + t, groups, stride=ly), :] = v[b]

    up_cells(before, nodes, coef_y, kept_y, put_y)
    for g in range(groups):
        out_ref[g * lanes : (g + 1) * lanes] = group(u_raw, g) + 2.0 * turned[g * ly : (g + 1) * ly].T

    line_y.done_sending(lambda o: out_y.at[0], got_y, ny - 1)


def on_device(nx, ny, state, kappa_x, kappa_y):
    nz, lx, ly = state.shape
    groups = nz * lx // 128
    flat = (nz * lx, ly)
    bx, by = lx // SUB, ly // SUB

    def line_scratch(n, blocks, rows):
        one = (rows, 128)
        return [
            pltpu.VMEM((3, SUB - 1, blocks) + one, F32),
            pltpu.VMEM((SUB - 1, blocks) + one, F32),
            pltpu.VMEM((3, blocks - 1) + one, F32),
            pltpu.VMEM((blocks - 1,) + one, F32),
            pltpu.VMEM((n, 3) + one, F32),
            pltpu.VMEM((n, 2) + one, F32),
            pltpu.VMEM((n, 2) + one, F32),
            pltpu.VMEM((6,) + one, F32),
            pltpu.VMEM((2,) + one, F32),
            pltpu.VMEM((n,) + one, F32),
        ]

    scratch = (
        [pltpu.VMEM(flat, F32)] * 5
        + [
            pltpu.VMEM((bx, SUB, nz, ly), F32),
            pltpu.VMEM((by, SUB, groups, 128), F32),
        ]
        + line_scratch(nx, bx, nz)
        + line_scratch(ny, by, groups)
        + [
            pltpu.VMEM((nz, ly), F32),
            pltpu.VMEM((nz, ly), F32),
            pltpu.VMEM((2, 2, groups, 128), F32),
            pltpu.VMEM((2, 2, groups, 128), F32),
            pltpu.SemaphoreType.DMA((3,)),
            pltpu.SemaphoreType.DMA((2 * nx - 1,)),
            pltpu.SemaphoreType.DMA((2 * nx - 1,)),
            pltpu.SemaphoreType.DMA((2 * ny,)),
            pltpu.SemaphoreType.DMA((2 * ny,)),
        ]
    )
    out = pl.pallas_call(
        functools.partial(kernel, nx, ny, (nz, lx, ly)),
        out_shape=jax.ShapeDtypeStruct(flat, F32),
        in_specs=[pl.BlockSpec(memory_space=pltpu.HBM)] * 3,
        out_specs=pl.BlockSpec(memory_space=pltpu.VMEM),
        scratch_shapes=scratch,
        compiler_params=pltpu.CompilerParams(
            collective_id=0, has_side_effects=True, vmem_limit_bytes=32 * 1024 * 1024
        ),
    )(*[pltpu.with_memory_space_constraint(v.reshape(flat), pltpu.HBM) for v in (state, kappa_x, kappa_y)])
    return out.reshape(state.shape)


def solution(mesh):
    spec = P(None, "gx", "gy")
    return jax.shard_map(
        functools.partial(on_device, mesh.shape["gx"], mesh.shape["gy"]),
        mesh=mesh,
        in_specs=(spec, spec, spec),
        out_specs=spec,
        check_vma=False,
    )
```

```python
import functools

import jax
import jax.numpy as jnp
from jax import lax
from jax.experimental import pallas as pl
from jax.experimental.pallas import tpu as pltpu
from jax.sharding import PartitionSpec as P

MESH = pl.DeviceIdType.MESH
F32 = jnp.float32
SUB = 8


def recip(p):
    r = pl.reciprocal(p, approx=True)
    return r * (2.0 - p * r)


def two_parts(v, axis):
    high = v.astype(jnp.bfloat16)
    low = (v - high.astype(F32)).astype(jnp.bfloat16)
    return jnp.concatenate([high, low], axis=axis)


def factor_cells(face, coef):
    s = jnp.ones_like(face(0))
    to_p = face(0)
    at_p = jnp.zeros_like(s)
    for t in range(SUB - 1):
        right = face(t + 1)
        r = recip(s + to_p + right)
        a = right * r
        b = to_p * r
        coef[0, t] = r
        coef[1, t] = a
        coef[2, t] = b
        at_p = at_p + s * b
        s = 1.0 + s * a
        to_p = to_p * a
    return at_p, to_p, s


def halves(v):
    v = v.reshape((v.shape[0] // 2, 2) + v.shape[1:])
    return v[:, 0], v[:, 1]


def factor_tree(at_p, series, at_l, tree):
    level = 0
    at = 0
    while at_p.shape[0] > 1:
        pa, pb = halves(at_p)
        ga, gb = halves(series)
        la, lb = halves(at_l)
        c = la + pb
        r = recip(c + ga + gb)
        a = gb * r
        b = ga * r
        m = r.shape[0]
        tree[0, at : at + m] = r
        tree[1, at : at + m] = a
        tree[2, at : at + m] = b
        at_p = pa + c * b
        at_l = lb + c * a
        series = ga * a
        at += m
        level += 1
    return at_p[0], series[0], at_l[0]


def down_cells(source, coef, kept):
    d = source(0)
    at_p = None
    for t in range(SUB - 1):
        kept[t] = d
        share = coef[2, t] * d
        at_p = share if at_p is None else at_p + share
        d = source(t + 1) + coef[1, t] * d
    return at_p, d


def down_tree(at_p, at_l, tree, kept):
    at = 0
    while at_p.shape[0] > 1:
        pa, pb = halves(at_p)
        la, lb = halves(at_l)
        d = la + pb
        m = d.shape[0]
        kept[at : at + m] = d
        at_p = pa + tree[2, at : at + m] * d
        at_l = lb + tree[1, at : at + m] * d
        at += m
    return at_p[0], at_l[0]


def up_tree(u_p, u_l, tree, kept):
    nodes = u_l[None]
    total = kept.shape[0]
    m = 1
    at = total - 1
    while at >= 0:
        before = u_p[None] if m == 1 else jnp.concatenate([u_p[None], nodes[:-1]], axis=0)
        mid = (
            tree[0, at : at + m] * kept[at : at + m]
            + tree[1, at : at + m] * nodes
            + tree[2, at : at + m] * before
        )
        nodes = jnp.stack([mid, nodes], axis=1).reshape((2 * m,) + nodes.shape[1:])
        m *= 2
        at -= m
    before = jnp.concatenate([u_p[None], nodes[:-1]], axis=0)
    return before, nodes


def up_cells(before, nodes, coef, kept, put):
    u = nodes
    put(SUB - 1, u)
    for t in range(SUB - 2, -1, -1):
        u = coef[0, t] * kept[t] + coef[1, t] * u + coef[2, t] * before
        put(t, u)


def line_ratios(me, n, every, chain, mine):
    zero = jnp.zeros(every.shape[2:], F32)
    ahead = []
    prior = None
    for j in range(n):
        p, g, l = every[j, 0], every[j, 1], every[j, 2]
        if prior is None:
            ahead.append((zero, zero, l + g))
            prior = l + g
        else:
            c = prior + p
            ratio = g * recip(c + g)
            now = l + c * ratio
            ahead.append((ratio, prior, now))
            prior = now
    back = [None] * n
    later = zero
    for j in range(n - 1, -1, -1):
        p, g, l = every[j, 0], every[j, 1], every[j, 2]
        c = later + l
        ratio = g * recip(c + g)
        now = p + c * ratio
        back[j] = (ratio, later, now)
        later = now
    own = [zero] * 6
    for j in range(n):
        here = me == j
        own = [jnp.where(here, v, o) for v, o in zip(ahead[j] + back[j], own)]
        chain[j, 0] = ahead[j][0]
        chain[j, 1] = back[j][0]
    for i, v in enumerate(own):
        mine[i] = v


def line_weights(me, n, chain, mine, weights):
    rho, sf_prior, sf_now, tau, sb_later, sb_now = [mine[i] for i in range(6)]
    zero = jnp.zeros_like(rho)
    inv_l = recip(sf_now + sb_later)
    inv_p = jnp.where(me > 0, recip(sf_prior + sb_now), zero)
    ahead = [None] * n
    w_p, w_l = inv_p, inv_l * rho
    for j in range(n - 1, -1, -1):
        left = me > j
        ahead[j] = (w_p, w_l)
        w_p = jnp.where(left, w_p * chain[j, 0], w_p)
        w_l = jnp.where(left, w_l * chain[j, 0], w_l)
    w_p, w_l = inv_p * tau, inv_l
    for j in range(n):
        left, right = me > j, me < j
        weights[j, 0] = jnp.where(left, ahead[j][0], w_p)
        weights[j, 1] = jnp.where(left, ahead[j][1], w_l)
        w_p = jnp.where(right, w_p * chain[j, 1], w_p)
        w_l = jnp.where(right, w_l * chain[j, 1], w_l)
    return inv_p, inv_l


class Line:
    def __init__(self, axis, n, me, send, recv):
        self.axis, self.n, self.me, self.send, self.recv = axis, n, me, send, recv

    def copy(self, src, dst, slot, target):
        return pltpu.make_async_remote_copy(
            src_ref=src,
            dst_ref=dst,
            send_sem=self.send.at[slot],
            recv_sem=self.recv.at[slot],
            device_id={self.axis: target},
            device_id_type=MESH,
        )

    def others(self):
        for o in sorted(range(1, self.n), key=lambda o: abs(2 * o - self.n)):
            yield o, lax.rem(self.me + o, self.n), lax.rem(self.me + self.n - o, self.n)

    def start_all(self, src_of, buf, base):
        for o, target, _ in self.others():
            self.copy(src_of(o), buf.at[self.me], base + o - 1, target).start()

    def await_one(self, o, src, buf, base):
        source = lax.rem(self.me + self.n - o, self.n)
        self.copy(src, buf.at[source], base + o - 1, source).wait_recv()

    def done_sending(self, src_of, buf, base):
        for o, target, _ in self.others():
            self.copy(src_of(o), buf.at[self.me], base + o - 1, target).wait_send()


def share_coefs(line, mine, every):
    for i, v in enumerate(mine):
        every[line.me, i] = v
    line.start_all(lambda o: every.at[line.me], every, 0)


def await_coefs(line, every):
    for o, _, _ in line.others():
        line.await_one(o, every.at[line.me], every, 0)


def send_values(line, at_p, at_l, out, got, mine):
    me = line.me
    out[0] = at_l + mine[0] * at_p
    out[1] = at_p + mine[3] * at_l
    line.start_all(lambda o: out.at[(me + o) // line.n], got, line.n - 1)


def take_values(line, inverses, out, got, weights):
    u_p = inverses[0] * out[1]
    u_l = inverses[1] * out[0]
    for o, _, source in reversed(list(line.others())):
        line.await_one(o, out.at[0], got, line.n - 1)
        v = got[source]
        u_p = u_p + weights[source, 0] * v
        u_l = u_l + weights[source, 1] * v
    return u_p, u_l


def kernel(
    nx, ny, dims,
    u_hbm, kx_hbm, ky_hbm, out_ref,
    u_raw, kx_raw, ky_raw, nat, turned, gx, gy,
    coef_x, kept_x, tree_x, tkept_x, every_x, weights_x, chain_x, mine_x, out_x, got_x,
    coef_y, kept_y, tree_y, tkept_y, every_y, weights_y, chain_y, mine_y, out_y, got_y,
    edge_x_in, edge_y_out, edge_y_in,
    local_sem, xs, xr, ys, yr,
):
    nz, lx, ly = dims
    lanes = 128
    groups = nz * lx // lanes
    bx, by = lx // SUB, ly // SUB
    ix = lax.axis_index("gx")
    iy = lax.axis_index("gy")
    line_x = Line("gx", nx, ix, xs, xr)
    line_y = Line("gy", ny, iy, ys, yr)
    barrier = pltpu.get_barrier_semaphore()
    for line in (line_x, line_y):
        for _, target, _ in line.others():
            pl.semaphore_signal(barrier, inc=1, device_id={line.axis: target}, device_id_type=MESH)
    loads = []
    for i, (src, dst) in enumerate(((ky_hbm, ky_raw), (u_hbm, u_raw), (kx_hbm, kx_raw))):
        cp = pltpu.make_async_copy(src, dst, local_sem.at[i])
        cp.start()
        loads.append(cp)

    def group(ref, g):
        return ref[g * lanes : (g + 1) * lanes]

    def x_rows(ref, x):
        return ref[pl.ds(x, nz, stride=lx), :]

    def y_rows(y):
        return turned[pl.ds(y, groups, stride=ly), :]

    hx = 2 * (nx - 1)
    hy = 2 * (ny - 1)

    def edge_x():
        return line_x.copy(kx_hbm.reshape(nz, lx, ly).at[:, lx - 1, :], edge_x_in, hx, jnp.minimum(ix + 1, nx - 1))

    def edge_y_right():
        return line_y.copy(edge_y_out.at[1], edge_y_in.at[0], hy, jnp.minimum(iy + 1, ny - 1))

    def edge_y_left():
        return line_y.copy(edge_y_out.at[0], edge_y_in.at[1], hy + 1, jnp.maximum(iy - 1, 0))

    row16 = lax.broadcasted_iota(jnp.int32, (16, ly), 0)
    lane16 = lax.broadcasted_iota(jnp.int32, (16, ly), 1)
    pick = jnp.where(((row16 == 0) & (lane16 == 0)) | ((row16 == 1) & (lane16 == ly - 1)), 1.0, 0.0)
    pick = jnp.concatenate([pick, pick], axis=1).astype(jnp.bfloat16)
    for kind, (load, raw) in enumerate(((loads[0], ky_raw), (loads[1], u_raw))):
        load.wait()
        for g in range(groups):
            edges = lax.dot_general(
                pick, two_parts(group(raw, g), 1), (((1,), (1,)), ((), ())), preferred_element_type=F32
            )
            edge_y_out[0, kind, g : g + 1] = edges[0:1]
            edge_y_out[1, kind, g : g + 1] = edges[1:2]
    pl.semaphore_wait(barrier, nx - 1 + ny - 1)

    @pl.when(ix < nx - 1)
    def _():
        edge_x().start()

    @pl.when(iy < ny - 1)
    def _():
        edge_y_right().start()

    @pl.when(iy > 0)
    def _():
        edge_y_left().start()

    loads[2].wait()
    kx_first = x_rows(kx_raw, 0)
    kx_last = x_rows(kx_raw, lx - 1)

    prior = kx_first
    for x in range(1, lx):
        now = x_rows(kx_raw, x)
        gx[x // SUB, x % SUB] = 0.5 * (prior + now)
        prior = now
    @pl.when(ix > 0)
    def _():
        edge_x().wait_recv()

    gx[0, 0] = 0.5 * (jnp.where(ix > 0, edge_x_in[...], 0.0) + kx_first)
    at_p, series, at_l = factor_tree(*factor_cells(lambda t: gx[:, t], coef_x), tree_x)
    at_l = at_l + jnp.where(ix == nx - 1, 0.5 * kx_last, 0.0)
    share_coefs(line_x, (at_p, series, at_l), every_x)

    for g in range(groups):
        turned[g * ly : (g + 1) * ly] = group(ky_raw, g).T
    prior = y_rows(0)
    for y in range(1, ly):
        now = y_rows(y)
        gy[y // SUB, y % SUB] = 0.5 * (prior + now)
        prior = now
    ky_last = prior

    @pl.when(iy > 0)
    def _():
        edge_y_right().wait_recv()

    @pl.when(iy < ny - 1)
    def _():
        edge_y_left().wait_recv()

    k0, u0, k1, u1 = edge_y_out[0, 0], edge_y_out[0, 1], edge_y_out[1, 0], edge_y_out[1, 1]
    inner, last = iy > 0, iy < ny - 1
    face_0 = 0.5 * (jnp.where(inner, edge_y_in[0, 0], 0.0) + k0)
    gy[0, 0] = face_0
    face_1 = 0.5 * (jnp.where(last, edge_y_in[1, 0], 0.0) + k1)
    flux_0 = face_0 * (jnp.where(inner, edge_y_in[0, 1], 0.0) - u0)
    flux_1 = face_1 * (jnp.where(last, edge_y_in[1, 1], 0.0) - u1)
    at_p, series, at_l = factor_tree(*factor_cells(lambda t: gy[:, t], coef_y), tree_y)
    at_l = at_l + jnp.where(iy == ny - 1, 0.5 * ky_last, 0.0)
    share_coefs(line_y, (at_p, series, at_l), every_y)


    ends = two_parts(jnp.concatenate([flux_0, flux_1], axis=0).T, 1)
    row = lax.broadcasted_iota(jnp.int32, (2 * groups, ly), 0)
    lane = lax.broadcasted_iota(jnp.int32, (2 * groups, ly), 1)
    inside = lax.broadcasted_iota(jnp.int32, (lanes, ly), 1) > 0
    for g in range(groups):
        put = jnp.where(((row == g) & (lane == 0)) | ((row == groups + g) & (lane == ly - 1)), 1.0, 0.0)
        put = jnp.concatenate([put, put], axis=0).astype(jnp.bfloat16)
        added = lax.dot_general(ends, put, (((1,), (0,)), ((), ())), preferred_element_type=F32)
        u = group(u_raw, g)
        k = group(ky_raw, g)
        flux = jnp.where(inside, 0.5 * (k + pltpu.roll(k, 1, 1)) * (u - pltpu.roll(u, 1, 1)), 0.0)
        nat[g * lanes : (g + 1) * lanes] = (u + added) + (pltpu.roll(flux, ly - 1, 1) - flux)

    def x_cells(t):
        return jnp.stack([x_rows(nat, b * SUB + t) for b in range(bx)], axis=0)

    d_p, d_l = down_cells(x_cells, coef_x, kept_x)
    d_p, d_l = down_tree(d_p, d_l, tree_x, tkept_x)
    await_coefs(line_x, every_x)
    line_ratios(ix, nx, every_x, chain_x, mine_x)
    send_values(line_x, d_p, d_l, out_x, got_x, mine_x)

    inverses = line_weights(ix, nx, chain_x, mine_x, weights_x)
    await_coefs(line_y, every_y)
    line_ratios(iy, ny, every_y, chain_y, mine_y)
    inverses_y = line_weights(iy, ny, chain_y, mine_y, weights_y)
    u_p, u_l = take_values(line_x, inverses, out_x, got_x, weights_x)
    before, nodes = up_tree(u_p, u_l, tree_x, tkept_x)

    def put_x(t, v):
        for b in range(bx):
            nat[pl.ds(b * SUB + t, nz, stride=lx), :] = v[b]

    up_cells(before, nodes, coef_x, kept_x, put_x)
    for g in range(groups):
        turned[g * ly : (g + 1) * ly] = (group(nat, g) - group(u_raw, g)).T

    def y_cells(t):
        return jnp.stack([y_rows(b * SUB + t) for b in range(by)], axis=0)

    d_p, d_l = down_cells(y_cells, coef_y, kept_y)
    d_p, d_l = down_tree(d_p, d_l, tree_y, tkept_y)
    send_values(line_y, d_p, d_l, out_y, got_y, mine_y)
    line_x.done_sending(lambda o: every_x.at[ix], every_x, 0)
    line_x.done_sending(lambda o: out_x.at[0], got_x, nx - 1)
    line_y.done_sending(lambda o: every_y.at[iy], every_y, 0)

    @pl.when(ix < nx - 1)
    def _():
        edge_x().wait_send()

    @pl.when(iy < ny - 1)
    def _():
        edge_y_right().wait_send()

    @pl.when(iy > 0)
    def _():
        edge_y_left().wait_send()

    u_p, u_l = take_values(line_y, inverses_y, out_y, got_y, weights_y)
    before, nodes = up_tree(u_p, u_l, tree_y, tkept_y)

    def put_y(t, v):
        for b in range(by):
            turned[pl.ds(b * SUB + t, groups, stride=ly), :] = v[b]

    up_cells(before, nodes, coef_y, kept_y, put_y)
    for g in range(groups):
        out_ref[g * lanes : (g + 1) * lanes] = group(u_raw, g) + 2.0 * turned[g * ly : (g + 1) * ly].T

    line_y.done_sending(lambda o: out_y.at[0], got_y, ny - 1)


def on_device(nx, ny, state, kappa_x, kappa_y):
    nz, lx, ly = state.shape
    groups = nz * lx // 128
    flat = (nz * lx, ly)
    bx, by = lx // SUB, ly // SUB

    def line_scratch(n, blocks, rows):
        one = (rows, 128)
        return [
            pltpu.VMEM((3, SUB - 1, blocks) + one, F32),
            pltpu.VMEM((SUB - 1, blocks) + one, F32),
            pltpu.VMEM((3, blocks - 1) + one, F32),
            pltpu.VMEM((blocks - 1,) + one, F32),
            pltpu.VMEM((n, 3) + one, F32),
            pltpu.VMEM((n, 2) + one, F32),
            pltpu.VMEM((n, 2) + one, F32),
            pltpu.VMEM((6,) + one, F32),
            pltpu.VMEM((2,) + one, F32),
            pltpu.VMEM((n,) + one, F32),
        ]

    scratch = (
        [pltpu.VMEM(flat, F32)] * 5
        + [
            pltpu.VMEM((bx, SUB, nz, ly), F32),
            pltpu.VMEM((by, SUB, groups, 128), F32),
        ]
        + line_scratch(nx, bx, nz)
        + line_scratch(ny, by, groups)
        + [
            pltpu.VMEM((nz, ly), F32),
            pltpu.VMEM((2, 2, groups, 128), F32),
            pltpu.VMEM((2, 2, groups, 128), F32),
            pltpu.SemaphoreType.DMA((3,)),
            pltpu.SemaphoreType.DMA((2 * nx - 1,)),
            pltpu.SemaphoreType.DMA((2 * nx - 1,)),
            pltpu.SemaphoreType.DMA((2 * ny,)),
            pltpu.SemaphoreType.DMA((2 * ny,)),
        ]
    )
    out = pl.pallas_call(
        functools.partial(kernel, nx, ny, (nz, lx, ly)),
        out_shape=jax.ShapeDtypeStruct(flat, F32),
        in_specs=[pl.BlockSpec(memory_space=pltpu.HBM)] * 3,
        out_specs=pl.BlockSpec(memory_space=pltpu.VMEM),
        scratch_shapes=scratch,
        compiler_params=pltpu.CompilerParams(
            collective_id=0, has_side_effects=True, vmem_limit_bytes=32 * 1024 * 1024
        ),
    )(*[pltpu.with_memory_space_constraint(v.reshape(flat), pltpu.HBM) for v in (state, kappa_x, kappa_y)])
    return out.reshape(state.shape)


def solution(mesh):
    spec = P(None, "gx", "gy")
    return jax.shard_map(
        functools.partial(on_device, mesh.shape["gx"], mesh.shape["gy"]),
        mesh=mesh,
        in_specs=(spec, spec, spec),
        out_specs=spec,
        check_vma=False,
    )
```

```python
import functools

import jax
import jax.numpy as jnp
from jax import lax
from jax.experimental import pallas as pl
from jax.experimental.pallas import tpu as pltpu
from jax.sharding import PartitionSpec as P

MESH = pl.DeviceIdType.MESH
F32 = jnp.float32
SUB = 8


def recip(p):
    r = pl.reciprocal(p, approx=True)
    return r * (2.0 - p * r)


def two_parts(v, axis):
    high = v.astype(jnp.bfloat16)
    low = (v - high.astype(F32)).astype(jnp.bfloat16)
    return jnp.concatenate([high, low], axis=axis)


def factor_cells(face, coef):
    s = jnp.ones_like(face(0))
    to_p = face(0)
    at_p = jnp.zeros_like(s)
    for t in range(SUB - 1):
        right = face(t + 1)
        r = recip(s + to_p + right)
        a = right * r
        b = to_p * r
        coef[0, t] = r
        coef[1, t] = a
        coef[2, t] = b
        at_p = at_p + s * b
        s = 1.0 + s * a
        to_p = to_p * a
    return at_p, to_p, s


def halves(v):
    v = v.reshape((v.shape[0] // 2, 2) + v.shape[1:])
    return v[:, 0], v[:, 1]


def factor_tree(at_p, series, at_l, tree):
    level = 0
    at = 0
    while at_p.shape[0] > 1:
        pa, pb = halves(at_p)
        ga, gb = halves(series)
        la, lb = halves(at_l)
        c = la + pb
        r = recip(c + ga + gb)
        a = gb * r
        b = ga * r
        m = r.shape[0]
        tree[0, at : at + m] = r
        tree[1, at : at + m] = a
        tree[2, at : at + m] = b
        at_p = pa + c * b
        at_l = lb + c * a
        series = ga * a
        at += m
        level += 1
    return at_p[0], series[0], at_l[0]


def down_cells(source, coef, kept):
    d = source(0)
    at_p = None
    for t in range(SUB - 1):
        kept[t] = d
        share = coef[2, t] * d
        at_p = share if at_p is None else at_p + share
        d = source(t + 1) + coef[1, t] * d
    return at_p, d


def down_tree(at_p, at_l, tree, kept):
    at = 0
    while at_p.shape[0] > 1:
        pa, pb = halves(at_p)
        la, lb = halves(at_l)
        d = la + pb
        m = d.shape[0]
        kept[at : at + m] = d
        at_p = pa + tree[2, at : at + m] * d
        at_l = lb + tree[1, at : at + m] * d
        at += m
    return at_p[0], at_l[0]


def up_tree(u_p, u_l, tree, kept):
    nodes = u_l[None]
    total = kept.shape[0]
    m = 1
    at = total - 1
    while at >= 0:
        before = u_p[None] if m == 1 else jnp.concatenate([u_p[None], nodes[:-1]], axis=0)
        mid = (
            tree[0, at : at + m] * kept[at : at + m]
            + tree[1, at : at + m] * nodes
            + tree[2, at : at + m] * before
        )
        nodes = jnp.stack([mid, nodes], axis=1).reshape((2 * m,) + nodes.shape[1:])
        m *= 2
        at -= m
    before = jnp.concatenate([u_p[None], nodes[:-1]], axis=0)
    return before, nodes


def up_cells(before, nodes, coef, kept, put):
    u = nodes
    put(SUB - 1, u)
    for t in range(SUB - 2, -1, -1):
        u = coef[0, t] * kept[t] + coef[1, t] * u + coef[2, t] * before
        put(t, u)


def line_ratios(me, n, every, chain, mine):
    zero = jnp.zeros(every.shape[2:], F32)
    ahead = []
    prior = None
    for j in range(n):
        p, g, l = every[j, 0], every[j, 1], every[j, 2]
        if prior is None:
            ahead.append((zero, zero, l + g))
            prior = l + g
        else:
            c = prior + p
            ratio = g * recip(c + g)
            now = l + c * ratio
            ahead.append((ratio, prior, now))
            prior = now
    back = [None] * n
    later = zero
    for j in range(n - 1, -1, -1):
        p, g, l = every[j, 0], every[j, 1], every[j, 2]
        c = later + l
        ratio = g * recip(c + g)
        now = p + c * ratio
        back[j] = (ratio, later, now)
        later = now
    own = [zero] * 6
    for j in range(n):
        here = me == j
        own = [jnp.where(here, v, o) for v, o in zip(ahead[j] + back[j], own)]
        chain[j, 0] = ahead[j][0]
        chain[j, 1] = back[j][0]
    for i, v in enumerate(own):
        mine[i] = v


def line_weights(me, n, chain, mine, weights):
    rho, sf_prior, sf_now, tau, sb_later, sb_now = [mine[i] for i in range(6)]
    zero = jnp.zeros_like(rho)
    inv_l = recip(sf_now + sb_later)
    inv_p = jnp.where(me > 0, recip(sf_prior + sb_now), zero)
    ahead = [None] * n
    w_p, w_l = inv_p, inv_l * rho
    for j in range(n - 1, -1, -1):
        left = me > j
        ahead[j] = (w_p, w_l)
        w_p = jnp.where(left, w_p * chain[j, 0], w_p)
        w_l = jnp.where(left, w_l * chain[j, 0], w_l)
    w_p, w_l = inv_p * tau, inv_l
    for j in range(n):
        left, right = me > j, me < j
        weights[j, 0] = jnp.where(left, ahead[j][0], w_p)
        weights[j, 1] = jnp.where(left, ahead[j][1], w_l)
        w_p = jnp.where(right, w_p * chain[j, 1], w_p)
        w_l = jnp.where(right, w_l * chain[j, 1], w_l)
    return inv_p, inv_l


class Line:
    def __init__(self, axis, n, me, send, recv):
        self.axis, self.n, self.me, self.send, self.recv = axis, n, me, send, recv

    def copy(self, src, dst, slot, target):
        return pltpu.make_async_remote_copy(
            src_ref=src,
            dst_ref=dst,
            send_sem=self.send.at[slot],
            recv_sem=self.recv.at[slot],
            device_id={self.axis: target},
            device_id_type=MESH,
        )

    def others(self):
        for o in range(1, self.n):
            yield o, lax.rem(self.me + o, self.n), lax.rem(self.me + self.n - o, self.n)

    def start_all(self, src_of, buf, base):
        for o, target, _ in self.others():
            self.copy(src_of(o), buf.at[self.me], base + o - 1, target).start()

    def await_one(self, o, src, buf, base):
        source = lax.rem(self.me + self.n - o, self.n)
        self.copy(src, buf.at[source], base + o - 1, source).wait_recv()

    def done_sending(self, src_of, buf, base):
        for o, target, _ in self.others():
            self.copy(src_of(o), buf.at[self.me], base + o - 1, target).wait_send()


def share_coefs(line, mine, every):
    for i, v in enumerate(mine):
        every[line.me, i] = v
    line.start_all(lambda o: every.at[line.me], every, 0)


def await_coefs(line, every):
    for o, _, _ in line.others():
        line.await_one(o, every.at[line.me], every, 0)


def send_values(line, at_p, at_l, out, got, mine):
    me = line.me
    out[0] = at_l + mine[0] * at_p
    out[1] = at_p + mine[3] * at_l
    line.start_all(lambda o: out.at[(me + o) // line.n], got, line.n - 1)


def take_values(line, inverses, out, got, weights):
    u_p = inverses[0] * out[1]
    u_l = inverses[1] * out[0]
    for o, _, source in line.others():
        line.await_one(o, out.at[0], got, line.n - 1)
        v = got[source]
        u_p = u_p + weights[source, 0] * v
        u_l = u_l + weights[source, 1] * v
    return u_p, u_l


def kernel(
    nx, ny, dims,
    u_hbm, kx_hbm, ky_hbm, out_ref,
    u_raw, kx_raw, ky_raw, nat, turned, gx, gy,
    coef_x, kept_x, tree_x, tkept_x, every_x, weights_x, chain_x, mine_x, out_x, got_x,
    coef_y, kept_y, tree_y, tkept_y, every_y, weights_y, chain_y, mine_y, out_y, got_y,
    edge_x_out, edge_x_in, edge_y_out, edge_y_in,
    local_sem, xs, xr, ys, yr,
):
    nz, lx, ly = dims
    lanes = 128
    groups = nz * lx // lanes
    bx, by = lx // SUB, ly // SUB
    ix = lax.axis_index("gx")
    iy = lax.axis_index("gy")
    line_x = Line("gx", nx, ix, xs, xr)
    line_y = Line("gy", ny, iy, ys, yr)
    barrier = pltpu.get_barrier_semaphore()
    for line in (line_x, line_y):
        for _, target, _ in line.others():
            pl.semaphore_signal(barrier, inc=1, device_id={line.axis: target}, device_id_type=MESH)
    loads = []
    for i, (src, dst) in enumerate(((ky_hbm, ky_raw), (u_hbm, u_raw), (kx_hbm, kx_raw))):
        cp = pltpu.make_async_copy(src, dst, local_sem.at[i])
        cp.start()
        loads.append(cp)

    def group(ref, g):
        return ref[g * lanes : (g + 1) * lanes]

    def x_rows(ref, x):
        return ref[pl.ds(x, nz, stride=lx), :]

    def y_rows(y):
        return turned[pl.ds(y, groups, stride=ly), :]

    hx = 2 * (nx - 1)
    hy = 2 * (ny - 1)

    def edge_x():
        return line_x.copy(edge_x_out, edge_x_in, hx, jnp.minimum(ix + 1, nx - 1))

    def edge_y_right():
        return line_y.copy(edge_y_out.at[1], edge_y_in.at[0], hy, jnp.minimum(iy + 1, ny - 1))

    def edge_y_left():
        return line_y.copy(edge_y_out.at[0], edge_y_in.at[1], hy + 1, jnp.maximum(iy - 1, 0))

    row16 = lax.broadcasted_iota(jnp.int32, (16, ly), 0)
    lane16 = lax.broadcasted_iota(jnp.int32, (16, ly), 1)
    pick = jnp.where(((row16 == 0) & (lane16 == 0)) | ((row16 == 1) & (lane16 == ly - 1)), 1.0, 0.0)
    pick = jnp.concatenate([pick, pick], axis=1).astype(jnp.bfloat16)
    for kind, (load, raw) in enumerate(((loads[0], ky_raw), (loads[1], u_raw))):
        load.wait()
        for g in range(groups):
            edges = lax.dot_general(
                pick, two_parts(group(raw, g), 1), (((1,), (1,)), ((), ())), preferred_element_type=F32
            )
            edge_y_out[0, kind, g : g + 1] = edges[0:1]
            edge_y_out[1, kind, g : g + 1] = edges[1:2]
    pl.semaphore_wait(barrier, nx - 1 + ny - 1)

    @pl.when(iy < ny - 1)
    def _():
        edge_y_right().start()

    @pl.when(iy > 0)
    def _():
        edge_y_left().start()

    loads[2].wait()
    kx_first = x_rows(kx_raw, 0)
    kx_last = x_rows(kx_raw, lx - 1)
    edge_x_out[...] = kx_last

    @pl.when(ix < nx - 1)
    def _():
        edge_x().start()

    prior = kx_first
    for x in range(1, lx):
        now = x_rows(kx_raw, x)
        gx[x // SUB, x % SUB] = 0.5 * (prior + now)
        prior = now
    @pl.when(ix > 0)
    def _():
        edge_x().wait_recv()

    gx[0, 0] = 0.5 * (jnp.where(ix > 0, edge_x_in[...], 0.0) + kx_first)
    at_p, series, at_l = factor_tree(*factor_cells(lambda t: gx[:, t], coef_x), tree_x)
    at_l = at_l + jnp.where(ix == nx - 1, 0.5 * kx_last, 0.0)
    share_coefs(line_x, (at_p, series, at_l), every_x)

    for g in range(groups):
        turned[g * ly : (g + 1) * ly] = group(ky_raw, g).T
    prior = y_rows(0)
    for y in range(1, ly):
        now = y_rows(y)
        gy[y // SUB, y % SUB] = 0.5 * (prior + now)
        prior = now
    ky_last = prior

    @pl.when(iy > 0)
    def _():
        edge_y_right().wait_recv()

    @pl.when(iy < ny - 1)
    def _():
        edge_y_left().wait_recv()

    k0, u0, k1, u1 = edge_y_out[0, 0], edge_y_out[0, 1], edge_y_out[1, 0], edge_y_out[1, 1]
    inner, last = iy > 0, iy < ny - 1
    face_0 = 0.5 * (jnp.where(inner, edge_y_in[0, 0], 0.0) + k0)
    gy[0, 0] = face_0
    face_1 = 0.5 * (jnp.where(last, edge_y_in[1, 0], 0.0) + k1)
    flux_0 = face_0 * (jnp.where(inner, edge_y_in[0, 1], 0.0) - u0)
    flux_1 = face_1 * (jnp.where(last, edge_y_in[1, 1], 0.0) - u1)
    at_p, series, at_l = factor_tree(*factor_cells(lambda t: gy[:, t], coef_y), tree_y)
    at_l = at_l + jnp.where(iy == ny - 1, 0.5 * ky_last, 0.0)
    share_coefs(line_y, (at_p, series, at_l), every_y)


    ends = two_parts(jnp.concatenate([flux_0, flux_1], axis=0).T, 1)
    row = lax.broadcasted_iota(jnp.int32, (2 * groups, ly), 0)
    lane = lax.broadcasted_iota(jnp.int32, (2 * groups, ly), 1)
    inside = lax.broadcasted_iota(jnp.int32, (lanes, ly), 1) > 0
    for g in range(groups):
        put = jnp.where(((row == g) & (lane == 0)) | ((row == groups + g) & (lane == ly - 1)), 1.0, 0.0)
        put = jnp.concatenate([put, put], axis=0).astype(jnp.bfloat16)
        added = lax.dot_general(ends, put, (((1,), (0,)), ((), ())), preferred_element_type=F32)
        u = group(u_raw, g)
        k = group(ky_raw, g)
        flux = jnp.where(inside, 0.5 * (k + pltpu.roll(k, 1, 1)) * (u - pltpu.roll(u, 1, 1)), 0.0)
        nat[g * lanes : (g + 1) * lanes] = (u + added) + (pltpu.roll(flux, ly - 1, 1) - flux)

    def x_cells(t):
        return jnp.stack([x_rows(nat, b * SUB + t) for b in range(bx)], axis=0)

    d_p, d_l = down_cells(x_cells, coef_x, kept_x)
    d_p, d_l = down_tree(d_p, d_l, tree_x, tkept_x)
    await_coefs(line_x, every_x)
    line_ratios(ix, nx, every_x, chain_x, mine_x)
    send_values(line_x, d_p, d_l, out_x, got_x, mine_x)

    inverses = line_weights(ix, nx, chain_x, mine_x, weights_x)
    await_coefs(line_y, every_y)
    line_ratios(iy, ny, every_y, chain_y, mine_y)
    inverses_y = line_weights(iy, ny, chain_y, mine_y, weights_y)
    u_p, u_l = take_values(line_x, inverses, out_x, got_x, weights_x)
    before, nodes = up_tree(u_p, u_l, tree_x, tkept_x)

    def put_x(t, v):
        for b in range(bx):
            nat[pl.ds(b * SUB + t, nz, stride=lx), :] = v[b]

    up_cells(before, nodes, coef_x, kept_x, put_x)
    for g in range(groups):
        turned[g * ly : (g + 1) * ly] = (group(nat, g) - group(u_raw, g)).T

    def y_cells(t):
        return jnp.stack([y_rows(b * SUB + t) for b in range(by)], axis=0)

    d_p, d_l = down_cells(y_cells, coef_y, kept_y)
    d_p, d_l = down_tree(d_p, d_l, tree_y, tkept_y)
    send_values(line_y, d_p, d_l, out_y, got_y, mine_y)
    line_x.done_sending(lambda o: every_x.at[ix], every_x, 0)
    line_x.done_sending(lambda o: out_x.at[0], got_x, nx - 1)
    line_y.done_sending(lambda o: every_y.at[iy], every_y, 0)

    @pl.when(ix < nx - 1)
    def _():
        edge_x().wait_send()

    @pl.when(iy < ny - 1)
    def _():
        edge_y_right().wait_send()

    @pl.when(iy > 0)
    def _():
        edge_y_left().wait_send()

    u_p, u_l = take_values(line_y, inverses_y, out_y, got_y, weights_y)
    before, nodes = up_tree(u_p, u_l, tree_y, tkept_y)

    def put_y(t, v):
        for b in range(by):
            turned[pl.ds(b * SUB + t, groups, stride=ly), :] = v[b]

    up_cells(before, nodes, coef_y, kept_y, put_y)
    for g in range(groups):
        out_ref[g * lanes : (g + 1) * lanes] = group(u_raw, g) + 2.0 * turned[g * ly : (g + 1) * ly].T

    line_y.done_sending(lambda o: out_y.at[0], got_y, ny - 1)


def on_device(nx, ny, state, kappa_x, kappa_y):
    nz, lx, ly = state.shape
    groups = nz * lx // 128
    flat = (nz * lx, ly)
    bx, by = lx // SUB, ly // SUB

    def line_scratch(n, blocks, rows):
        one = (rows, 128)
        return [
            pltpu.VMEM((3, SUB - 1, blocks) + one, F32),
            pltpu.VMEM((SUB - 1, blocks) + one, F32),
            pltpu.VMEM((3, blocks - 1) + one, F32),
            pltpu.VMEM((blocks - 1,) + one, F32),
            pltpu.VMEM((n, 3) + one, F32),
            pltpu.VMEM((n, 2) + one, F32),
            pltpu.VMEM((n, 2) + one, F32),
            pltpu.VMEM((6,) + one, F32),
            pltpu.VMEM((2,) + one, F32),
            pltpu.VMEM((n,) + one, F32),
        ]

    scratch = (
        [pltpu.VMEM(flat, F32)] * 5
        + [
            pltpu.VMEM((bx, SUB, nz, ly), F32),
            pltpu.VMEM((by, SUB, groups, 128), F32),
        ]
        + line_scratch(nx, bx, nz)
        + line_scratch(ny, by, groups)
        + [
            pltpu.VMEM((nz, ly), F32),
            pltpu.VMEM((nz, ly), F32),
            pltpu.VMEM((2, 2, groups, 128), F32),
            pltpu.VMEM((2, 2, groups, 128), F32),
            pltpu.SemaphoreType.DMA((3,)),
            pltpu.SemaphoreType.DMA((2 * nx - 1,)),
            pltpu.SemaphoreType.DMA((2 * nx - 1,)),
            pltpu.SemaphoreType.DMA((2 * ny,)),
            pltpu.SemaphoreType.DMA((2 * ny,)),
        ]
    )
    out = pl.pallas_call(
        functools.partial(kernel, nx, ny, (nz, lx, ly)),
        out_shape=jax.ShapeDtypeStruct(flat, F32),
        in_specs=[pl.BlockSpec(memory_space=pltpu.HBM)] * 3,
        out_specs=pl.BlockSpec(memory_space=pltpu.VMEM),
        scratch_shapes=scratch,
        compiler_params=pltpu.CompilerParams(
            collective_id=0, has_side_effects=True, vmem_limit_bytes=32 * 1024 * 1024
        ),
    )(*[pltpu.with_memory_space_constraint(v.reshape(flat), pltpu.HBM) for v in (state, kappa_x, kappa_y)])
    return out.reshape(state.shape)


def solution(mesh):
    spec = P(None, "gx", "gy")
    return jax.shard_map(
        functools.partial(on_device, mesh.shape["gx"], mesh.shape["gy"]),
        mesh=mesh,
        in_specs=(spec, spec, spec),
        out_specs=spec,
        check_vma=False,
    )
```
